32 devices in a mesh: shard: 4 (over x, core), ctx: 4 (over z), tp: 2 (over y).
Axes of the slice: x: 2, y: 2, z: 4, core: 2. Of those that a mesh axis runs over, the one named last changes fastest.
Arguments:
- tokens: bfloat16 [16384, 1536], P(('shard', 'ctx')), may hold values from -6 to 6
- cotangent: bfloat16 [16384, 1536], P(('shard', 'ctx')), may hold values from -6 to 6
- segment: int32 [4, 4096], P('shard'), may hold values from 0 to 16, as said below
- parent: int32 [4, 17], P('shard'), may hold values from -1 to 16, as said below
- gain_attn: bfloat16 [1536], replicated, may hold values from 0.5 to 1.5
- qkv_weight: bfloat16 [1536, 2048], P('shard', 'tp'), may hold values from -0.15625 to 0.15625
- qkv_bias: bfloat16 [2048], P('tp'), may hold values from -0.59765625 to 0.59765625
- out_weight: bfloat16 [1536, 1536], P('shard', 'tp'), may hold values from -2.5 to 2.5
- gain_ffn: bfloat16 [1536], replicated, may hold values from 0.5 to 1.5
- gate_weight: bfloat16 [1536, 8960], P('shard', 'tp'), may hold values from -0.15625 to 0.15625
- up_weight: bfloat16 [1536, 8960], P('shard', 'tp'), may hold values from -0.15625 to 0.15625
- down_weight: bfloat16 [1536, 8960], P('shard', 'tp'), may hold values from -0.125 to 0.125
Outputs:
- output: bfloat16 [16384, 1536], P(('shard', 'ctx'))
- input_grad: float32 [16384, 1536], P(('shard', 'ctx'))
- grad_gain_attn: float32 [1536], replicated
- grad_qkv: float32 [1536, 2048], P('shard', 'tp')
- grad_bias: float32 [2048], P('tp')
- grad_out: float32 [1536, 1536], P('shard', 'tp')
- grad_gain_ffn: float32 [1536], replicated
- grad_gate: float32 [1536, 8960], P('shard', 'tp')
- grad_up: float32 [1536, 8960], P('shard', 'tp')
- grad_down: float32 [1536, 8960], P('shard', 'tp')
- clip: float32 [12], P('tp')
The draws below stay inside these ranges and needn't reach their ends.
Inputs may be any that keep to these rules, and one draw needn't show every extreme that they name: `segment`: in each row ids never fall, and every id of 0 to 16 occurs in one run. parent[s] is -1 for a root, s for a padding segment, or an id below s that is not a padding segment; a parent's parent is a root or -1 is reached within two steps.
All inputs are finite; a program needn't handle non-finite values.
Results may differ from the reference program's by a relative error of at most 0.019.
Values may be sent and summed in bfloat16 or wider, within the bound.
A program may use at most 320 MiB of HBM per device.

```python
import math
import jax
import jax.numpy as jnp
from jax import lax

D = 1536
FF = 8960
HEADS = 12
KV_HEADS = 2
HEAD = 128
QKV = 2048
SLOTS = 4096
TOKENS = 16384


def tree_row(key, row_index):
    unit_len = SLOTS // 32
    row_key = jax.random.fold_in(jax.random.fold_in(key, 9001), row_index)
    key_shape, key_pair, key_tail, key_leaves = jax.random.split(row_key, 4)
    parent_table = jnp.array([[-1, -1, 0, 0, 0, 0, 1, 1, 2, 2, 3, 3, 4, 4, 5, 5, 16], [-1, 0, 0, -1, 3, 3, 3, 4, 4, 5, 6, 1, 1, 1, 2, 2, 16], [-1, -1, 2, 0, 0, 0, 1, 6, 6, 3, 3, 3, 4, 4, 5, 5, 16]], dtype=jnp.int32)
    unit_table = jnp.array([[9, 5, 1, 1, 1, 1, 2, 2, 1, 1, 1, 1, 1, 1, 1, 1, 2], [9, 2, 2, 5, 1, 1, 1, 1, 1, 1, 1, 1, 1, 1, 1, 1, 2], [10, 5, 1, 1, 1, 1, 2, 1, 1, 1, 1, 1, 1, 1, 1, 1, 2]], dtype=jnp.int32)
    leaf_first = jnp.array([8, 11, 9], dtype=jnp.int32)
    shape_pick = jax.random.randint(key_shape, (), 0, 3, dtype=jnp.int32)
    parent_base = parent_table[shape_pick]
    unit_row = unit_table[shape_pick]
    pair_shift = jax.random.randint(key_pair, (8,), 0, unit_len, dtype=jnp.int32)
    tail_shift = jax.random.randint(key_tail, (), 0, unit_len, dtype=jnp.int32)
    seg_ids = jnp.arange(17, dtype=jnp.int32)
    shifts = jnp.concatenate([jnp.stack([pair_shift, -pair_shift], axis=1).reshape(16), jnp.zeros((1,), jnp.int32)])
    shifts = shifts + jnp.where(seg_ids == 16, tail_shift, 0) - jnp.where(seg_ids == 0, tail_shift, 0)
    lengths = unit_row * unit_len + shifts
    seg_ends = jnp.cumsum(lengths, dtype=jnp.int32)
    slot_ids = jnp.arange(SLOTS, dtype=jnp.int32)
    seg_row = jnp.sum((slot_ids[:, None] >= seg_ends[None, :16]).astype(jnp.int32), axis=1, dtype=jnp.int32)
    leaf_low = leaf_first[shape_pick]
    inside = (seg_ids >= leaf_low) & (seg_ids < 16)
    mixing = jax.random.permutation(key_leaves, 17).astype(jnp.int32)
    order_score = jnp.where(inside, leaf_low * 64 + 1 + mixing, seg_ids * 64)
    leaf_order = jnp.argsort(order_score, stable=True).astype(jnp.int32)
    parent_row = parent_base[leaf_order]
    return (seg_row, parent_row)


def draw_segment(key, part):

    def one_row(row_index):
        return tree_row(key, row_index)[0]
    return jax.vmap(one_row)(jnp.arange(TOKENS // SLOTS, dtype=jnp.int32))


def draw_parent(key, part):

    def one_row(row_index):
        return tree_row(key, row_index)[1]
    return jax.vmap(one_row)(jnp.arange(TOKENS // SLOTS, dtype=jnp.int32))


def block_levels(own_key, dims, pieces, least, high):
    def one(axis_at, parts):
        heights = jax.random.uniform(jax.random.fold_in(jax.random.fold_in(own_key, 6), axis_at), (parts,), jnp.float32, least / len(pieces), high / len(pieces))
        return jnp.repeat(jnp.exp(heights), dims[axis_at] // parts).reshape((-1,) + (1,) * (len(dims) - axis_at - 1))

    factor_of = one(*pieces[0])
    for cut in pieces[1:]:
        factor_of = factor_of * one(*cut)
    return factor_of


def centred(own_key, shape, width, reach, pieces=(), kind=jnp.bfloat16):
    values = width * jax.random.normal(own_key, shape, jnp.float32)
    if pieces:
        values = values * block_levels(own_key, shape, pieces, -0.22, 0.18)
    return jnp.clip(values, -reach, reach).astype(kind)


def setup_inputs(seed: int = 0) -> dict:
    keys = jax.random.split(jax.random.key(seed), 13)
    return {
        "tokens": centred(keys[0], (TOKENS, D), 1.0, 6.0, ((0, 16),)),
        "cotangent": centred(keys[1], (TOKENS, D), 1.0, 6.0, ((0, 16),)),
        "segment": draw_segment(jax.random.fold_in(keys[12], 71), 0),
        "parent": draw_parent(jax.random.fold_in(keys[12], 71), 0),
        "gain_attn": jnp.clip(1.0 + 0.1 * jax.random.normal(keys[4], (D,), jnp.float32), 0.5, 1.5).astype(jnp.bfloat16),
        "qkv_weight": centred(keys[5], (D, QKV), D ** -0.5, 0.15625, ((0, 4), (1, 2))),
        "qkv_bias": centred(keys[6], (QKV,), 0.1, 0.59765625, ((0, 2),)),
        "out_weight": centred(keys[7], (D, HEADS * HEAD), (max(1, HEADS * HEAD * 16 // SLOTS)) ** -0.5, 2.5, ((0, 4), (1, 2))),
        "gain_ffn": jnp.clip(1.0 + 0.1 * jax.random.normal(keys[8], (D,), jnp.float32), 0.5, 1.5).astype(jnp.bfloat16),
        "gate_weight": centred(keys[9], (D, FF), D ** -0.5, 0.15625, ((0, 4), (1, 2))),
        "up_weight": centred(keys[10], (D, FF), D ** -0.5, 0.15625, ((0, 4), (1, 2))),
        "down_weight": centred(keys[11], (D, FF), (FF // 4) ** -0.5, 0.125, ((0, 4), (1, 2))),
    }


EPSILON = 1e-06
THETA = 1000000.0
CLIP_BOUND = 4.0
NEG_FILL = -1e+30
PRECISE = lax.Precision.HIGHEST

@jax.custom_vjp
def low(v):
    return lax.optimization_barrier(v.astype(jnp.bfloat16)).astype(jnp.float32)

@jax.custom_vjp
def low_back(v):
    return v

def low_keep(v):
    return (low(v), None)

def low_pass(kept, grad):
    return (grad,)

def back_keep(v):
    return (v, None)

def back_low(kept, grad):
    return (low(grad),)
low.defvjp(low_keep, low_pass)
low_back.defvjp(back_keep, back_low)

def tree_tables(seg_row, parent_row):
    seg_count = parent_row.shape[0]
    seg_ids = jnp.arange(seg_count, dtype=jnp.int32)
    slot_ids = jnp.arange(seg_row.shape[0], dtype=jnp.int32)
    one_hot = (seg_row[:, None] == seg_ids[None, :]).astype(jnp.int32)
    lengths = lax.optimization_barrier(jnp.sum(one_hot, axis=0, dtype=jnp.int32))
    starts = jnp.cumsum(lengths, dtype=jnp.int32) - lengths
    parent_link = ((parent_row[:, None] == seg_ids[None, :]) & (parent_row[:, None] != seg_ids[:, None])).astype(jnp.int32)
    padding = (parent_row == seg_ids).astype(jnp.int32)
    strict = jnp.minimum(parent_link + jnp.dot(parent_link, parent_link), 1)
    reachable = jnp.minimum(strict + jnp.diag(1 - padding), 1)
    offsets = jnp.dot(strict, lengths) - starts
    positions = jnp.dot(one_hot, offsets) + slot_ids
    return (one_hot, reachable, positions)

def visible(reach_rows, row_ids, hot_cols, col_ids):
    linked = jnp.dot(reach_rows, hot_cols.T) > 0
    before = col_ids[None, :] <= row_ids[:, None]
    diagonal = col_ids[None, :] == row_ids[:, None]
    return linked & before | diagonal

def rotate(values_in, positions, direction):
    head_dim = values_in.shape[-1]
    half_dim = head_dim // 2
    frequency = THETA ** (-2.0 * jnp.arange(half_dim, dtype=jnp.float32) / head_dim)
    angles = positions.astype(jnp.float32)[:, None] * frequency[None, :]
    view_shape = (angles.shape[0],) + (1,) * (values_in.ndim - 2) + (half_dim,)
    cosine = jnp.cos(angles).reshape(view_shape)
    sine_part = direction * jnp.sin(angles).reshape(view_shape)
    first_half = values_in[..., :half_dim]
    second = values_in[..., half_dim:]
    return jnp.concatenate([first_half * cosine - second * sine_part, second * cosine + first_half * sine_part], axis=-1)

def rms_norm(values_in):
    return values_in * lax.rsqrt(lax.optimization_barrier(jnp.mean(values_in * values_in, axis=-1, keepdims=True)) + EPSILON)

def layer_tree(x_row, seg_row, parent_row, weights):
    gain_attn, qkv_weight, qkv_bias, out_weight, gain_ffn, gate_weight, up_weight, down_weight = weights
    slot_count = x_row.shape[0]
    one_hot, reachable, positions = tree_tables(seg_row, parent_row)
    slot_ids = jnp.arange(slot_count, dtype=jnp.int32)
    hidden_one = low(rms_norm(x_row) * gain_attn)
    mixed = low_back(jnp.dot(hidden_one, qkv_weight, precision=PRECISE) + qkv_bias)
    per_group = HEADS // KV_HEADS
    mixed = mixed.reshape(slot_count, KV_HEADS, (per_group + 2) * HEAD)
    queries = low(rotate(mixed[:, :, :per_group * HEAD].reshape(slot_count, KV_HEADS, per_group, HEAD), positions, 1.0))
    keys_all = low(rotate(mixed[:, :, per_group * HEAD:(per_group + 1) * HEAD], positions, 1.0))
    values_all = low(mixed[:, :, (per_group + 1) * HEAD:])
    block_len = math.gcd(slot_count, 512)
    score_scale = HEAD ** (-0.5)

    def attend(tree_item):
        query_blk, begin_at = tree_item
        row_ids = begin_at + jnp.arange(block_len, dtype=jnp.int32)
        reach_rows = jnp.dot(lax.dynamic_slice_in_dim(one_hot, begin_at, block_len, 0), reachable)
        seen_mask = visible(reach_rows, row_ids, one_hot, slot_ids)
        scores = low_back(jnp.einsum('ikgd,jkd->kgij', query_blk, keys_all, precision=PRECISE) * score_scale)
        masked = jnp.where(seen_mask[None, None], scores, NEG_FILL)
        peak_blk = lax.optimization_barrier(jnp.max(masked, axis=(2, 3)))
        log_norm = jax.nn.logsumexp(masked, axis=-1, keepdims=True)
        softmax_w = low(jnp.exp(masked - log_norm))
        attended = jnp.einsum('kgij,jkd->ikgd', softmax_w, values_all, precision=PRECISE)
        return (attended, peak_blk)
    blocks = queries.reshape(slot_count // block_len, block_len, KV_HEADS, per_group, HEAD)
    begins = jnp.arange(slot_count // block_len, dtype=jnp.int32) * block_len
    attended, peak_blocks = lax.map(jax.checkpoint(attend), (blocks, begins))
    attended = low(low_back(attended.reshape(slot_count, HEADS * HEAD)))
    branch = low_back(jnp.dot(attended, out_weight.T, precision=PRECISE))
    mid = x_row + branch
    hidden_two = low(rms_norm(mid) * gain_ffn)
    gate_pre = low_back(jnp.dot(hidden_two, gate_weight, precision=PRECISE))
    up_pre = low_back(jnp.dot(hidden_two, up_weight, precision=PRECISE))
    inner_act = low(jax.nn.silu(gate_pre) * up_pre)
    ffn_out = low_back(jnp.dot(inner_act, down_weight.T, precision=PRECISE))
    return (mid + ffn_out, lax.optimization_barrier(jnp.max(peak_blocks, axis=0)).reshape(HEADS))

def reference(tokens, cotangent, segment, parent, gain_attn, qkv_weight, qkv_bias, out_weight, gain_ffn, gate_weight, up_weight, down_weight):
    tree_count = segment.shape[0]
    slot_count = segment.shape[1]
    model_width = tokens.shape[1]
    inputs = tokens.astype(jnp.float32).reshape(tree_count, slot_count, model_width)
    weights = tuple((weight_in.astype(jnp.float32) for weight_in in (gain_attn, qkv_weight, qkv_bias, out_weight, gain_ffn, gate_weight, up_weight, down_weight)))

    def forward(inputs_all, weights_all):

        def one_tree(tree_item):
            return layer_tree(tree_item[0], tree_item[1], tree_item[2], weights_all)
        results, peak_trees = lax.map(jax.checkpoint(one_tree), (inputs_all, segment, parent))
        return (results, lax.optimization_barrier(jnp.max(peak_trees, axis=0)))
    results, pullback, peak_all = jax.vjp(forward, inputs, weights, has_aux=True)
    grad_inputs, grad_weights = pullback(cotangent.astype(jnp.float32).reshape(tree_count, slot_count, model_width))
    clip_out = CLIP_BOUND / jnp.maximum(peak_all, CLIP_BOUND)
    output = results.reshape(tree_count * slot_count, model_width).astype(jnp.bfloat16)
    input_grad = grad_inputs.reshape(tree_count * slot_count, model_width)
    return (output, input_grad, grad_weights[0], grad_weights[1], grad_weights[2], grad_weights[3], grad_weights[4], grad_weights[5], grad_weights[6], grad_weights[7], clip_out)
```

```python
import functools
import math

import jax
import jax.numpy as jnp
from jax import lax
from jax.experimental import pallas as pl
from jax.experimental.pallas import tpu as pltpu
from jax.sharding import PartitionSpec as P

HEAD = 128
EPSILON = 1e-06
THETA = 1000000.0
CLIP_BOUND = 4.0
NEG_FILL = -1e30
SCALE = HEAD ** (-0.5)
SCALE_2 = SCALE * math.log2(math.e)
MIB = 1 << 20
BF16 = jnp.bfloat16
F32 = jnp.float32


def dot_nt(left, right):
    return lax.dot_general(left, right, (((1,), (1,)), ((), ())), preferred_element_type=F32)


def dot_nn(left, right):
    return jnp.dot(left, right, preferred_element_type=F32)


def seen_block(hot, reach_rows, col_at, row_at, bk, bq):
    linked = dot_nt(hot, reach_rows) > 0.5
    cols = col_at + lax.broadcasted_iota(jnp.int32, (bk, bq), 0)
    rows = row_at + lax.broadcasted_iota(jnp.int32, (bk, bq), 1)
    return (linked & (cols <= rows)) | (cols == rows)


def attention_forward_kernel(
    group, bq, bk, blocks, count, chosen, places, q_ref, kv_ref, reach_ref, hot_ref,
    out_ref, lse_ref, top_ref, max_s, sum_s, acc_s,
):
    row_block = pl.program_id(0)
    max_s[...] = jnp.full_like(max_s, NEG_FILL)
    sum_s[...] = jnp.zeros_like(sum_s)
    acc_s[...] = jnp.zeros_like(acc_s)
    row_at = places[blocks] + row_block * bq

    def body(step, carry):
        block = chosen[row_block * blocks + step]
        here = pl.ds(pl.multiple_of(block * bk, bk), bk)
        keys = kv_ref[here, :HEAD]
        values_t = kv_ref[here, HEAD:].T
        seen = seen_block(hot_ref[here, :], reach_ref[...], places[block], row_at, bk, bq)
        for h in range(group):
            score = jnp.where(seen, dot_nt(keys, q_ref[:, h * HEAD : (h + 1) * HEAD]), NEG_FILL)
            old = max_s[h : h + 1, :]
            new = jnp.maximum(old, jnp.max(score, axis=0, keepdims=True))
            prob = jnp.exp2((score - new) * SCALE_2)
            fade = jnp.exp2((old - new) * SCALE_2)
            max_s[h : h + 1, :] = new
            sum_s[h : h + 1, :] = sum_s[h : h + 1, :] * fade + jnp.sum(prob, axis=0, keepdims=True)
            acc_s[h] = acc_s[h] * fade + dot_nn(values_t, prob.astype(BF16))
        return carry

    lax.fori_loop(0, count[row_block], body, 0)
    top_ref[...] = max_s[...] * SCALE
    lse_ref[...] = max_s[...] * SCALE_2 + jnp.log2(sum_s[...])
    for h in range(group):
        out_ref[:, h * HEAD : (h + 1) * HEAD] = (acc_s[h] / sum_s[h : h + 1, :]).T.astype(BF16)


def attention_forward(lists, queries, kv, reach_rows, hot, bq, bk):
    rows, width = queries.shape
    slots = kv.shape[0]
    group = width // HEAD
    whole = lambda *_: (0, 0)
    row = lambda i, *_: (i, 0)
    col = lambda i, *_: (0, i)
    return pl.pallas_call(
        functools.partial(attention_forward_kernel, group, bq, bk, slots // bk),
        grid_spec=pltpu.PrefetchScalarGridSpec(
            num_scalar_prefetch=3,
            grid=(rows // bq,),
            in_specs=[
                pl.BlockSpec((bq, width), row),
                pl.BlockSpec((slots, 2 * HEAD), whole),
                pl.BlockSpec((bq, HEAD), row),
                pl.BlockSpec((slots, HEAD), whole),
            ],
            out_specs=[
                pl.BlockSpec((bq, width), row),
                pl.BlockSpec((group, bq), col),
                pl.BlockSpec((group, bq), col),
            ],
            scratch_shapes=[
                pltpu.VMEM((group, bq), F32),
                pltpu.VMEM((group, bq), F32),
                pltpu.VMEM((group, HEAD, bq), F32),
            ],
        ),
        out_shape=[
            jax.ShapeDtypeStruct((rows, width), BF16),
            jax.ShapeDtypeStruct((group, rows), F32),
            jax.ShapeDtypeStruct((group, rows), F32),
        ],
        compiler_params=pltpu.CompilerParams(vmem_limit_bytes=32 * MIB),
        cost_estimate=pl.CostEstimate(
            flops=18_000_000_000, bytes_accessed=8_000_000, transcendentals=0
        ),
        name="attention_forward",
    )(*lists, queries, kv, reach_rows, hot)


def attention_backward_kernel(
    group, bq, bk, blocks, count, chosen, places, q_ref, do_ref, lse_ref, delta_ref, kv_ref,
    reach_ref, hot_ref, cos_ref, sin_ref, dq_ref, dkv_ref, acc_s, dk_s, dv_s,
):
    row_block = pl.program_id(0)

    @pl.when(row_block == 0)
    def _():
        dk_s[...] = jnp.zeros_like(dk_s)
        dv_s[...] = jnp.zeros_like(dv_s)

    acc_s[...] = jnp.zeros_like(acc_s)
    row_at = places[blocks] + row_block * bq

    def body(step, carry):
        block = chosen[row_block * blocks + step]
        here = pl.ds(pl.multiple_of(block * bk, bk), bk)
        keys = kv_ref[here, :HEAD]
        values = kv_ref[here, HEAD:]
        keys_t = keys.T
        seen = seen_block(hot_ref[here, :], reach_ref[...], places[block], row_at, bk, bq)
        dk = jnp.zeros((bk, HEAD), F32)
        dv = jnp.zeros((bk, HEAD), F32)
        for h in range(group):
            qh = q_ref[:, h * HEAD : (h + 1) * HEAD]
            doh = do_ref[:, h * HEAD : (h + 1) * HEAD]
            prob = jnp.where(
                seen, jnp.exp2(dot_nt(keys, qh) * SCALE_2 - lse_ref[h : h + 1, :]), 0.0
            )
            ds = (prob * (dot_nt(values, doh) - delta_ref[h : h + 1, :])).astype(BF16)
            dv = dv + dot_nn(prob.astype(BF16), doh)
            dk = dk + dot_nn(ds, qh)
            acc_s[h] = acc_s[h] + dot_nn(keys_t, ds)
        dk_s[here, :] += dk
        dv_s[here, :] += dv
        return carry

    lax.fori_loop(0, count[row_block], body, 0)
    for h in range(group):
        d_query = (acc_s[h] * SCALE).T
        dq_ref[:, h * HEAD : (h + 1) * HEAD] = turned(
            d_query, cos_ref[...], -sin_ref[...]
        ).astype(BF16)

    @pl.when(row_block == pl.num_programs(0) - 1)
    def _():
        dkv_ref[:, :HEAD] = (dk_s[...] * SCALE).astype(BF16)
        dkv_ref[:, HEAD:] = dv_s[...].astype(BF16)


def attention_backward(
    lists, queries, d_att, lse, delta, kv, reach_rows, hot, cosine, sine, bq, bk
):
    rows, width = queries.shape
    slots = kv.shape[0]
    group = width // HEAD
    whole = lambda *_: (0, 0)
    row = lambda i, *_: (i, 0)
    col = lambda i, *_: (0, i)
    return pl.pallas_call(
        functools.partial(attention_backward_kernel, group, bq, bk, slots // bk),
        grid_spec=pltpu.PrefetchScalarGridSpec(
            num_scalar_prefetch=3,
            grid=(rows // bq,),
            in_specs=[
                pl.BlockSpec((bq, width), row),
                pl.BlockSpec((bq, width), row),
                pl.BlockSpec((group, bq), col),
                pl.BlockSpec((group, bq), col),
                pl.BlockSpec((slots, 2 * HEAD), whole),
                pl.BlockSpec((bq, HEAD), row),
                pl.BlockSpec((slots, HEAD), whole),
                pl.BlockSpec((bq, HEAD), row),
                pl.BlockSpec((bq, HEAD), row),
            ],
            out_specs=[
                pl.BlockSpec((bq, width), row),
                pl.BlockSpec((slots, 2 * HEAD), whole),
            ],
            scratch_shapes=[
                pltpu.VMEM((group, HEAD, bq), F32),
                pltpu.VMEM((slots, HEAD), F32),
                pltpu.VMEM((slots, HEAD), F32),
            ],
        ),
        out_shape=[
            jax.ShapeDtypeStruct((rows, width), BF16),
            jax.ShapeDtypeStruct((slots, 2 * HEAD), BF16),
        ],
        compiler_params=pltpu.CompilerParams(vmem_limit_bytes=40 * MIB),
        cost_estimate=pl.CostEstimate(
            flops=32_000_000_000, bytes_accessed=12_000_000, transcendentals=0
        ),
        name="attention_backward",
    )(*lists, queries, d_att, lse, delta, kv, reach_rows, hot, cosine, sine)


def join(mine, pieces, joined, at_col=None):
    depth, cols = pieces[0].shape
    where = slice(None) if at_col is None else pl.ds(pl.multiple_of(at_col, HEAD), cols)
    for j, piece in enumerate(pieces):
        joined[pl.ds(pl.multiple_of((mine ^ j) * depth, 16), depth), where] = piece[...]


def whole_block(*_):
    return (0, 0)


def row_block(i, *_):
    return (i, 0)


def col_block(i, *_):
    return (0, i)


def once(shape):
    return pl.BlockSpec(shape, whole_block, pipeline_mode=pl.Buffered(1))


def call(kernel, grid, in_specs, out_specs, out_shape, scratch, vmem, flops, size, name):
    return pl.pallas_call(
        kernel,
        grid_spec=pltpu.PrefetchScalarGridSpec(
            num_scalar_prefetch=1,
            grid=(grid,),
            in_specs=in_specs,
            out_specs=out_specs,
            scratch_shapes=scratch,
        ),
        out_shape=out_shape,
        compiler_params=pltpu.CompilerParams(vmem_limit_bytes=vmem * MIB),
        cost_estimate=pl.CostEstimate(flops=flops, bytes_accessed=size, transcendentals=0),
        name=name,
    )


def shape(dims, dtype):
    return jax.ShapeDtypeStruct(dims, dtype)


def ffn_middle_kernel(parts, tail, place, h_ref, c_ref, *refs):
    gates, ups, downs = refs[:parts], refs[parts : 2 * parts], refs[2 * parts : 3 * parts]
    act_ref, dg_ref, du_ref, dh_ref, gate_s, up_s, down_s, sum_s = refs[3 * parts :]
    step = pl.program_id(0)
    join(place[0], gates, gate_s)
    join(place[0], ups, up_s)
    join(place[0], downs, down_s)
    if tail:

        @pl.when(step == pl.num_programs(0) - 1)
        def _():
            for joined in (gate_s, up_s, down_s):
                joined[:, tail:] = jnp.zeros_like(joined[:, tail:])

    gate = dot_nn(h_ref[...], gate_s[...])
    up = dot_nn(h_ref[...], up_s[...])
    d_act = dot_nn(c_ref[...], down_s[...])
    sig = jax.nn.sigmoid(gate)
    silu = gate * sig
    act_ref[...] = (silu * up).astype(BF16)
    d_gate = (d_act * up * sig * (1.0 + gate * (1.0 - sig))).astype(BF16)
    d_up = (d_act * silu).astype(BF16)
    dg_ref[...] = d_gate
    du_ref[...] = d_up

    @pl.when(step == 0)
    def _():
        sum_s[...] = jnp.zeros_like(sum_s)

    sum_s[...] += dot_nt(d_gate, gate_s[...]) + dot_nt(d_up, up_s[...])

    @pl.when(step == pl.num_programs(0) - 1)
    def _():
        dh_ref[...] = sum_s[...].astype(BF16)


def ffn_middle(place, hidden, cotangent, gates, ups, downs, tf):
    rows, width = hidden.shape
    depth, units = gates[0].shape
    parts = len(gates)
    return call(
        functools.partial(ffn_middle_kernel, parts, units % tf),
        pl.cdiv(units, tf),
        [once((rows, width))] * 2 + [pl.BlockSpec((depth, tf), col_block)] * (3 * parts),
        [pl.BlockSpec((rows, tf), col_block)] * 3 + [once((rows, width))],
        [shape((rows, units), BF16)] * 3 + [shape((rows, width), BF16)],
        [pltpu.VMEM((width, tf), BF16)] * 3 + [pltpu.VMEM((rows, width), F32)],
        60,
        10 * rows * width * units,
        6 * width * units + 6 * rows * units,
        "ffn_middle",
    )(place, hidden, cotangent, *gates, *ups, *downs)


def weight_grad_kernel(depth, parts, place, left_ref, right_ref, keep_ref, send_ref):
    for j in range(parts):
        half = keep_ref if j % 2 == 0 else send_ref
        rows = pl.ds(pl.multiple_of((place[0] ^ j) * depth, 16), depth)
        at = (j // 2) * depth
        half[at : at + depth, :] = dot_nn(left_ref[rows, :], right_ref[...]).astype(BF16)


def weight_grad(place, left_t, right, parts, tf):
    width, rows = left_t.shape
    units = right.shape[1]
    return call(
        functools.partial(weight_grad_kernel, width // parts, parts),
        pl.cdiv(units, tf),
        [once((width, rows)), pl.BlockSpec((rows, tf), col_block)],
        [pl.BlockSpec((width // 2, tf), col_block)] * 2,
        [shape((width // 2, units), BF16)] * 2,
        [],
        48,
        2 * rows * width * units,
        2 * width * units + 2 * rows * units,
        "weight_grad",
    )(place, left_t, right)


def down_project_kernel(parts, place, act_ref, *refs):
    downs, (out_ref, down_s, sum_s) = refs[:parts], refs[parts:]
    step = pl.program_id(0)
    join(place[0], downs, down_s)

    @pl.when(step == 0)
    def _():
        sum_s[...] = jnp.zeros_like(sum_s)

    sum_s[...] += dot_nt(act_ref[...], down_s[...])

    @pl.when(step == pl.num_programs(0) - 1)
    def _():
        out_ref[...] = sum_s[...].astype(BF16)


def down_project(place, act, downs, tf):
    rows, units = act.shape
    parts = len(downs)
    depth = downs[0].shape[0]
    width = depth * parts
    return call(
        functools.partial(down_project_kernel, parts),
        units // tf,
        [pl.BlockSpec((rows, tf), col_block)] + [pl.BlockSpec((depth, tf), col_block)] * parts,
        once((rows, width)),
        shape((rows, width), BF16),
        [pltpu.VMEM((width, tf), BF16), pltpu.VMEM((rows, width), F32)],
        48,
        2 * rows * width * units,
        2 * width * units + 2 * rows * units,
        "down_project",
    )(place, act, *downs)


def inverse_rms(values):
    return lax.rsqrt(jnp.mean(values * values, axis=-1, keepdims=True) + EPSILON)


def turned(values, cosine, sine):
    return values * cosine + pltpu.roll(values, HEAD // 2, 1) * sine


def mix_kernel(parts, group, place, x_ref, gain_ref, bias_ref, cos_ref, sin_ref, *refs):
    pieces, (q_ref, kv_ref, ht_ref, weight_s) = refs[:parts], refs[parts:]

    @pl.when(pl.program_id(0) == 0)
    def _():
        join(place[0], pieces, weight_s)

    x = x_ref[...].astype(F32)
    hidden = (x * inverse_rms(x) * gain_ref[...].astype(F32)).astype(BF16)
    ht_ref[...] = hidden.T
    mixed = dot_nn(hidden, weight_s[...]) + bias_ref[...].astype(F32)
    cosine, sine = cos_ref[...], sin_ref[...]
    for h in range(group):
        at = slice(h * HEAD, (h + 1) * HEAD)
        q_ref[:, at] = turned(mixed[:, at], cosine, sine).astype(BF16)
    split = group * HEAD
    kv_ref[:, :HEAD] = turned(mixed[:, split : split + HEAD], cosine, sine).astype(BF16)
    kv_ref[:, HEAD:] = mixed[:, split + HEAD :].astype(BF16)


def mix(place, tokens, gain, bias, cosine, sine, pieces, group, bq):
    rows, width = tokens.shape
    depth, cols = pieces[0].shape
    parts = len(pieces)
    return call(
        functools.partial(mix_kernel, parts, group),
        rows // bq,
        [
            pl.BlockSpec((bq, width), row_block),
            once((1, width)),
            once((1, cols)),
            pl.BlockSpec((bq, HEAD), row_block),
            pl.BlockSpec((bq, HEAD), row_block),
        ]
        + [once((depth, cols))] * parts,
        [
            pl.BlockSpec((bq, group * HEAD), row_block),
            pl.BlockSpec((bq, 2 * HEAD), row_block),
            pl.BlockSpec((width, bq), col_block),
        ],
        [
            shape((rows, group * HEAD), BF16),
            shape((rows, 2 * HEAD), BF16),
            shape((width, rows), BF16),
        ],
        [pltpu.VMEM((width, cols), BF16)],
        32,
        2 * rows * width * cols,
        2 * width * cols + 10 * rows * width,
        "mix",
    )(place, tokens, gain[None], bias[None], cosine, sine, *pieces)


def branch_kernel(parts, place, x_ref, own_ref, other_ref, gain_ref, *refs):
    own_w, other_w = refs[:parts], refs[parts : 2 * parts]
    mid_ref, h_ref, ht_ref, weight_s, att_s = refs[2 * parts :]
    split = own_ref.shape[1]
    own_at = pl.multiple_of(place[1] * split, HEAD)
    other_at = pl.multiple_of((1 - place[1]) * split, HEAD)

    @pl.when(pl.program_id(0) == 0)
    def _():
        join(place[0], own_w, weight_s, own_at)
        join(place[0], other_w, weight_s, other_at)

    att_s[:, pl.ds(own_at, split)] = own_ref[...]
    att_s[:, pl.ds(other_at, split)] = other_ref[...]
    mid = x_ref[...].astype(F32) + dot_nt(att_s[...], weight_s[...])
    mid_ref[...] = mid
    hidden = (mid * inverse_rms(mid) * gain_ref[...].astype(F32)).astype(BF16)
    h_ref[...] = hidden
    ht_ref[...] = hidden.T


def branch(place, tokens, own, other, gain, own_pieces, other_pieces, bq):
    rows, width = tokens.shape
    depth, cols = own_pieces[0].shape
    parts = len(own_pieces)
    wide = pl.BlockSpec((bq, width), row_block)
    narrow = pl.BlockSpec((bq, cols), row_block)
    return call(
        functools.partial(branch_kernel, parts),
        rows // bq,
        [wide, narrow, narrow, once((1, width))] + [once((depth, cols))] * (2 * parts),
        [wide, wide, pl.BlockSpec((width, bq), col_block)],
        [shape((rows, width), F32), shape((rows, width), BF16), shape((width, rows), BF16)],
        [pltpu.VMEM((width, 2 * cols), BF16), pltpu.VMEM((bq, 2 * cols), BF16)],
        40,
        4 * rows * width * cols,
        4 * width * cols + 14 * rows * width,
        "branch",
    )(place, tokens, own, other, gain[None], *own_pieces, *other_pieces)


def middle_back_kernel(
    parts, group, place, own_ref, other_ref, mid_ref, c_ref, gain_ref, att_ref, *refs
):
    pieces, (dm_ref, dbt_ref, da_ref, delta_ref, dgain_ref, weight_s) = refs[:parts], refs[parts:]

    @pl.when(pl.program_id(0) == 0)
    def _():
        join(place[0], pieces, weight_s)
        dgain_ref[...] = jnp.zeros_like(dgain_ref)

    mid = mid_ref[...]
    inverse = inverse_rms(mid)
    normed = mid * inverse
    own = own_ref[...].astype(F32)
    dgain_ref[...] += jnp.sum(own * normed, axis=0, keepdims=True)
    scaled = (own + other_ref[...].astype(F32)) * gain_ref[...].astype(F32)
    d_mid = c_ref[...].astype(F32) + inverse * (
        scaled - normed * jnp.mean(scaled * normed, axis=-1, keepdims=True)
    )
    dm_ref[...] = d_mid
    d_branch = d_mid.astype(BF16)
    dbt_ref[...] = d_branch.T
    d_att = dot_nn(d_branch, weight_s[...]).astype(BF16)
    da_ref[...] = d_att
    product = d_att.astype(F32) * att_ref[...].astype(F32)
    for h in range(group):
        delta_ref[h : h + 1, :] = jnp.sum(
            product[:, h * HEAD : (h + 1) * HEAD].T, axis=0, keepdims=True
        )


def middle_back(place, own, other, mid, cotangent, gain, attended, pieces, bq):
    rows, width = mid.shape
    depth, cols = pieces[0].shape
    parts = len(pieces)
    group = cols // HEAD
    wide = pl.BlockSpec((bq, width), row_block)
    narrow = pl.BlockSpec((bq, cols), row_block)
    return call(
        functools.partial(middle_back_kernel, parts, group),
        rows // bq,
        [wide, wide, wide, wide, once((1, width)), narrow] + [once((depth, cols))] * parts,
        [
            wide,
            pl.BlockSpec((width, bq), col_block),
            narrow,
            pl.BlockSpec((group, bq), col_block),
            pl.BlockSpec((1, width), whole_block),
        ],
        [
            shape((rows, width), F32),
            shape((width, rows), BF16),
            shape((rows, cols), BF16),
            shape((group, rows), F32),
            shape((1, width), F32),
        ],
        [pltpu.VMEM((width, cols), BF16)],
        48,
        2 * rows * width * cols,
        2 * width * cols + 18 * rows * width,
        "middle_back",
    )(place, own, other, mid, cotangent, gain[None], attended, *pieces)


def mix_back_kernel(
    parts, group, place, dq_ref, dkv_ref, cos_ref, sin_ref, x_ref, *refs
):
    pieces, (dm_ref, dh_ref, dbias_ref, dgain_ref, weight_s) = refs[:parts], refs[parts:]

    @pl.when(pl.program_id(0) == 0)
    def _():
        join(place[0], pieces, weight_s)
        dgain_ref[...] = jnp.zeros_like(dgain_ref)
        dbias_ref[...] = jnp.zeros_like(dbias_ref)

    split = group * HEAD
    dm_ref[:, :split] = dq_ref[...]
    d_keys = dkv_ref[:, :HEAD].astype(F32)
    dm_ref[:, split : split + HEAD] = turned(d_keys, cos_ref[...], -sin_ref[...]).astype(BF16)
    dm_ref[:, split + HEAD :] = dkv_ref[:, HEAD:]
    d_mixed = dm_ref[...]
    dbias_ref[...] += jnp.sum(d_mixed.astype(F32), axis=0, keepdims=True)
    d_hidden = dot_nt(d_mixed, weight_s[...])
    x = x_ref[...].astype(F32)
    dgain_ref[...] += jnp.sum(d_hidden * (x * inverse_rms(x)), axis=0, keepdims=True)
    dh_ref[...] = d_hidden.astype(BF16)


def mix_back(place, dq, dkv, cosine, sine, tokens, pieces, bq):
    rows, width = tokens.shape
    depth, cols = pieces[0].shape
    parts = len(pieces)
    group = dq.shape[1] // HEAD
    wide = pl.BlockSpec((bq, width), row_block)
    return call(
        functools.partial(mix_back_kernel, parts, group),
        rows // bq,
        [
            pl.BlockSpec((bq, group * HEAD), row_block),
            pl.BlockSpec((bq, 2 * HEAD), row_block),
            pl.BlockSpec((bq, HEAD), row_block),
            pl.BlockSpec((bq, HEAD), row_block),
            wide,
        ]
        + [once((depth, cols))] * parts,
        [
            pl.BlockSpec((bq, cols), row_block),
            wide,
            pl.BlockSpec((1, cols), whole_block),
            pl.BlockSpec((1, width), whole_block),
        ],
        [
            shape((rows, cols), BF16),
            shape((rows, width), BF16),
            shape((1, cols), F32),
            shape((1, width), F32),
        ],
        [pltpu.VMEM((width, cols), BF16)],
        32,
        2 * rows * width * cols,
        2 * width * cols + 8 * rows * width,
        "mix_back",
    )(place, dq, dkv, cosine, sine, tokens, *pieces)


def input_back_kernel(place, own_ref, other_ref, x_ref, gain_ref, dm_ref, out_ref):
    x = x_ref[...].astype(F32)
    inverse = inverse_rms(x)
    normed = x * inverse
    scaled = (own_ref[...].astype(F32) + other_ref[...].astype(F32)) * gain_ref[...].astype(F32)
    out_ref[...] = dm_ref[...] + inverse * (
        scaled - normed * jnp.mean(scaled * normed, axis=-1, keepdims=True)
    )


def input_back(place, own, other, tokens, gain, d_mid, bq):
    rows, width = tokens.shape
    wide = pl.BlockSpec((bq, width), row_block)
    return call(
        input_back_kernel,
        rows // bq,
        [wide, wide, wide, once((1, width)), wide],
        wide,
        shape((rows, width), F32),
        [],
        32,
        20 * rows * width,
        14 * rows * width,
        "input_back",
    )(place, own, other, tokens, gain[None], d_mid)


def after(values, *first):
    return lax.optimization_barrier((values, first))[0]


def swap(value, axis, size, bit):
    return lax.ppermute(value, axis, [(i, i ^ bit) for i in range(size)])


def gather_pieces(own, size):
    pieces = {0: own}
    bit = size // 2
    while bit:
        pieces.update({j ^ bit: swap(p, "shard", size, bit) for j, p in pieces.items()})
        bit //= 2
    return [pieces[j] for j in range(size)]


def sum_over_ctx(value, size):
    if size != 4:
        return lax.psum(value, "ctx").astype(F32)
    place = lax.axis_index("ctx")
    inner = value + lax.ppermute(value, "ctx", [(0, 1), (3, 2)])
    total = inner + lax.ppermute(inner, "ctx", [(1, 2), (2, 1)])
    outer = lax.ppermute(total, "ctx", [(1, 0), (2, 3)])
    middle = (place == 1) | (place == 2)
    return jnp.where(middle, total, outer).astype(F32)


def reduce_rows(halves, shards, contexts):
    keep, send = halves
    held = [keep, swap(send, "shard", shards, 1)]
    bit = 2
    while bit < shards:
        count = shards // bit
        size = keep.shape[0] // (bit // 2) // count

        def pick(odd):
            return [
                sum(part[at * size : (at + 1) * size] for part in held)
                for at in range(odd, count, 2)
            ]

        away, here = pick(1), pick(0)
        away = away[0] if len(away) == 1 else jnp.concatenate(away, axis=0)
        here = here[0] if len(here) == 1 else jnp.concatenate(here, axis=0)
        held = [here, swap(away, "shard", shards, bit)]
        bit *= 2
    return sum_over_ctx(sum(held), contexts)


def sum_of_all(value, sizes):
    for axis, size in sizes.items():
        bit = 1
        while bit < size:
            value = value + swap(value, axis, size, bit)
            bit *= 2
    return value


def tree_tables(seg_row, parent_row):
    seg_count = parent_row.shape[0]
    seg_ids = jnp.arange(seg_count, dtype=jnp.int32)
    one_hot = (seg_row[:, None] == seg_ids[None, :]).astype(jnp.int32)
    lengths = jnp.sum(one_hot, axis=0, dtype=jnp.int32)
    before = seg_ids[None, :] < seg_ids[:, None]
    starts = jnp.sum(jnp.where(before, lengths[None, :], 0), axis=1, dtype=jnp.int32)
    link = (parent_row[:, None] == seg_ids[None, :]) & (parent_row[:, None] != seg_ids[:, None])
    twice = jnp.any(link[:, :, None] & link[None, :, :], axis=1)
    strict = link | twice
    padding = parent_row == seg_ids
    reach = strict | ((seg_ids[:, None] == seg_ids[None, :]) & ~padding[:, None])
    offsets = jnp.sum(jnp.where(strict, lengths[None, :], 0), axis=1, dtype=jnp.int32) - starts
    return reach, offsets


def block_lists(row_hot, col_hot, reach, col_places, row_first, bq, bk):
    segs = reach.shape[0]
    row_has = jnp.any(row_hot.reshape(-1, bq, segs), axis=1)
    col_has = jnp.any(col_hot.reshape(-1, bk, segs), axis=1)
    row_blocks, col_blocks = row_has.shape[0], col_has.shape[0]
    row_reach = jnp.any(row_has[:, :, None] & reach[None], axis=1)
    meets = jnp.any(row_reach[:, None, :] & col_has[None], axis=2)
    col_at = col_places.reshape(-1, bk)[:, 0]
    row_at = row_first + bq * jnp.arange(row_blocks, dtype=jnp.int32)
    causal = col_at[None, :] < row_at[:, None] + bq
    diagonal = causal & (col_at[None, :] + bk > row_at[:, None])
    active = ((meets & causal) | diagonal) & (col_at >= 0)[None, :]
    ids = jnp.arange(col_blocks, dtype=jnp.int32)
    rank = jnp.sum(
        (active[:, None, :] & (ids[None, :] < ids[:, None])[None]).astype(jnp.int32), axis=2
    )
    placed = active[:, :, None] & (rank[:, :, None] == ids[None, None, :])
    chosen = jnp.sum(jnp.where(placed, ids[None, :, None], 0), axis=1, dtype=jnp.int32)
    count = jnp.sum(active.astype(jnp.int32), axis=1, dtype=jnp.int32)
    places = jnp.concatenate([col_at, row_first[None]])
    return count, chosen.reshape(-1), places


def layer(
    sizes, tokens, cotangent, segment, parent, gain_attn, qkv_weight, qkv_bias,
    out_weight, gain_ffn, gate_weight, up_weight, down_weight,
):
    shards, contexts, halves = sizes["shard"], sizes["ctx"], sizes["tp"]
    rows, width = tokens.shape
    group = out_weight.shape[1] // HEAD
    shard, ctx, half = lax.axis_index("shard"), lax.axis_index("ctx"), lax.axis_index("tp")
    place = jnp.stack([shard, half]).astype(jnp.int32)
    across = [(i, i ^ 1) for i in range(halves)]

    qkv_pieces = gather_pieces(qkv_weight, shards)
    out_pieces = gather_pieces(after(out_weight, qkv_pieces[-1]), shards)
    gate_pieces = gather_pieces(after(gate_weight, qkv_pieces[-1]), shards)
    up_pieces = gather_pieces(after(up_weight, out_pieces[-1]), shards)
    down_pieces = gather_pieces(after(down_weight, gate_pieces[-1]), shards)
    out_other = [lax.ppermute(piece, "tp", across) for piece in out_pieces]

    row_first = (ctx * rows).astype(jnp.int32)
    reach, offsets = tree_tables(segment[0], parent[0])
    seg_ids = jnp.arange(reach.shape[0], dtype=jnp.int32)
    behind = [jnp.maximum(ctx - k, 0) * rows for k in range(contexts)]
    seg_back = jnp.concatenate(
        [lax.dynamic_slice_in_dim(segment[0], at, rows, 0) for at in behind]
    )
    places_back = jnp.concatenate(
        [(ctx - k) * rows + jnp.arange(rows, dtype=jnp.int32) for k in range(contexts)]
    )
    col_hot = seg_back[:, None] == seg_ids[None, :]
    row_hot = col_hot[:rows]
    own_pos = places_back[:rows] + jnp.sum(
        jnp.where(row_hot, offsets[None, :], 0), axis=1, dtype=jnp.int32
    )
    pad = ((0, 0), (0, HEAD - reach.shape[0]))
    row_reach = jnp.any(row_hot[:, :, None] & reach[None], axis=1)
    reach_rows = jnp.pad(row_reach.astype(BF16), pad)
    hot = jnp.pad(col_hot.astype(BF16), pad)
    bq = math.gcd(rows, 256)
    bk_f, bk_b = math.gcd(rows, 128), math.gcd(rows, 512)
    lists_f = block_lists(row_hot, col_hot, reach, places_back, row_first, bq, bk_f)
    lists_b = block_lists(row_hot, col_hot, reach, places_back, row_first, bq, bk_b)
    lane = jnp.arange(HEAD, dtype=jnp.int32)
    frequency = THETA ** (-2.0 * (lane % (HEAD // 2)).astype(F32) / HEAD)
    angles = own_pos.astype(F32)[:, None] * frequency[None, :]
    cosine = jnp.cos(angles)
    sine = jnp.sin(angles) * jnp.where(lane < HEAD // 2, -1.0, 1.0)

    queries, kv_own, hidden_one_t = mix(
        place, tokens, gain_attn, qkv_bias, cosine, sine, qkv_pieces, group, bq
    )
    rightward = [(i, i + 1) for i in range(contexts - 1)]
    leftward = [(i + 1, i) for i in range(contexts - 1)]
    kv_blocks = [kv_own]
    for _ in range(contexts - 1):
        kv_blocks.append(lax.ppermute(kv_blocks[-1], "ctx", rightward))
    kv_back = jnp.concatenate(kv_blocks, axis=0)
    attended, lse, tops = attention_forward(lists_f, queries, kv_back, reach_rows, hot, bq, bk_f)
    attended_other = lax.ppermute(attended, "tp", across)
    mid, hidden_two, hidden_two_t = branch(
        place, tokens, attended, attended_other, gain_ffn, out_pieces, out_other, bq
    )
    top_grad_t = cotangent.T
    act, d_gate, d_up, d_hidden_two = ffn_middle(
        place, hidden_two, cotangent, gate_pieces, up_pieces, down_pieces, 512
    )

    d_hidden_two_other = lax.ppermute(d_hidden_two, "tp", across)
    gate_halves = weight_grad(place, hidden_two_t, d_gate, shards, 512)
    up_halves = weight_grad(place, after(hidden_two_t, gate_halves), d_up, shards, 512)
    down_halves = weight_grad(place, after(top_grad_t, up_halves), act, shards, 512)
    ffn_own = down_project(place, after(act, down_halves), down_pieces, 896)
    ffn_other = lax.ppermute(ffn_own, "tp", across)
    output = (mid + (ffn_own.astype(F32) + ffn_other.astype(F32))).astype(BF16)
    gate_total = reduce_rows(gate_halves, shards, contexts)
    up_total = reduce_rows(up_halves, shards, contexts)
    down_total = reduce_rows(down_halves, shards, contexts)

    d_hidden_two_other = after(d_hidden_two_other, ffn_own)
    d_mid, d_branch_t, d_att, delta, gain_two_part = middle_back(
        place, d_hidden_two, d_hidden_two_other, mid, cotangent, gain_ffn, attended, out_pieces, bq
    )
    d_query, d_kv = attention_backward(
        lists_b, queries, d_att, lse, delta, kv_back, reach_rows, hot, cosine, sine, bq, bk_b
    )
    d_kv_own = d_kv[(contexts - 1) * rows :]
    for k in range(contexts - 2, -1, -1):
        d_kv_own = d_kv[k * rows : (k + 1) * rows] + lax.ppermute(d_kv_own, "ctx", leftward)
    out_halves = weight_grad(place, after(d_branch_t, d_kv), attended, shards, 768)
    out_total = reduce_rows(out_halves, shards, contexts)
    d_mixed, d_hidden_one, bias_part, gain_one_part = mix_back(
        place, d_query, d_kv_own, cosine, sine, tokens, qkv_pieces, bq
    )
    d_hidden_one_other = lax.ppermute(d_hidden_one, "tp", across)
    qkv_halves = weight_grad(place, hidden_one_t, d_mixed, shards, 512)
    qkv_total = reduce_rows(qkv_halves, shards, contexts)
    input_grad = input_back(place, d_hidden_one, d_hidden_one_other, tokens, gain_attn, d_mid, bq)

    peak_own = jnp.max(tops, axis=1)
    device = shard * contexts + ctx
    spread = jnp.where(
        (jnp.arange(shards * contexts)[:, None, None] == device)
        & (jnp.arange(halves)[None, :, None] == half),
        peak_own[None, None, :],
        0.0,
    )
    bias_both = jnp.where(jnp.arange(halves)[:, None] == half, bias_part, 0.0)
    vector = jnp.concatenate(
        [gain_one_part[0], gain_two_part[0], bias_both.reshape(-1), spread.reshape(-1)]
    )
    vector = sum_of_all(vector, sizes)
    bias_at = 2 * width
    spread_at = bias_at + bias_both.size
    bias_grad = lax.dynamic_slice_in_dim(
        vector[bias_at:spread_at], half * bias_part.size, bias_part.size, 0
    )
    peaks = jnp.max(vector[spread_at:].reshape(shards * contexts, halves, group), axis=0)
    peak_all = lax.dynamic_index_in_dim(peaks, half, 0, keepdims=False)
    clip_out = CLIP_BOUND / jnp.maximum(peak_all, CLIP_BOUND)
    return (
        output,
        input_grad,
        vector[:width],
        qkv_total,
        bias_grad,
        out_total,
        vector[width:bias_at],
        gate_total,
        up_total,
        down_total,
        clip_out,
    )


def solution(mesh):
    token = P(("shard", "ctx"), None)
    weight = P("shard", "tp")
    return jax.shard_map(
        functools.partial(layer, dict(mesh.shape)),
        mesh=mesh,
        in_specs=(
            token,
            token,
            P("shard", None),
            P("shard", None),
            P(),
            weight,
            P("tp"),
            weight,
            P(),
            weight,
            weight,
            weight,
        ),
        out_specs=(
            token,
            token,
            P(),
            weight,
            P("tp"),
            weight,
            P(),
            weight,
            weight,
            weight,
            P("tp"),
        ),
        check_vma=False,
    )
```

```python
import functools
import math

import jax
import jax.numpy as jnp
from jax import lax
from jax.experimental import pallas as pl
from jax.experimental.pallas import tpu as pltpu
from jax.sharding import PartitionSpec as P

HEAD = 128
EPSILON = 1e-06
THETA = 1000000.0
CLIP_BOUND = 4.0
NEG_FILL = -1e30
SCALE = HEAD ** (-0.5)
SCALE_2 = SCALE * math.log2(math.e)
MIB = 1 << 20
CUTS = 3
LONG = pl.CostEstimate(flops=1_000_000_000_000, bytes_accessed=1_000_000, transcendentals=0)
BF16 = jnp.bfloat16
F32 = jnp.float32


def dot_nt(left, right):
    return lax.dot_general(left, right, (((1,), (1,)), ((), ())), preferred_element_type=F32)


def dot_nn(left, right):
    return jnp.dot(left, right, preferred_element_type=F32)


def seen_block(hot, reach_rows, col_at, row_at, bk, bq):
    linked = dot_nt(hot, reach_rows) > 0.5
    cols = col_at + lax.broadcasted_iota(jnp.int32, (bk, bq), 0)
    rows = row_at + lax.broadcasted_iota(jnp.int32, (bk, bq), 1)
    return (linked & (cols <= rows)) | (cols == rows)


def attention_forward_kernel(
    group, bq, bk, blocks, count, chosen, places, q_ref, kv_ref, reach_ref, hot_ref,
    out_ref, lse_ref, top_ref, max_s, sum_s, acc_s,
):
    row_block = pl.program_id(0)
    max_s[...] = jnp.full_like(max_s, NEG_FILL)
    sum_s[...] = jnp.zeros_like(sum_s)
    acc_s[...] = jnp.zeros_like(acc_s)
    row_at = places[blocks] + row_block * bq

    def body(step, carry):
        block = chosen[row_block * blocks + step]
        here = pl.ds(pl.multiple_of(block * bk, bk), bk)
        keys = kv_ref[here, :HEAD]
        values_t = kv_ref[here, HEAD:].T
        seen = seen_block(hot_ref[here, :], reach_ref[...], places[block], row_at, bk, bq)
        for h in range(group):
            score = jnp.where(seen, dot_nt(keys, q_ref[:, h * HEAD : (h + 1) * HEAD]), NEG_FILL)
            old = max_s[h : h + 1, :]
            new = jnp.maximum(old, jnp.max(score, axis=0, keepdims=True))
            prob = jnp.exp2((score - new) * SCALE_2)
            fade = jnp.exp2((old - new) * SCALE_2)
            max_s[h : h + 1, :] = new
            sum_s[h : h + 1, :] = sum_s[h : h + 1, :] * fade + jnp.sum(prob, axis=0, keepdims=True)
            acc_s[h] = acc_s[h] * fade + dot_nn(values_t, prob.astype(BF16))
        return carry

    lax.fori_loop(0, count[row_block], body, 0)
    top_ref[...] = max_s[...] * SCALE
    lse_ref[...] = max_s[...] * SCALE_2 + jnp.log2(sum_s[...])
    for h in range(group):
        out_ref[:, h * HEAD : (h + 1) * HEAD] = (acc_s[h] / sum_s[h : h + 1, :]).T.astype(BF16)


def attention_forward(lists, queries, kv, reach_rows, hot, bq, bk):
    rows, width = queries.shape
    slots = kv.shape[0]
    group = width // HEAD
    whole = lambda *_: (0, 0)
    row = lambda i, *_: (i, 0)
    col = lambda i, *_: (0, i)
    return pl.pallas_call(
        functools.partial(attention_forward_kernel, group, bq, bk, slots // bk),
        grid_spec=pltpu.PrefetchScalarGridSpec(
            num_scalar_prefetch=3,
            grid=(rows // bq,),
            in_specs=[
                pl.BlockSpec((bq, width), row),
                pl.BlockSpec((slots, 2 * HEAD), whole),
                pl.BlockSpec((bq, HEAD), row),
                pl.BlockSpec((slots, HEAD), whole),
            ],
            out_specs=[
                pl.BlockSpec((bq, width), row),
                pl.BlockSpec((group, bq), col),
                pl.BlockSpec((group, bq), col),
            ],
            scratch_shapes=[
                pltpu.VMEM((group, bq), F32),
                pltpu.VMEM((group, bq), F32),
                pltpu.VMEM((group, HEAD, bq), F32),
            ],
        ),
        out_shape=[
            jax.ShapeDtypeStruct((rows, width), BF16),
            jax.ShapeDtypeStruct((group, rows), F32),
            jax.ShapeDtypeStruct((group, rows), F32),
        ],
        compiler_params=pltpu.CompilerParams(vmem_limit_bytes=32 * MIB),
        cost_estimate=LONG,
        name="attention_forward",
    )(*lists, queries, kv, reach_rows, hot)


def attention_backward_kernel(
    group, bq, bk, blocks, count, chosen, places, q_ref, do_ref, lse_ref, delta_ref, kv_ref,
    reach_ref, hot_ref, cos_ref, sin_ref, dq_ref, dkv_ref, acc_s, dk_s, dv_s,
):
    row_block = pl.program_id(0)

    @pl.when(row_block == 0)
    def _():
        dk_s[...] = jnp.zeros_like(dk_s)
        dv_s[...] = jnp.zeros_like(dv_s)

    acc_s[...] = jnp.zeros_like(acc_s)
    row_at = places[blocks] + row_block * bq

    def body(step, carry):
        block = chosen[row_block * blocks + step]
        here = pl.ds(pl.multiple_of(block * bk, bk), bk)
        keys = kv_ref[here, :HEAD]
        values = kv_ref[here, HEAD:]
        keys_t = keys.T
        seen = seen_block(hot_ref[here, :], reach_ref[...], places[block], row_at, bk, bq)
        dk = jnp.zeros((bk, HEAD), F32)
        dv = jnp.zeros((bk, HEAD), F32)
        for h in range(group):
            qh = q_ref[:, h * HEAD : (h + 1) * HEAD]
            doh = do_ref[:, h * HEAD : (h + 1) * HEAD]
            prob = jnp.where(
                seen, jnp.exp2(dot_nt(keys, qh) * SCALE_2 - lse_ref[h : h + 1, :]), 0.0
            )
            ds = (prob * (dot_nt(values, doh) - delta_ref[h : h + 1, :])).astype(BF16)
            dv = dv + dot_nn(prob.astype(BF16), doh)
            dk = dk + dot_nn(ds, qh)
            acc_s[h] = acc_s[h] + dot_nn(keys_t, ds)
        dk_s[here, :] += dk
        dv_s[here, :] += dv
        return carry

    lax.fori_loop(0, count[row_block], body, 0)
    for h in range(group):
        d_query = (acc_s[h] * SCALE).T
        dq_ref[:, h * HEAD : (h + 1) * HEAD] = turned(
            d_query, cos_ref[...], -sin_ref[...]
        ).astype(BF16)

    @pl.when(row_block == pl.num_programs(0) - 1)
    def _():
        dkv_ref[:, :HEAD] = (dk_s[...] * SCALE).astype(BF16)
        dkv_ref[:, HEAD:] = dv_s[...].astype(BF16)


def attention_backward(
    lists, queries, d_att, lse, delta, kv, reach_rows, hot, cosine, sine, bq, bk
):
    rows, width = queries.shape
    slots = kv.shape[0]
    group = width // HEAD
    whole = lambda *_: (0, 0)
    row = lambda i, *_: (i, 0)
    col = lambda i, *_: (0, i)
    return pl.pallas_call(
        functools.partial(attention_backward_kernel, group, bq, bk, slots // bk),
        grid_spec=pltpu.PrefetchScalarGridSpec(
            num_scalar_prefetch=3,
            grid=(rows // bq,),
            in_specs=[
                pl.BlockSpec((bq, width), row),
                pl.BlockSpec((bq, width), row),
                pl.BlockSpec((group, bq), col),
                pl.BlockSpec((group, bq), col),
                pl.BlockSpec((slots, 2 * HEAD), whole),
                pl.BlockSpec((bq, HEAD), row),
                pl.BlockSpec((slots, HEAD), whole),
                pl.BlockSpec((bq, HEAD), row),
                pl.BlockSpec((bq, HEAD), row),
            ],
            out_specs=[
                pl.BlockSpec((bq, width), row),
                pl.BlockSpec((slots, 2 * HEAD), whole),
            ],
            scratch_shapes=[
                pltpu.VMEM((group, HEAD, bq), F32),
                pltpu.VMEM((slots, HEAD), F32),
                pltpu.VMEM((slots, HEAD), F32),
            ],
        ),
        out_shape=[
            jax.ShapeDtypeStruct((rows, width), BF16),
            jax.ShapeDtypeStruct((slots, 2 * HEAD), BF16),
        ],
        compiler_params=pltpu.CompilerParams(vmem_limit_bytes=40 * MIB),
        cost_estimate=LONG,
        name="attention_backward",
    )(*lists, queries, d_att, lse, delta, kv, reach_rows, hot, cosine, sine)


def join(mine, depth, places, pieces, joined, at_col=None):
    cols = pieces[0].shape[1]
    where = slice(None) if at_col is None else pl.ds(pl.multiple_of(at_col, HEAD), cols)
    for (j, row), piece in zip(places, pieces):
        at = pl.multiple_of((mine ^ j) * depth + row, 16)
        joined[pl.ds(at, piece.shape[0]), where] = piece[...]


class Rows:
    def __init__(self, pieces, depth, tf=None):
        self.depth = depth
        self.places = [(j, row) for j, row, _ in pieces]
        self.arrays = [array for _, _, array in pieces]
        if tf is None:
            self.specs = [once(array.shape) for array in self.arrays]
        else:
            self.specs = [pl.BlockSpec((array.shape[0], tf), col_block) for array in self.arrays]

    def __len__(self):
        return len(self.arrays)

    def join(self, mine, refs, joined, at_col=None):
        join(mine, self.depth, self.places, refs, joined, at_col)


def whole_block(*_):
    return (0, 0)


def row_block(i, *_):
    return (i, 0)


def col_block(i, *_):
    return (0, i)


def once(shape):
    return pl.BlockSpec(shape, whole_block, pipeline_mode=pl.Buffered(1))


def call(kernel, grid, in_specs, out_specs, out_shape, scratch, vmem, name):
    return pl.pallas_call(
        kernel,
        grid_spec=pltpu.PrefetchScalarGridSpec(
            num_scalar_prefetch=1,
            grid=(grid,),
            in_specs=in_specs,
            out_specs=out_specs,
            scratch_shapes=scratch,
        ),
        out_shape=out_shape,
        compiler_params=pltpu.CompilerParams(vmem_limit_bytes=vmem * MIB),
        cost_estimate=LONG,
        name=name,
    )


def shape(dims, dtype):
    return jax.ShapeDtypeStruct(dims, dtype)


def clear_tail(tail, *joined):
    if tail:

        @pl.when(pl.program_id(0) == pl.num_programs(0) - 1)
        def _():
            for one in joined:
                one[:, tail:] = jnp.zeros_like(one[:, tail:])


def gate_up_kernel(gates, ups, place, h_ref, *refs):
    gate_refs, refs = refs[: len(gates)], refs[len(gates) :]
    up_refs, refs = refs[: len(ups)], refs[len(ups) :]
    act_ref, by_gate_ref, by_up_ref, gate_s, up_s = refs
    gates.join(place[0], gate_refs, gate_s)
    ups.join(place[0], up_refs, up_s)
    gate = dot_nn(h_ref[...], gate_s[...])
    up = dot_nn(h_ref[...], up_s[...])
    sig = jax.nn.sigmoid(gate)
    silu = gate * sig
    act_ref[...] = (silu * up).astype(BF16)
    by_up_ref[...] = silu.astype(BF16)
    by_gate_ref[...] = (up * sig * (1.0 + gate * (1.0 - sig))).astype(BF16)


def gate_up(place, hidden, gates, ups, depth, tf):
    rows, width = hidden.shape
    units = gates[0][2].shape[1]
    gates, ups = Rows(gates, depth, tf), Rows(ups, depth, tf)
    return call(
        functools.partial(gate_up_kernel, gates, ups),
        pl.cdiv(units, tf),
        [once((rows, width))] + gates.specs + ups.specs,
        [pl.BlockSpec((rows, tf), col_block)] * 3,
        [shape((rows, units), BF16)] * 3,
        [pltpu.VMEM((width, tf), BF16)] * 2,
        60,
        "gate_up",
    )(place, hidden, *gates.arrays, *ups.arrays)


def gate_up_back_kernel(gates, ups, downs, tail, place, c_ref, by_gate_ref, by_up_ref, *refs):
    gate_refs, refs = refs[: len(gates)], refs[len(gates) :]
    up_refs, refs = refs[: len(ups)], refs[len(ups) :]
    down_refs, refs = refs[: len(downs)], refs[len(downs) :]
    dg_ref, du_ref, *dh_refs, gate_s, up_s, down_s, sum_s = refs
    step = pl.program_id(0)
    gates.join(place[0], gate_refs, gate_s)
    ups.join(place[0], up_refs, up_s)
    downs.join(place[0], down_refs, down_s)
    clear_tail(tail, gate_s, up_s, down_s)
    d_act = dot_nn(c_ref[...], down_s[...])
    by_gate, by_up = by_gate_ref[...].astype(F32), by_up_ref[...].astype(F32)
    if tail:
        last = step == pl.num_programs(0) - 1
        inside = lax.broadcasted_iota(jnp.int32, by_gate.shape, 1) < jnp.where(
            last, tail, by_gate.shape[1]
        )
        by_gate = jnp.where(inside, by_gate, 0.0)
        by_up = jnp.where(inside, by_up, 0.0)
    d_gate = (d_act * by_gate).astype(BF16)
    d_up = (d_act * by_up).astype(BF16)
    dg_ref[...] = d_gate
    du_ref[...] = d_up

    @pl.when(step == 0)
    def _():
        sum_s[...] = jnp.zeros_like(sum_s)

    sum_s[...] += dot_nt(d_gate, gate_s[...]) + dot_nt(d_up, up_s[...])

    @pl.when(step == pl.num_programs(0) - 1)
    def _():
        cols = dh_refs[0].shape[1]
        for k, dh_ref in enumerate(dh_refs):
            dh_ref[...] = sum_s[:, k * cols : (k + 1) * cols].astype(BF16)


def gate_up_back(place, cotangent, by_gate, by_up, gates, ups, downs, depth, tf):
    rows, width = cotangent.shape
    units = by_gate.shape[1]
    gates, ups, downs = (Rows(p, depth, tf) for p in (gates, ups, downs))
    return call(
        functools.partial(gate_up_back_kernel, gates, ups, downs, units % tf),
        pl.cdiv(units, tf),
        [once((rows, width))]
        + [pl.BlockSpec((rows, tf), col_block)] * 2
        + gates.specs
        + ups.specs
        + downs.specs,
        [pl.BlockSpec((rows, tf), col_block)] * 2 + [once((rows, width // CUTS))] * CUTS,
        [shape((rows, units), BF16)] * 2 + [shape((rows, width // CUTS), BF16)] * CUTS,
        [pltpu.VMEM((width, tf), BF16)] * 3 + [pltpu.VMEM((rows, width), F32)],
        60,
        "gate_up_back",
    )(place, cotangent, by_gate, by_up, *gates.arrays, *ups.arrays, *downs.arrays)


def whole_grad_kernel(left_ref, right_ref, out_ref):
    out_ref[...] = dot_nn(left_ref[...], right_ref[...]).astype(BF16)


def whole_grad(left_t, right, tf):
    width, rows = left_t.shape
    units = right.shape[1]
    return pl.pallas_call(
        whole_grad_kernel,
        grid=(pl.cdiv(units, tf),),
        in_specs=[once((width, rows)), pl.BlockSpec((rows, tf), col_block)],
        out_specs=pl.BlockSpec((width, tf), col_block),
        out_shape=shape((width, units), BF16),
        compiler_params=pltpu.CompilerParams(vmem_limit_bytes=48 * MIB),
        cost_estimate=LONG,
        name="whole_grad",
    )(left_t, right)


def weight_grad_kernel(depth, parts, place, left_ref, right_ref, keep_ref, send_ref):
    for j in range(parts):
        half = keep_ref if j % 2 == 0 else send_ref
        rows = pl.ds(pl.multiple_of((place[0] ^ j) * depth, 16), depth)
        at = (j // 2) * depth
        half[at : at + depth, :] = dot_nn(left_ref[rows, :], right_ref[...]).astype(BF16)


def weight_grad(place, left_t, right, parts, tf):
    width, rows = left_t.shape
    units = right.shape[1]
    return call(
        functools.partial(weight_grad_kernel, width // parts, parts),
        pl.cdiv(units, tf),
        [once((width, rows)), pl.BlockSpec((rows, tf), col_block)],
        [pl.BlockSpec((width // 2, tf), col_block)] * 2,
        [shape((width // 2, units), BF16)] * 2,
        [],
        48,
        "weight_grad",
    )(place, left_t, right)


def down_project_kernel(downs, place, act_ref, *refs):
    down_refs, (out_ref, down_s, sum_s) = refs[: len(downs)], refs[len(downs) :]
    step = pl.program_id(0)
    downs.join(place[0], down_refs, down_s)

    @pl.when(step == 0)
    def _():
        sum_s[...] = jnp.zeros_like(sum_s)

    sum_s[...] += dot_nt(act_ref[...], down_s[...])

    @pl.when(step == pl.num_programs(0) - 1)
    def _():
        out_ref[...] = sum_s[...].astype(BF16)


def down_project(place, act, downs, width, depth, tf):
    rows, units = act.shape
    downs = Rows(downs, depth, tf)
    return call(
        functools.partial(down_project_kernel, downs),
        units // tf,
        [pl.BlockSpec((rows, tf), col_block)] + downs.specs,
        once((rows, width)),
        shape((rows, width), BF16),
        [pltpu.VMEM((width, tf), BF16), pltpu.VMEM((rows, width), F32)],
        48,
        "down_project",
    )(place, act, *downs.arrays)


def inverse_rms(values):
    return lax.rsqrt(jnp.mean(values * values, axis=-1, keepdims=True) + EPSILON)


def turned(values, cosine, sine):
    return values * cosine + pltpu.roll(values, HEAD // 2, 1) * sine


def mix_kernel(weight, group, place, x_ref, gain_ref, bias_ref, cos_ref, sin_ref, *refs):
    pieces, (q_ref, kv_ref, ht_ref, weight_s) = refs[: len(weight)], refs[len(weight) :]

    @pl.when(pl.program_id(0) == 0)
    def _():
        weight.join(place[0], pieces, weight_s)

    x = x_ref[...].astype(F32)
    hidden = (x * inverse_rms(x) * gain_ref[...].astype(F32)).astype(BF16)
    ht_ref[...] = hidden.T
    mixed = dot_nn(hidden, weight_s[...]) + bias_ref[...].astype(F32)
    cosine, sine = cos_ref[...], sin_ref[...]
    for h in range(group):
        at = slice(h * HEAD, (h + 1) * HEAD)
        q_ref[:, at] = turned(mixed[:, at], cosine, sine).astype(BF16)
    split = group * HEAD
    kv_ref[:, :HEAD] = turned(mixed[:, split : split + HEAD], cosine, sine).astype(BF16)
    kv_ref[:, HEAD:] = mixed[:, split + HEAD :].astype(BF16)


def mix(place, tokens, gain, bias, cosine, sine, pieces, depth, group, bq):
    rows, width = tokens.shape
    cols = pieces[0][2].shape[1]
    weight = Rows(pieces, depth)
    return call(
        functools.partial(mix_kernel, weight, group),
        rows // bq,
        [
            pl.BlockSpec((bq, width), row_block),
            once((1, width)),
            once((1, cols)),
            pl.BlockSpec((bq, HEAD), row_block),
            pl.BlockSpec((bq, HEAD), row_block),
        ]
        + weight.specs,
        [
            pl.BlockSpec((bq, group * HEAD), row_block),
            pl.BlockSpec((bq, 2 * HEAD), row_block),
            pl.BlockSpec((width, bq), col_block),
        ],
        [
            shape((rows, group * HEAD), BF16),
            shape((rows, 2 * HEAD), BF16),
            shape((width, rows), BF16),
        ],
        [pltpu.VMEM((width, cols), BF16)],
        32,
        "mix",
    )(place, tokens, gain[None], bias[None], cosine, sine, *weight.arrays)


def branch_kernel(weight, parts, place, x_ref, own_ref, other_ref, gain_ref, *refs):
    own_w, other_w = refs[: len(weight)], refs[len(weight) : len(weight) + parts]
    mid_ref, h_ref, ht_ref, weight_s, att_s = refs[len(weight) + parts :]
    split = own_ref.shape[1]
    own_at = pl.multiple_of(place[1] * split, HEAD)
    other_at = pl.multiple_of((1 - place[1]) * split, HEAD)

    @pl.when(pl.program_id(0) == 0)
    def _():
        weight.join(place[0], own_w, weight_s, own_at)
        join(place[0], weight.depth, [(j, 0) for j in range(parts)], other_w, weight_s, other_at)

    att_s[:, pl.ds(own_at, split)] = own_ref[...]
    att_s[:, pl.ds(other_at, split)] = other_ref[...]
    mid = x_ref[...].astype(F32) + dot_nt(att_s[...], weight_s[...])
    mid_ref[...] = mid
    hidden = (mid * inverse_rms(mid) * gain_ref[...].astype(F32)).astype(BF16)
    h_ref[...] = hidden
    ht_ref[...] = hidden.T


def branch(place, tokens, own, other, gain, pieces, other_weight, depth, bq):
    rows, width = tokens.shape
    cols = own.shape[1]
    parts = width // depth
    weight = Rows(pieces, depth)
    wide = pl.BlockSpec((bq, width), row_block)
    narrow = pl.BlockSpec((bq, cols), row_block)
    other_specs = [
        pl.BlockSpec((depth, cols), lambda *_, j=j: (j, 0), pipeline_mode=pl.Buffered(1))
        for j in range(parts)
    ]
    return call(
        functools.partial(branch_kernel, weight, parts),
        rows // bq,
        [wide, narrow, narrow, once((1, width))] + weight.specs + other_specs,
        [wide, wide, pl.BlockSpec((width, bq), col_block)],
        [shape((rows, width), F32), shape((rows, width), BF16), shape((width, rows), BF16)],
        [pltpu.VMEM((width, 2 * cols), BF16), pltpu.VMEM((bq, 2 * cols), BF16)],
        40,
        "branch",
    )(place, tokens, own, other, gain[None], *weight.arrays, *([other_weight] * parts))


def middle_back_kernel(
    weight, group, place, mid_ref, c_ref, gain_ref, att_ref, *refs
):
    own_refs, other_refs, refs = refs[:CUTS], refs[CUTS : 2 * CUTS], refs[2 * CUTS :]
    pieces, refs = refs[: len(weight)], refs[len(weight) :]
    dm_ref, dbt_ref, da_ref, delta_ref, dgain_ref, weight_s = refs

    @pl.when(pl.program_id(0) == 0)
    def _():
        weight.join(place[0], pieces, weight_s)
        dgain_ref[...] = jnp.zeros_like(dgain_ref)

    mid = mid_ref[...]
    inverse = inverse_rms(mid)
    normed = mid * inverse
    own = jnp.concatenate([ref[...] for ref in own_refs], axis=1).astype(F32)
    other = jnp.concatenate([ref[...] for ref in other_refs], axis=1).astype(F32)
    dgain_ref[...] += jnp.sum(own * normed, axis=0, keepdims=True)
    scaled = (own + other) * gain_ref[...].astype(F32)
    d_mid = c_ref[...].astype(F32) + inverse * (
        scaled - normed * jnp.mean(scaled * normed, axis=-1, keepdims=True)
    )
    dm_ref[...] = d_mid
    d_branch = d_mid.astype(BF16)
    dbt_ref[...] = d_branch.T
    d_att = dot_nn(d_branch, weight_s[...]).astype(BF16)
    da_ref[...] = d_att
    product = d_att.astype(F32) * att_ref[...].astype(F32)
    for h in range(group):
        delta_ref[h : h + 1, :] = jnp.sum(
            product[:, h * HEAD : (h + 1) * HEAD].T, axis=0, keepdims=True
        )


def middle_back(place, own, other, mid, cotangent, gain, attended, pieces, depth, bq):
    rows, width = mid.shape
    cols = attended.shape[1]
    weight = Rows(pieces, depth)
    group = cols // HEAD
    wide = pl.BlockSpec((bq, width), row_block)
    narrow = pl.BlockSpec((bq, cols), row_block)
    return call(
        functools.partial(middle_back_kernel, weight, group),
        rows // bq,
        [wide, wide, once((1, width)), narrow]
        + [pl.BlockSpec((bq, width // CUTS), row_block)] * (2 * CUTS)
        + weight.specs,
        [
            wide,
            pl.BlockSpec((width, bq), col_block),
            narrow,
            pl.BlockSpec((group, bq), col_block),
            pl.BlockSpec((1, width), whole_block),
        ],
        [
            shape((rows, width), F32),
            shape((width, rows), BF16),
            shape((rows, cols), BF16),
            shape((group, rows), F32),
            shape((1, width), F32),
        ],
        [pltpu.VMEM((width, cols), BF16)],
        48,
        "middle_back",
    )(place, mid, cotangent, gain[None], attended, *own, *other, *weight.arrays)


def mix_back_kernel(
    weight, group, place, dq_ref, dkv_ref, cos_ref, sin_ref, x_ref, *refs
):
    pieces, refs = refs[: len(weight)], refs[len(weight) :]
    dm_ref, dbias_ref, dgain_ref, *dh_refs, weight_s = refs

    @pl.when(pl.program_id(0) == 0)
    def _():
        weight.join(place[0], pieces, weight_s)
        dgain_ref[...] = jnp.zeros_like(dgain_ref)
        dbias_ref[...] = jnp.zeros_like(dbias_ref)

    split = group * HEAD
    dm_ref[:, :split] = dq_ref[...]
    d_keys = dkv_ref[:, :HEAD].astype(F32)
    dm_ref[:, split : split + HEAD] = turned(d_keys, cos_ref[...], -sin_ref[...]).astype(BF16)
    dm_ref[:, split + HEAD :] = dkv_ref[:, HEAD:]
    d_mixed = dm_ref[...]
    dbias_ref[...] += jnp.sum(d_mixed.astype(F32), axis=0, keepdims=True)
    d_hidden = dot_nt(d_mixed, weight_s[...])
    x = x_ref[...].astype(F32)
    dgain_ref[...] += jnp.sum(d_hidden * (x * inverse_rms(x)), axis=0, keepdims=True)
    cols = dh_refs[0].shape[1]
    for k, dh_ref in enumerate(dh_refs):
        dh_ref[...] = d_hidden[:, k * cols : (k + 1) * cols].astype(BF16)


def mix_back(place, dq, dkv, cosine, sine, tokens, pieces, depth, bq):
    rows, width = tokens.shape
    cols = pieces[0][2].shape[1]
    weight = Rows(pieces, depth)
    group = dq.shape[1] // HEAD
    wide = pl.BlockSpec((bq, width), row_block)
    return call(
        functools.partial(mix_back_kernel, weight, group),
        rows // bq,
        [
            pl.BlockSpec((bq, group * HEAD), row_block),
            pl.BlockSpec((bq, 2 * HEAD), row_block),
            pl.BlockSpec((bq, HEAD), row_block),
            pl.BlockSpec((bq, HEAD), row_block),
            wide,
        ]
        + weight.specs,
        [
            pl.BlockSpec((bq, cols), row_block),
            pl.BlockSpec((1, cols), whole_block),
            pl.BlockSpec((1, width), whole_block),
        ]
        + [pl.BlockSpec((bq, width // CUTS), row_block)] * CUTS,
        [
            shape((rows, cols), BF16),
            shape((1, cols), F32),
            shape((1, width), F32),
        ]
        + [shape((rows, width // CUTS), BF16)] * CUTS,
        [pltpu.VMEM((width, cols), BF16)],
        32,
        "mix_back",
    )(place, dq, dkv, cosine, sine, tokens, *weight.arrays)


def input_back_kernel(place, x_ref, gain_ref, dm_ref, *refs):
    own_refs, other_refs, (out_ref,) = refs[:CUTS], refs[CUTS : 2 * CUTS], refs[2 * CUTS :]
    own = jnp.concatenate([ref[...] for ref in own_refs], axis=1).astype(F32)
    other = jnp.concatenate([ref[...] for ref in other_refs], axis=1).astype(F32)
    x = x_ref[...].astype(F32)
    inverse = inverse_rms(x)
    normed = x * inverse
    scaled = (own + other) * gain_ref[...].astype(F32)
    out_ref[...] = dm_ref[...] + inverse * (
        scaled - normed * jnp.mean(scaled * normed, axis=-1, keepdims=True)
    )


def input_back(place, own, other, tokens, gain, d_mid, bq):
    rows, width = tokens.shape
    wide = pl.BlockSpec((bq, width), row_block)
    return call(
        input_back_kernel,
        rows // bq,
        [wide, once((1, width)), wide] + [pl.BlockSpec((bq, width // CUTS), row_block)] * (2 * CUTS),
        wide,
        shape((rows, width), F32),
        [],
        32,
        "input_back",
    )(place, tokens, gain[None], d_mid, *own, *other)


def after(values, *first):
    return lax.optimization_barrier((values, first))[0]


def swap(value, axis, size, bit):
    return lax.ppermute(value, axis, [(i, i ^ bit) for i in range(size)])


class Pieces:
    def __init__(self, own, size, slabs=1):
        if size != 4 or own.shape[0] % (16 * slabs):
            slabs = 1
        self.size, self.own, self.slabs = size, own, slabs
        self.depth = own.shape[0] // slabs
        self.got = {}

    def far(self, slab, *first):
        if slab >= self.slabs:
            return ()
        own = after(self.own, first)
        own = own[slab * self.depth : (slab + 1) * self.depth]
        got, bit = {0: own}, self.size // 2
        while bit > 1:
            got.update({j ^ bit: swap(p, "shard", self.size, bit) for j, p in got.items()})
            bit //= 2
        self.got.update({(j, slab): p for j, p in got.items() if j})
        return [p for j, p in got.items() if j]

    def far_by_ctx(self, contexts, *first):
        own = after(self.own, first)
        rows = own.shape[0] // contexts
        own = lax.dynamic_slice_in_dim(own, lax.axis_index("ctx") * rows, rows, 0)
        got, bit = {0: own}, self.size // 2
        while bit > 1:
            got.update({j ^ bit: swap(p, "shard", self.size, bit) for j, p in got.items()})
            bit //= 2
        self.parts = {j: p for j, p in got.items() if j}
        return list(self.parts.values())

    def spread(self, *first):
        js = list(self.parts)
        parts = after(list(self.parts.values()), first)
        for j, part in zip(js, parts):
            self.got[j, 0] = lax.all_gather(part, "ctx", axis=0, tiled=True)
        return [self.got[j, 0] for j in js]

    def near_own(self, *first):
        self.near = swap(after(self.own, first), "shard", self.size, 1)
        return self.near

    def near_rest(self, slab, *first):
        if slab >= self.slabs:
            return ()
        far = [j for j in range(2, self.size, 2)]
        held = after([self.got[j, slab] for j in far], first)
        for j, piece in zip(far, held):
            self.got[j ^ 1, slab] = swap(piece, "shard", self.size, 1)
        return [self.got[j ^ 1, slab] for j in far]

    def all(self):
        found = [(0, 0, self.own), (1, 0, self.near)]
        found += [(j, k * self.depth, p) for (j, k), p in sorted(self.got.items(), key=lambda i: i[0])]
        return found


class Reduction:
    def __init__(self, halves, shards, contexts, slabs=1):
        self.keep, self.send = halves
        self.shards, self.chain = shards, contexts == 4
        self.slabs = slabs if shards == 4 else 1
        self.own, self.one, self.inner, self.two, self.total, self.three = ({} for _ in range(6))

    def cores(self, *first):
        self.got = swap(after(self.send, first), "shard", self.shards, 1)
        return self.got

    def chips(self, *first):
        held = list(after((self.keep, self.got), first))
        bit, count = 2, self.shards // 2
        while bit < self.shards:
            size = held[0].shape[0] // count // self.slabs

            def pick(odd, slab):
                blocks = [
                    [part[(at * self.slabs + slab) * size :][:size] for part in held]
                    for at in range(odd, count, 2)
                ]
                return blocks[0] if len(blocks) == 1 else [
                    jnp.concatenate(same, axis=0) for same in zip(*blocks)
                ]

            self.away = [sum(pick(1, slab)) for slab in range(self.slabs)]
            self.last = [swap(part, "shard", self.shards, bit) for part in self.away]
            self.here = [pick(0, slab) for slab in range(self.slabs)]
            held = self.here[0] + self.last
            bit, count = 2 * bit, count // 2
        return self.last

    def arrived(self, slab, *first):
        if slab >= self.slabs:
            return ()
        *here, last = after(self.here[slab] + [self.last[slab]], first)
        self.own[slab] = sum(here) + last
        return self.own[slab]

    def inward(self, slab, *first):
        if slab >= self.slabs:
            return ()
        own = after(self.own[slab], first)
        if self.chain:
            self.own[slab] = own
            self.one[slab] = lax.ppermute(own, "ctx", [(0, 1), (3, 2)])
        else:
            self.one[slab] = self.total[slab] = lax.psum(own, "ctx")
        return self.one[slab]

    def middle(self, slab, *first):
        if not self.chain or slab >= self.slabs:
            return ()
        own, one = after((self.own[slab], self.one[slab]), first)
        self.inner[slab] = own + one
        self.two[slab] = lax.ppermute(self.inner[slab], "ctx", [(1, 2), (2, 1)])
        return self.two[slab]

    def outward(self, slab, *first):
        if not self.chain or slab >= self.slabs:
            return ()
        inner, two = after((self.inner[slab], self.two[slab]), first)
        self.total[slab] = inner + two
        self.three[slab] = lax.ppermute(self.total[slab], "ctx", [(1, 0), (2, 3)])
        return self.three[slab]

    def result(self):
        totals = [self.total[slab] for slab in range(self.slabs)]
        if self.chain:
            place = lax.axis_index("ctx")
            inside = (place == 1) | (place == 2)
            totals = [
                jnp.where(inside, total, self.three[slab]) for slab, total in enumerate(totals)
            ]
        whole = totals[0] if len(totals) == 1 else jnp.concatenate(totals, axis=0)
        return whole.astype(F32)


def sum_of_all(value, sizes):
    for axis, size in sizes.items():
        bit = 1
        while bit < size:
            value = value + swap(value, axis, size, bit)
            bit *= 2
    return value


def tree_tables(seg_row, parent_row):
    seg_count = parent_row.shape[0]
    seg_ids = jnp.arange(seg_count, dtype=jnp.int32)
    one_hot = (seg_row[:, None] == seg_ids[None, :]).astype(jnp.int32)
    lengths = jnp.sum(one_hot, axis=0, dtype=jnp.int32)
    before = seg_ids[None, :] < seg_ids[:, None]
    starts = jnp.sum(jnp.where(before, lengths[None, :], 0), axis=1, dtype=jnp.int32)
    link = (parent_row[:, None] == seg_ids[None, :]) & (parent_row[:, None] != seg_ids[:, None])
    twice = jnp.any(link[:, :, None] & link[None, :, :], axis=1)
    strict = link | twice
    padding = parent_row == seg_ids
    reach = strict | ((seg_ids[:, None] == seg_ids[None, :]) & ~padding[:, None])
    offsets = jnp.sum(jnp.where(strict, lengths[None, :], 0), axis=1, dtype=jnp.int32) - starts
    return reach, offsets


def block_lists(row_hot, col_hot, reach, col_places, row_first, bq, bk):
    segs = reach.shape[0]
    row_has = jnp.any(row_hot.reshape(-1, bq, segs), axis=1)
    col_has = jnp.any(col_hot.reshape(-1, bk, segs), axis=1)
    row_blocks, col_blocks = row_has.shape[0], col_has.shape[0]
    row_reach = jnp.any(row_has[:, :, None] & reach[None], axis=1)
    meets = jnp.any(row_reach[:, None, :] & col_has[None], axis=2)
    col_at = col_places.reshape(-1, bk)[:, 0]
    row_at = row_first + bq * jnp.arange(row_blocks, dtype=jnp.int32)
    causal = col_at[None, :] < row_at[:, None] + bq
    diagonal = causal & (col_at[None, :] + bk > row_at[:, None])
    active = ((meets & causal) | diagonal) & (col_at >= 0)[None, :]
    ids = jnp.arange(col_blocks, dtype=jnp.int32)
    rank = jnp.sum(
        (active[:, None, :] & (ids[None, :] < ids[:, None])[None]).astype(jnp.int32), axis=2
    )
    placed = active[:, :, None] & (rank[:, :, None] == ids[None, None, :])
    chosen = jnp.sum(jnp.where(placed, ids[None, :, None], 0), axis=1, dtype=jnp.int32)
    count = jnp.sum(active.astype(jnp.int32), axis=1, dtype=jnp.int32)
    places = jnp.concatenate([col_at, row_first[None]])
    return count, chosen.reshape(-1), places


def layer(
    sizes, tokens, cotangent, segment, parent, gain_attn, qkv_weight, qkv_bias,
    out_weight, gain_ffn, gate_weight, up_weight, down_weight,
):
    shards, contexts, halves = sizes["shard"], sizes["ctx"], sizes["tp"]
    rows, width = tokens.shape
    group = out_weight.shape[1] // HEAD
    shard, ctx, half = lax.axis_index("shard"), lax.axis_index("ctx"), lax.axis_index("tp")
    place = jnp.stack([shard, half]).astype(jnp.int32)
    across = [(i, i ^ 1) for i in range(halves)]

    row_first = (ctx * rows).astype(jnp.int32)
    reach, offsets = tree_tables(segment[0], parent[0])
    seg_ids = jnp.arange(reach.shape[0], dtype=jnp.int32)
    behind = [jnp.maximum(ctx - k, 0) * rows for k in range(contexts)]
    seg_back = jnp.concatenate(
        [lax.dynamic_slice_in_dim(segment[0], at, rows, 0) for at in behind]
    )
    places_back = jnp.concatenate(
        [(ctx - k) * rows + jnp.arange(rows, dtype=jnp.int32) for k in range(contexts)]
    )
    col_hot = seg_back[:, None] == seg_ids[None, :]
    row_hot = col_hot[:rows]
    own_pos = places_back[:rows] + jnp.sum(
        jnp.where(row_hot, offsets[None, :], 0), axis=1, dtype=jnp.int32
    )
    pad = ((0, 0), (0, HEAD - reach.shape[0]))
    row_reach = jnp.any(row_hot[:, :, None] & reach[None], axis=1)
    reach_rows = jnp.pad(row_reach.astype(BF16), pad)
    hot = jnp.pad(col_hot.astype(BF16), pad)
    bq = math.gcd(rows, 256)
    bk_f, bk_b = math.gcd(rows, 128), math.gcd(rows, 512)
    lists_f = block_lists(row_hot, col_hot, reach, places_back, row_first, bq, bk_f)
    lists_b = block_lists(row_hot, col_hot, reach, places_back, row_first, bq, bk_b)
    lane = jnp.arange(HEAD, dtype=jnp.int32)
    frequency = THETA ** (-2.0 * (lane % (HEAD // 2)).astype(F32) / HEAD)
    angles = own_pos.astype(F32)[:, None] * frequency[None, :]
    cosine = jnp.cos(angles)
    sine = jnp.sin(angles) * jnp.where(lane < HEAD // 2, -1.0, 1.0)

    depth = width // shards
    qkv, out_w, gate, up, down = (
        Pieces(qkv_weight, shards),
        Pieces(out_weight, shards),
        Pieces(gate_weight, shards, 3),
        Pieces(up_weight, shards),
        Pieces(down_weight, shards, 3),
    )
    qkv_far = qkv.far(0)
    tables = (reach_rows, hot, lists_f, lists_b, cosine, sine, place)
    tables, qkv_far, top_grad_t = after((tables, qkv_far, cotangent.T))
    reach_rows, hot, lists_f, lists_b, cosine, sine, place = tables
    out_far = out_w.far(0, qkv_far)
    qkv_near = qkv.near_own(qkv_far), qkv.near_rest(0, qkv_far)
    out_near = out_w.near_own(qkv_far)
    place, qkv_near = after((place, qkv_near))
    up_parts = up.far_by_ctx(contexts, qkv_near)

    queries, kv_own, hidden_one_t = mix(
        place, tokens, gain_attn, qkv_bias, cosine, sine, qkv.all(), depth, group, bq
    )
    kv_own, out_far, out_near = after((kv_own, out_far, out_near))
    out_rest = out_w.near_rest(0, out_far)
    out_joined = jnp.concatenate([p for _, _, p in out_w.all()], axis=0)
    kv_own, out_joined = after((kv_own, out_joined))
    out_other = lax.ppermute(out_joined, "tp", across)
    kv_far = [
        lax.ppermute(kv_own, "ctx", [(i, i + k) for i in range(contexts - k)])
        for k in range(1, contexts)
    ]
    gate_far_0 = gate.far(0, kv_own)
    kv_far, gate_far_0, up_parts = after((kv_far, gate_far_0, up_parts))
    kv_back = jnp.concatenate([kv_own] + kv_far, axis=0)
    up_spread = up.spread(up_parts)
    gate_far_1 = gate.far(1, gate_far_0)
    own_near = gate.near_own(kv_far), up.near_own(kv_far), down.near_own(kv_far)
    attended, lse, tops = attention_forward(lists_f, queries, kv_back, reach_rows, hot, bq, bk_f)
    attended, gate_far_1, out_other, own_near = after((attended, gate_far_1, out_other, own_near))
    gate_far_2 = gate.far(2, attended)
    attended_other = lax.ppermute(attended, "tp", across)
    gate_near = gate.near_rest(0, attended), gate.near_rest(1, attended)
    attended_other, gate_near, gate_far_2 = after((attended_other, gate_near, gate_far_2))
    place = after(place, attended_other)
    down_far_0 = down.far(0, attended_other)
    gate_near_2 = gate.near_rest(2, attended_other)
    mid, hidden_two, hidden_two_t = branch(
        place, tokens, attended, attended_other, gain_ffn, out_w.all(), out_other, depth, bq
    )
    mid, gate_near_2, up_spread = after((mid, gate_near_2, up_spread))
    up_near = up.near_rest(0, up_spread)
    place, up_near = after((place, up_near))
    down_far_1 = down.far(1, up_near)
    act, by_gate, by_up = gate_up(place, hidden_two, gate.all(), up.all(), depth, 512)
    act, down_far_0, down_far_1 = after((act, down_far_0, down_far_1))
    down_far_2 = down.far(2, act)
    down_near = down.near_rest(0, act), down.near_rest(1, act)
    down_part = whole_grad(top_grad_t, act, 512)
    down_part, down_near, down_far_2 = after((down_part, down_near, down_far_2))
    down_part = lax.psum_scatter(
        down_part, ("shard", "ctx"), scatter_dimension=0, tiled=True
    )
    down_near_2 = down.near_rest(2, down_far_2)
    place, down_near_2 = after((place, down_near_2))
    d_gate, d_up, *d_hidden_two = gate_up_back(
        place, cotangent, by_gate, by_up, gate.all(), up.all(), down.all(), depth, 512
    )

    d_gate, d_hidden_two = after((d_gate, d_hidden_two))
    other = [lax.ppermute(d_hidden_two[0], "tp", across)]
    gate_grad = Reduction(weight_grad(place, hidden_two_t, d_gate, shards, 512), shards, contexts, 2)
    gate_grad.send, other[0] = after((gate_grad.send, other[0]))
    place = after(place, gate_grad.send)
    gate_cores = gate_grad.cores()
    other.append(lax.ppermute(after(d_hidden_two[1], gate_grad.send), "tp", across))
    up_grad = Reduction(weight_grad(place, hidden_two_t, d_up, shards, 512), shards, contexts, 2)
    up_grad.send, gate_cores, other[1] = after((up_grad.send, gate_cores, other[1]))
    gate_chips = gate_grad.chips(gate_cores)
    gate_away, up_grad.send = after((gate_grad.away, up_grad.send))
    up_cores = up_grad.cores(gate_away)
    other.append(lax.ppermute(after(d_hidden_two[2], gate_away), "tp", across))
    place = after(place, gate_away)
    ffn_own = down_project(place, act, down.all(), width, depth, 896)
    ffn_own, other[2], up_cores = after((ffn_own, other[2], up_cores))
    ffn_other = lax.ppermute(ffn_own, "tp", across)
    up_chips = up_grad.chips(up_cores)

    place = after(place, ffn_own, up_grad.away)
    d_mid, d_branch_t, d_att, delta, gain_two_part = middle_back(
        place, d_hidden_two, other, mid, cotangent, gain_ffn, attended, out_w.all(), depth, bq
    )
    place = after(place, d_mid)
    out_grad = Reduction(weight_grad(place, d_branch_t, attended, shards, 768), shards, contexts)
    out_grad.send, gate_grad.last[0], down_part = after(
        (out_grad.send, gate_grad.last[0], down_part)
    )
    down_total = lax.all_gather(down_part, "ctx", axis=0, tiled=True)
    out_cores = out_grad.cores()
    gate_own_0 = gate_grad.arrived(0)
    lists_b, gate_grad.own[0] = after((lists_b, gate_own_0), down_part)
    gate_in_0 = gate_grad.inward(0)
    d_query, d_kv = attention_backward(
        lists_b, queries, d_att, lse, delta, kv_back, reach_rows, hot, cosine, sine, bq, bk_b
    )
    d_kv, gate_grad.last, gate_grad.one, out_grad.got, ffn_other = after(
        (d_kv, gate_grad.last, gate_grad.one, out_grad.got, ffn_other)
    )
    d_kv_far = [
        lax.ppermute(d_kv[k * rows : (k + 1) * rows], "ctx", [(i + k, i) for i in range(contexts - k)])
        for k in range(1, contexts)
    ]
    gate_mid_0 = gate_grad.middle(0, d_kv)
    gate_own_1 = gate_grad.arrived(1, d_kv)
    gate_in_1 = gate_grad.inward(1)
    out_chips = out_grad.chips(d_kv)
    output = (after(mid, d_kv) + (ffn_own.astype(F32) + ffn_other.astype(F32))).astype(BF16)
    d_kv_far, output, down_total = after(
        (d_kv_far, output, down_total), out_grad.away, gate_grad.own, gate_grad.inner
    )
    d_kv_own = sum((p.astype(F32) for p in d_kv_far), d_kv[:rows].astype(F32)).astype(BF16)
    d_mixed, bias_part, gain_one_part, *d_hidden_one = mix_back(
        place, d_query, d_kv_own, cosine, sine, tokens, qkv.all(), depth, bq
    )
    peak_own = jnp.max(tops, axis=1)
    device = shard * contexts + ctx
    spread = jnp.where(
        (jnp.arange(shards * contexts)[:, None, None] == device)
        & (jnp.arange(halves)[None, :, None] == half),
        peak_own[None, None, :],
        0.0,
    )
    bias_both = jnp.where(jnp.arange(halves)[:, None] == half, bias_part, 0.0)
    vector = jnp.concatenate(
        [gain_one_part[0], gain_two_part[0], bias_both.reshape(-1), spread.reshape(-1)]
    )
    d_mixed, vector, d_hidden_one = after((d_mixed, vector, d_hidden_one))
    place = after(place, d_mixed)
    back = [lax.ppermute(d_hidden_one[0], "tp", across)]
    vector_got = swap(vector, "shard", shards, 1)
    qkv_grad = Reduction(weight_grad(place, hidden_one_t, d_mixed, shards, 512), shards, contexts)

    qkv_grad.send, vector_got, gate_grad.one, gate_grad.two, up_grad.last[0] = after(
        (qkv_grad.send, vector_got, gate_grad.one, gate_grad.two, up_grad.last[0])
    )
    qkv_cores = qkv_grad.cores()
    vector = vector + vector_got
    up_grad.arrived(0)
    up_grad.inward(0)
    gate_grad.middle(1)
    gate_grad.outward(0)
    qkv_cores, vector, up_grad.last, out_grad.last = after(
        (qkv_cores, vector, up_grad.last, out_grad.last),
        up_grad.own, gate_grad.inner, gate_grad.total,
    )
    qkv_grad.got = qkv_cores
    qkv_chips = qkv_grad.chips()
    bit = 2
    while bit < shards:
        vector = vector + swap(vector, "shard", shards, bit)
        bit *= 2
    up_grad.arrived(1)
    up_grad.inward(1)
    out_grad.arrived(0)
    out_grad.inward(0)
    back.append(lax.ppermute(after(d_hidden_one[1], vector_got), "tp", across))
    vector, back[0], up_grad.one, gate_grad.two = after(
        (vector, back[0], up_grad.one, gate_grad.two), qkv_grad.away, up_grad.own, out_grad.own
    )
    up_grad.middle(0)
    gate_grad.outward(1)
    back.append(lax.ppermute(after(d_hidden_one[2], back[0]), "tp", across))
    vector = sum_of_all(vector, {"ctx": contexts})
    vector, qkv_grad.last, up_grad.one, up_grad.two, out_grad.one = after(
        (vector, qkv_grad.last, up_grad.one, up_grad.two, out_grad.one),
        up_grad.inner, gate_grad.total,
    )
    up_grad.middle(1)
    up_grad.outward(0)
    out_grad.middle(0)
    qkv_grad.arrived(0)
    qkv_grad.inward(0)
    back = after(back, up_grad.inner, up_grad.total, out_grad.inner, qkv_grad.own)
    vector_got = swap(vector, "tp", halves, 1)
    input_grad = input_back(place, d_hidden_one, back, tokens, gain_attn, d_mid, bq)
    input_grad, vector_got, qkv_grad.one, out_grad.two, up_grad.two = after(
        (input_grad, vector_got, qkv_grad.one, out_grad.two, up_grad.two)
    )
    vector = vector + vector_got
    up_grad.outward(1)
    out_grad.outward(0)
    qkv_grad.middle(0)
    qkv_grad.outward(0)
    down_total = down_total.astype(F32)
    gate_total, up_total, out_total, qkv_total = (
        one.result() for one in (gate_grad, up_grad, out_grad, qkv_grad)
    )
    bias_at = 2 * width
    spread_at = bias_at + bias_both.size
    bias_grad = lax.dynamic_slice_in_dim(
        vector[bias_at:spread_at], half * bias_part.size, bias_part.size, 0
    )
    peaks = jnp.max(vector[spread_at:].reshape(shards * contexts, halves, group), axis=0)
    peak_all = lax.dynamic_index_in_dim(peaks, half, 0, keepdims=False)
    clip_out = CLIP_BOUND / jnp.maximum(peak_all, CLIP_BOUND)
    return (
        output,
        input_grad,
        vector[:width],
        qkv_total,
        bias_grad,
        out_total,
        vector[width:bias_at],
        gate_total,
        up_total,
        down_total,
        clip_out,
    )


def solution(mesh):
    token = P(("shard", "ctx"), None)
    weight = P("shard", "tp")
    return jax.shard_map(
        functools.partial(layer, dict(mesh.shape)),
        mesh=mesh,
        in_specs=(
            token,
            token,
            P("shard", None),
            P("shard", None),
            P(),
            weight,
            P("tp"),
            weight,
            P(),
            weight,
            weight,
            weight,
        ),
        out_specs=(
            token,
            token,
            P(),
            weight,
            P("tp"),
            weight,
            P(),
            weight,
            weight,
            weight,
            P("tp"),
        ),
        check_vma=False,
    )
```

```python
import functools
import math

import jax
import jax.numpy as jnp
from jax import lax
from jax.experimental import pallas as pl
from jax.experimental.pallas import tpu as pltpu
from jax.sharding import PartitionSpec as P

HEAD = 128
EPSILON = 1e-06
THETA = 1000000.0
CLIP_BOUND = 4.0
NEG_FILL = -1e30
SCALE = HEAD ** (-0.5)
SCALE_2 = SCALE * math.log2(math.e)
MIB = 1 << 20
CUTS = 3


def cuts(width):
    return [width // 4, width // 4, width // 2]


PACE = 175_000_000


def cost(us):
    return pl.CostEstimate(flops=int(us * PACE), bytes_accessed=1000, transcendentals=0)


BF16 = jnp.bfloat16
F32 = jnp.float32


def dot_nt(left, right):
    return lax.dot_general(left, right, (((1,), (1,)), ((), ())), preferred_element_type=F32)


def dot_nn(left, right):
    return jnp.dot(left, right, preferred_element_type=F32)


def seen_block(hot, reach_rows, col_at, row_at, bk, bq):
    linked = dot_nt(hot, reach_rows) > 0.5
    cols = col_at + lax.broadcasted_iota(jnp.int32, (bk, bq), 0)
    rows = row_at + lax.broadcasted_iota(jnp.int32, (bk, bq), 1)
    return (linked & (cols <= rows)) | (cols == rows)


def attention_forward_kernel(
    group, bq, bk, blocks, first, count, chosen, places, q_ref, kv_ref, reach_ref, hot_ref,
    out_ref, lse_ref, top_ref, max_s, sum_s, acc_s,
):
    row_block = pl.program_id(0) + first
    max_s[...] = jnp.full_like(max_s, NEG_FILL)
    sum_s[...] = jnp.zeros_like(sum_s)
    acc_s[...] = jnp.zeros_like(acc_s)
    row_at = places[blocks] + row_block * bq

    def body(step, carry):
        block = chosen[row_block * blocks + step]
        here = pl.ds(pl.multiple_of(block * bk, bk), bk)
        keys = kv_ref[here, :HEAD]
        values_t = kv_ref[here, HEAD:].T
        seen = seen_block(hot_ref[here, :], reach_ref[...], places[block], row_at, bk, bq)
        for h in range(group):
            score = jnp.where(seen, dot_nt(keys, q_ref[:, h * HEAD : (h + 1) * HEAD]), NEG_FILL)
            old = max_s[h : h + 1, :]
            new = jnp.maximum(old, jnp.max(score, axis=0, keepdims=True))
            prob = jnp.exp2((score - new) * SCALE_2)
            fade = jnp.exp2((old - new) * SCALE_2)
            max_s[h : h + 1, :] = new
            sum_s[h : h + 1, :] = sum_s[h : h + 1, :] * fade + jnp.sum(prob, axis=0, keepdims=True)
            acc_s[h] = acc_s[h] * fade + dot_nn(values_t, prob.astype(BF16))
        return carry

    lax.fori_loop(0, count[row_block], body, 0)
    top_ref[...] = max_s[...] * SCALE
    lse_ref[...] = max_s[...] * SCALE_2 + jnp.log2(sum_s[...])
    for h in range(group):
        out_ref[:, h * HEAD : (h + 1) * HEAD] = (acc_s[h] / sum_s[h : h + 1, :]).T.astype(BF16)


def attention_forward(lists, queries, kv, reach_rows, hot, bq, bk, first, rows):
    width = queries.shape[1]
    first //= bq
    slots = kv.shape[0]
    group = width // HEAD
    whole = lambda *_: (0, 0)
    row = lambda i, *_: (i, 0)
    col = lambda i, *_: (0, i)
    return pl.pallas_call(
        functools.partial(attention_forward_kernel, group, bq, bk, slots // bk, first),
        grid_spec=pltpu.PrefetchScalarGridSpec(
            num_scalar_prefetch=3,
            grid=(rows // bq,),
            in_specs=[
                pl.BlockSpec((bq, width), lambda i, *_: (i + first, 0)),
                pl.BlockSpec((slots, 2 * HEAD), whole),
                pl.BlockSpec((bq, HEAD), lambda i, *_: (i + first, 0)),
                pl.BlockSpec((slots, HEAD), whole),
            ],
            out_specs=[
                pl.BlockSpec((bq, width), row),
                pl.BlockSpec((group, bq), col),
                pl.BlockSpec((group, bq), col),
            ],
            scratch_shapes=[
                pltpu.VMEM((group, bq), F32),
                pltpu.VMEM((group, bq), F32),
                pltpu.VMEM((group, HEAD, bq), F32),
            ],
        ),
        out_shape=[
            jax.ShapeDtypeStruct((rows, width), BF16),
            jax.ShapeDtypeStruct((group, rows), F32),
            jax.ShapeDtypeStruct((group, rows), F32),
        ],
        compiler_params=pltpu.CompilerParams(vmem_limit_bytes=32 * MIB),
        cost_estimate=cost(15),
        name="attention_forward",
    )(*lists, queries, kv, reach_rows, hot)


def attention_backward_kernel(
    group, bq, bk, blocks, count, chosen, places, q_ref, do_ref, lse_ref, delta_ref, kv_ref,
    reach_ref, hot_ref, cos_ref, sin_ref, dq_ref, dkv_ref, acc_s, dk_s, dv_s,
):
    row_block = pl.program_id(0)

    @pl.when(row_block == 0)
    def _():
        dk_s[...] = jnp.zeros_like(dk_s)
        dv_s[...] = jnp.zeros_like(dv_s)

    acc_s[...] = jnp.zeros_like(acc_s)
    row_at = places[blocks] + row_block * bq

    def body(step, carry):
        block = chosen[row_block * blocks + step]
        here = pl.ds(pl.multiple_of(block * bk, bk), bk)
        keys = kv_ref[here, :HEAD]
        values = kv_ref[here, HEAD:]
        keys_t = keys.T
        seen = seen_block(hot_ref[here, :], reach_ref[...], places[block], row_at, bk, bq)
        dk = jnp.zeros((bk, HEAD), F32)
        dv = jnp.zeros((bk, HEAD), F32)
        for h in range(group):
            qh = q_ref[:, h * HEAD : (h + 1) * HEAD]
            doh = do_ref[:, h * HEAD : (h + 1) * HEAD]
            prob = jnp.where(
                seen, jnp.exp2(dot_nt(keys, qh) * SCALE_2 - lse_ref[h : h + 1, :]), 0.0
            )
            ds = (prob * (dot_nt(values, doh) - delta_ref[h : h + 1, :])).astype(BF16)
            dv = dv + dot_nn(prob.astype(BF16), doh)
            dk = dk + dot_nn(ds, qh)
            acc_s[h] = acc_s[h] + dot_nn(keys_t, ds)
        dk_s[here, :] += dk
        dv_s[here, :] += dv
        return carry

    lax.fori_loop(0, count[row_block], body, 0)
    for h in range(group):
        d_query = (acc_s[h] * SCALE).T
        dq_ref[:, h * HEAD : (h + 1) * HEAD] = turned(
            d_query, cos_ref[...], -sin_ref[...]
        ).astype(BF16)

    @pl.when(row_block == pl.num_programs(0) - 1)
    def _():
        dkv_ref[:, :HEAD] = (dk_s[...] * SCALE).astype(BF16)
        dkv_ref[:, HEAD:] = dv_s[...].astype(BF16)


def attention_backward(
    lists, queries, d_att, lse, delta, kv, reach_rows, hot, cosine, sine, bq, bk
):
    rows, width = queries.shape
    slots = kv.shape[0]
    group = width // HEAD
    whole = lambda *_: (0, 0)
    row = lambda i, *_: (i, 0)
    col = lambda i, *_: (0, i)
    return pl.pallas_call(
        functools.partial(attention_backward_kernel, group, bq, bk, slots // bk),
        grid_spec=pltpu.PrefetchScalarGridSpec(
            num_scalar_prefetch=3,
            grid=(rows // bq,),
            in_specs=[
                pl.BlockSpec((bq, width), row),
                pl.BlockSpec((bq, width), row),
                pl.BlockSpec((group, bq), col),
                pl.BlockSpec((group, bq), col),
                pl.BlockSpec((slots, 2 * HEAD), whole),
                pl.BlockSpec((bq, HEAD), row),
                pl.BlockSpec((slots, HEAD), whole),
                pl.BlockSpec((bq, HEAD), row),
                pl.BlockSpec((bq, HEAD), row),
            ],
            out_specs=[
                pl.BlockSpec((bq, width), row),
                pl.BlockSpec((slots, 2 * HEAD), whole),
            ],
            scratch_shapes=[
                pltpu.VMEM((group, HEAD, bq), F32),
                pltpu.VMEM((slots, HEAD), F32),
                pltpu.VMEM((slots, HEAD), F32),
            ],
        ),
        out_shape=[
            jax.ShapeDtypeStruct((rows, width), BF16),
            jax.ShapeDtypeStruct((slots, 2 * HEAD), BF16),
        ],
        compiler_params=pltpu.CompilerParams(vmem_limit_bytes=40 * MIB),
        cost_estimate=cost(54),
        name="attention_backward",
    )(*lists, queries, d_att, lse, delta, kv, reach_rows, hot, cosine, sine)


def join(mine, depth, places, pieces, joined, at_col=None):
    cols = pieces[0].shape[1]
    where = slice(None) if at_col is None else pl.ds(pl.multiple_of(at_col, HEAD), cols)
    for (j, row), piece in zip(places, pieces):
        at = pl.multiple_of((mine ^ j) * depth + row, 16)
        joined[pl.ds(at, piece.shape[0]), where] = piece[...]


class Rows:
    def __init__(self, pieces, depth, tf=None):
        self.depth = depth
        self.places = [(j, row) for j, row, _ in pieces]
        self.arrays = [array for _, _, array in pieces]
        if tf is None:
            self.specs = [once(array.shape) for array in self.arrays]
        else:
            self.specs = [pl.BlockSpec((array.shape[0], tf), col_block) for array in self.arrays]

    def __len__(self):
        return len(self.arrays)

    def join(self, mine, refs, joined, at_col=None):
        join(mine, self.depth, self.places, refs, joined, at_col)


def whole_block(*_):
    return (0, 0)


def row_block(i, *_):
    return (i, 0)


def col_block(i, *_):
    return (0, i)


def once(shape):
    return pl.BlockSpec(shape, whole_block, pipeline_mode=pl.Buffered(1))


def call(kernel, grid, in_specs, out_specs, out_shape, scratch, vmem, us, name):
    return pl.pallas_call(
        kernel,
        grid_spec=pltpu.PrefetchScalarGridSpec(
            num_scalar_prefetch=1,
            grid=(grid,),
            in_specs=in_specs,
            out_specs=out_specs,
            scratch_shapes=scratch,
        ),
        out_shape=out_shape,
        compiler_params=pltpu.CompilerParams(vmem_limit_bytes=vmem * MIB),
        cost_estimate=cost(us),
        name=name,
    )


def shape(dims, dtype):
    return jax.ShapeDtypeStruct(dims, dtype)


def clear_tail(tail, *joined):
    if tail:

        @pl.when(pl.program_id(0) == pl.num_programs(0) - 1)
        def _():
            for one in joined:
                one[:, tail:] = jnp.zeros_like(one[:, tail:])


def gate_up_kernel(gates, ups, place, h_ref, *refs):
    gate_refs, refs = refs[: len(gates)], refs[len(gates) :]
    up_refs, refs = refs[: len(ups)], refs[len(ups) :]
    act_ref, by_gate_ref, by_up_ref, gate_s, up_s = refs
    gates.join(place[0], gate_refs, gate_s)
    ups.join(place[0], up_refs, up_s)
    gate = dot_nn(h_ref[...], gate_s[...])
    up = dot_nn(h_ref[...], up_s[...])
    sig = jax.nn.sigmoid(gate)
    silu = gate * sig
    act_ref[...] = (silu * up).astype(BF16)
    by_up_ref[...] = silu.astype(BF16)
    by_gate_ref[...] = (up * sig * (1.0 + gate * (1.0 - sig))).astype(BF16)


def gate_up(place, hidden, gates, ups, depth, tf):
    rows, width = hidden.shape
    units = gates[0][2].shape[1]
    gates, ups = Rows(gates, depth, tf), Rows(ups, depth, tf)
    return call(
        functools.partial(gate_up_kernel, gates, ups),
        pl.cdiv(units, tf),
        [once((rows, width))] + gates.specs + ups.specs,
        [pl.BlockSpec((rows, tf), col_block)] * 3,
        [shape((rows, units), BF16)] * 3,
        [pltpu.VMEM((width, tf), BF16)] * 2,
        60,
        40,
        "gate_up",
    )(place, hidden, *gates.arrays, *ups.arrays)


def gate_up_back_kernel(gates, ups, downs, tail, place, c_ref, by_gate_ref, by_up_ref, *refs):
    gate_refs, refs = refs[: len(gates)], refs[len(gates) :]
    up_refs, refs = refs[: len(ups)], refs[len(ups) :]
    down_refs, refs = refs[: len(downs)], refs[len(downs) :]
    dg_ref, du_ref, *dh_refs, gate_s, up_s, down_s, sum_s = refs
    step = pl.program_id(0)
    gates.join(place[0], gate_refs, gate_s)
    ups.join(place[0], up_refs, up_s)
    downs.join(place[0], down_refs, down_s)
    clear_tail(tail, gate_s, up_s, down_s)
    d_act = dot_nn(c_ref[...], down_s[...])
    by_gate, by_up = by_gate_ref[...].astype(F32), by_up_ref[...].astype(F32)
    if tail:
        last = step == pl.num_programs(0) - 1
        inside = lax.broadcasted_iota(jnp.int32, by_gate.shape, 1) < jnp.where(
            last, tail, by_gate.shape[1]
        )
        by_gate = jnp.where(inside, by_gate, 0.0)
        by_up = jnp.where(inside, by_up, 0.0)
    d_gate = (d_act * by_gate).astype(BF16)
    d_up = (d_act * by_up).astype(BF16)
    dg_ref[...] = d_gate
    du_ref[...] = d_up

    @pl.when(step == 0)
    def _():
        sum_s[...] = jnp.zeros_like(sum_s)

    sum_s[...] += dot_nt(d_gate, gate_s[...]) + dot_nt(d_up, up_s[...])

    @pl.when(step == pl.num_programs(0) - 1)
    def _():
        at = 0
        for dh_ref in dh_refs:
            cols = dh_ref.shape[1]
            dh_ref[...] = sum_s[:, at : at + cols].astype(BF16)
            at += cols


def gate_up_back(place, cotangent, by_gate, by_up, gates, ups, downs, depth, tf):
    rows, width = cotangent.shape
    units = by_gate.shape[1]
    gates, ups, downs = (Rows(p, depth, tf) for p in (gates, ups, downs))
    return call(
        functools.partial(gate_up_back_kernel, gates, ups, downs, units % tf),
        pl.cdiv(units, tf),
        [once((rows, width))]
        + [pl.BlockSpec((rows, tf), col_block)] * 2
        + gates.specs
        + ups.specs
        + downs.specs,
        [pl.BlockSpec((rows, tf), col_block)] * 2 + [once((rows, cut)) for cut in cuts(width)],
        [shape((rows, units), BF16)] * 2 + [shape((rows, cut), BF16) for cut in cuts(width)],
        [pltpu.VMEM((width, tf), BF16)] * 3 + [pltpu.VMEM((rows, width), F32)],
        60,
        62,
        "gate_up_back",
    )(place, cotangent, by_gate, by_up, *gates.arrays, *ups.arrays, *downs.arrays)


def whole_grad_kernel(left_ref, right_ref, out_ref):
    out_ref[...] = dot_nn(left_ref[...], right_ref[...]).astype(BF16)


def whole_grad(left_t, right, tf):
    width, rows = left_t.shape
    units = right.shape[1]
    return pl.pallas_call(
        whole_grad_kernel,
        grid=(pl.cdiv(units, tf),),
        in_specs=[once((width, rows)), pl.BlockSpec((rows, tf), col_block)],
        out_specs=pl.BlockSpec((width, tf), col_block),
        out_shape=shape((width, units), BF16),
        compiler_params=pltpu.CompilerParams(vmem_limit_bytes=48 * MIB),
        cost_estimate=cost(19 if units > 2048 else 6),
        name="whole_grad",
    )(left_t, right)


def weight_grad_kernel(depth, parts, place, left_ref, right_ref, keep_ref, send_ref):
    for j in range(parts):
        half = keep_ref if j % 2 == 0 else send_ref
        rows = pl.ds(pl.multiple_of((place[0] ^ j) * depth, 16), depth)
        at = (j // 2) * depth
        half[at : at + depth, :] = dot_nn(left_ref[rows, :], right_ref[...]).astype(BF16)


def weight_grad(place, left_t, right, parts, tf):
    width, rows = left_t.shape
    units = right.shape[1]
    return call(
        functools.partial(weight_grad_kernel, width // parts, parts),
        pl.cdiv(units, tf),
        [once((width, rows)), pl.BlockSpec((rows, tf), col_block)],
        [pl.BlockSpec((width // 2, tf), col_block)] * 2,
        [shape((width // 2, units), BF16)] * 2,
        [],
        48,
        19 if units > 2048 else 7,
        "weight_grad",
    )(place, left_t, right)


def add_kernel(counts, *refs):
    out_ref, at, col = refs[-1], 0, 0
    for count in counts:
        parts = refs[at : at + count]
        cols = parts[0].shape[1]
        total = sum(ref[...].astype(F32) for ref in parts)
        out_ref[:, col : col + cols] = total.astype(BF16)
        at, col = at + count, col + cols


def add_rows(rows, *groups):
    parts = [part for group in groups for part in group]
    cols = sum(group[0][0].shape[1] for group in groups)
    step = math.gcd(rows, 64, *[row for _, row in parts])
    return pl.pallas_call(
        functools.partial(add_kernel, [len(group) for group in groups]),
        grid=(rows // step,),
        in_specs=[
            pl.BlockSpec((step, array.shape[1]), lambda i, at=row // step: (at + i, 0))
            for array, row in parts
        ],
        out_specs=pl.BlockSpec((step, cols), lambda i: (i, 0)),
        out_shape=shape((rows, cols), BF16),
        compiler_params=pltpu.CompilerParams(vmem_limit_bytes=32 * MIB),
        cost_estimate=cost(4),
        name="add_rows",
    )(*[array for array, _ in parts])


def mark_kernel(place_ref, out_ref):
    for at in range(2):
        out_ref[at] = place_ref[at]


def mark(place):
    place.v = pl.pallas_call(
        mark_kernel,
        in_specs=[pl.BlockSpec(memory_space=pltpu.SMEM)],
        out_specs=pl.BlockSpec(memory_space=pltpu.SMEM),
        out_shape=shape((2,), jnp.int32),
        cost_estimate=cost(1),
        name="mark",
    )(place.v)
    return place


def down_project_kernel(downs, place, act_ref, *refs):
    down_refs, (out_ref, down_s, sum_s) = refs[: len(downs)], refs[len(downs) :]
    step = pl.program_id(0)
    downs.join(place[0], down_refs, down_s)

    @pl.when(step == 0)
    def _():
        sum_s[...] = jnp.zeros_like(sum_s)

    sum_s[...] += dot_nt(act_ref[...], down_s[...])

    @pl.when(step == pl.num_programs(0) - 1)
    def _():
        out_ref[...] = sum_s[...].astype(BF16)


def down_project(place, act, downs, width, depth, tf):
    rows, units = act.shape
    downs = Rows(downs, depth, tf)
    return call(
        functools.partial(down_project_kernel, downs),
        units // tf,
        [pl.BlockSpec((rows, tf), col_block)] + downs.specs,
        once((rows, width)),
        shape((rows, width), BF16),
        [pltpu.VMEM((width, tf), BF16), pltpu.VMEM((rows, width), F32)],
        48,
        24,
        "down_project",
    )(place, act, *downs.arrays)


def inverse_rms(values):
    return lax.rsqrt(jnp.mean(values * values, axis=-1, keepdims=True) + EPSILON)


def turned(values, cosine, sine):
    return values * cosine + pltpu.roll(values, HEAD // 2, 1) * sine


def mix_kernel(weight, group, place, x_ref, gain_ref, bias_ref, cos_ref, sin_ref, *refs):
    pieces, (q_ref, kv_ref, ht_ref, weight_s) = refs[: len(weight)], refs[len(weight) :]

    @pl.when(pl.program_id(0) == 0)
    def _():
        weight.join(place[0], pieces, weight_s)

    x = x_ref[...].astype(F32)
    hidden = (x * inverse_rms(x) * gain_ref[...].astype(F32)).astype(BF16)
    ht_ref[...] = hidden.T
    mixed = dot_nn(hidden, weight_s[...]) + bias_ref[...].astype(F32)
    cosine, sine = cos_ref[...], sin_ref[...]
    for h in range(group):
        at = slice(h * HEAD, (h + 1) * HEAD)
        q_ref[:, at] = turned(mixed[:, at], cosine, sine).astype(BF16)
    split = group * HEAD
    kv_ref[:, :HEAD] = turned(mixed[:, split : split + HEAD], cosine, sine).astype(BF16)
    kv_ref[:, HEAD:] = mixed[:, split + HEAD :].astype(BF16)


def mix(place, tokens, gain, bias, cosine, sine, pieces, depth, group, bq):
    rows, width = tokens.shape
    cols = pieces[0][2].shape[1]
    weight = Rows(pieces, depth)
    return call(
        functools.partial(mix_kernel, weight, group),
        rows // bq,
        [
            pl.BlockSpec((bq, width), row_block),
            once((1, width)),
            once((1, cols)),
            pl.BlockSpec((bq, HEAD), row_block),
            pl.BlockSpec((bq, HEAD), row_block),
        ]
        + weight.specs,
        [
            pl.BlockSpec((bq, group * HEAD), row_block),
            pl.BlockSpec((bq, 2 * HEAD), row_block),
            pl.BlockSpec((width, bq), col_block),
        ],
        [
            shape((rows, group * HEAD), BF16),
            shape((rows, 2 * HEAD), BF16),
            shape((width, rows), BF16),
        ],
        [pltpu.VMEM((width, cols), BF16)],
        32,
        8,
        "mix",
    )(place, tokens, gain[None], bias[None], cosine, sine, *weight.arrays)


def branch_kernel(weight, parts, place, x_ref, own_ref, upper_ref, lower_ref, gain_ref, *refs):
    own_w, other_w = refs[: len(weight)], refs[len(weight) : len(weight) + parts]
    mid_ref, h_ref, ht_ref, weight_s, att_s = refs[len(weight) + parts :]
    split = own_ref.shape[1]
    own_at = pl.multiple_of(place[1] * split, HEAD)
    other_at = pl.multiple_of((1 - place[1]) * split, HEAD)

    @pl.when(pl.program_id(0) == 0)
    def _():
        weight.join(place[0], own_w, weight_s, own_at)
        join(place[0], weight.depth, [(j, 0) for j in range(parts)], other_w, weight_s, other_at)

    att_s[:, pl.ds(own_at, split)] = own_ref[...]
    steps = pl.num_programs(0)

    @pl.when(pl.program_id(0) < steps // 2)
    def _():
        att_s[:, pl.ds(other_at, split)] = upper_ref[...]

    @pl.when(pl.program_id(0) >= steps // 2)
    def _():
        att_s[:, pl.ds(other_at, split)] = lower_ref[...]

    mid = x_ref[...].astype(F32) + dot_nt(att_s[...], weight_s[...])
    mid_ref[...] = mid
    hidden = (mid * inverse_rms(mid) * gain_ref[...].astype(F32)).astype(BF16)
    h_ref[...] = hidden
    ht_ref[...] = hidden.T


def branch(place, tokens, own, upper, lower, gain, pieces, other_pieces, depth, bq):
    rows, width = tokens.shape
    cols = own.shape[1]
    parts = width // depth
    weight = Rows(pieces, depth)
    wide = pl.BlockSpec((bq, width), row_block)
    narrow = pl.BlockSpec((bq, cols), row_block)
    other_specs = [once((depth, cols))] * parts
    half = rows // bq // 2
    return call(
        functools.partial(branch_kernel, weight, parts),
        rows // bq,
        [
            wide,
            narrow,
            pl.BlockSpec((bq, cols), lambda i, *_: (jnp.minimum(i, half - 1), 0)),
            pl.BlockSpec((bq, cols), lambda i, *_: (jnp.maximum(i - half, 0), 0)),
            once((1, width)),
        ]
        + weight.specs
        + other_specs,
        [wide, wide, pl.BlockSpec((width, bq), col_block)],
        [shape((rows, width), F32), shape((rows, width), BF16), shape((width, rows), BF16)],
        [pltpu.VMEM((width, 2 * cols), BF16), pltpu.VMEM((bq, 2 * cols), BF16)],
        40,
        12,
        "branch",
    )(place, tokens, own, upper, lower, gain[None], *weight.arrays, *other_pieces)


def middle_back_kernel(
    weight, group, place, mid_ref, c_ref, gain_ref, att_ref, *refs
):
    own_refs, other_refs, refs = refs[:CUTS], refs[CUTS : 2 * CUTS], refs[2 * CUTS :]
    pieces, refs = refs[: len(weight)], refs[len(weight) :]
    dm_ref, dbt_ref, da_ref, delta_ref, dgain_ref, weight_s = refs

    @pl.when(pl.program_id(0) == 0)
    def _():
        weight.join(place[0], pieces, weight_s)
        dgain_ref[...] = jnp.zeros_like(dgain_ref)

    mid = mid_ref[...]
    inverse = inverse_rms(mid)
    normed = mid * inverse
    own = jnp.concatenate([ref[...] for ref in own_refs], axis=1).astype(F32)
    other = jnp.concatenate([ref[...] for ref in other_refs], axis=1).astype(F32)
    dgain_ref[...] += jnp.sum(own * normed, axis=0, keepdims=True)
    scaled = (own + other) * gain_ref[...].astype(F32)
    d_mid = c_ref[...].astype(F32) + inverse * (
        scaled - normed * jnp.mean(scaled * normed, axis=-1, keepdims=True)
    )
    dm_ref[...] = d_mid
    d_branch = d_mid.astype(BF16)
    dbt_ref[...] = d_branch.T
    d_att = dot_nn(d_branch, weight_s[...]).astype(BF16)
    da_ref[...] = d_att
    product = d_att.astype(F32) * att_ref[...].astype(F32)
    for h in range(group):
        delta_ref[h : h + 1, :] = jnp.sum(
            product[:, h * HEAD : (h + 1) * HEAD].T, axis=0, keepdims=True
        )


def middle_back(place, own, other, mid, cotangent, gain, attended, pieces, depth, bq):
    rows, width = mid.shape
    cols = attended.shape[1]
    weight = Rows(pieces, depth)
    group = cols // HEAD
    wide = pl.BlockSpec((bq, width), row_block)
    narrow = pl.BlockSpec((bq, cols), row_block)
    return call(
        functools.partial(middle_back_kernel, weight, group),
        rows // bq,
        [wide, wide, once((1, width)), narrow]
        + [pl.BlockSpec((bq, cut), row_block) for cut in cuts(width)] * 2
        + weight.specs,
        [
            wide,
            pl.BlockSpec((width, bq), col_block),
            narrow,
            pl.BlockSpec((group, bq), col_block),
            pl.BlockSpec((1, width), whole_block),
        ],
        [
            shape((rows, width), F32),
            shape((width, rows), BF16),
            shape((rows, cols), BF16),
            shape((group, rows), F32),
            shape((1, width), F32),
        ],
        [pltpu.VMEM((width, cols), BF16)],
        48,
        13,
        "middle_back",
    )(place, mid, cotangent, gain[None], attended, *own, *other, *weight.arrays)


def mix_back_kernel(
    weight, group, place, dq_ref, dkv_ref, cos_ref, sin_ref, x_ref, *refs
):
    pieces, refs = refs[: len(weight)], refs[len(weight) :]
    dm_ref, dbias_ref, dgain_ref, *dh_refs, weight_s = refs

    @pl.when(pl.program_id(0) == 0)
    def _():
        weight.join(place[0], pieces, weight_s)
        dgain_ref[...] = jnp.zeros_like(dgain_ref)
        dbias_ref[...] = jnp.zeros_like(dbias_ref)

    split = group * HEAD
    dm_ref[:, :split] = dq_ref[...]
    d_keys = dkv_ref[:, :HEAD].astype(F32)
    dm_ref[:, split : split + HEAD] = turned(d_keys, cos_ref[...], -sin_ref[...]).astype(BF16)
    dm_ref[:, split + HEAD :] = dkv_ref[:, HEAD:]
    d_mixed = dm_ref[...]
    dbias_ref[...] += jnp.sum(d_mixed.astype(F32), axis=0, keepdims=True)
    d_hidden = dot_nt(d_mixed, weight_s[...])
    x = x_ref[...].astype(F32)
    dgain_ref[...] += jnp.sum(d_hidden * (x * inverse_rms(x)), axis=0, keepdims=True)
    at = 0
    for dh_ref in dh_refs:
        cols = dh_ref.shape[1]
        dh_ref[...] = d_hidden[:, at : at + cols].astype(BF16)
        at += cols


def mix_back(place, dq, dkv, cosine, sine, tokens, pieces, depth, bq):
    rows, width = tokens.shape
    cols = pieces[0][2].shape[1]
    weight = Rows(pieces, depth)
    group = dq.shape[1] // HEAD
    wide = pl.BlockSpec((bq, width), row_block)
    return call(
        functools.partial(mix_back_kernel, weight, group),
        rows // bq,
        [
            pl.BlockSpec((bq, group * HEAD), row_block),
            pl.BlockSpec((bq, 2 * HEAD), row_block),
            pl.BlockSpec((bq, HEAD), row_block),
            pl.BlockSpec((bq, HEAD), row_block),
            wide,
        ]
        + weight.specs,
        [
            pl.BlockSpec((bq, cols), row_block),
            pl.BlockSpec((1, cols), whole_block),
            pl.BlockSpec((1, width), whole_block),
        ]
        + [pl.BlockSpec((bq, cut), row_block) for cut in cuts(width)],
        [
            shape((rows, cols), BF16),
            shape((1, cols), F32),
            shape((1, width), F32),
        ]
        + [shape((rows, cut), BF16) for cut in cuts(width)],
        [pltpu.VMEM((width, cols), BF16)],
        32,
        8,
        "mix_back",
    )(place, dq, dkv, cosine, sine, tokens, *weight.arrays)


def input_back_kernel(place, x_ref, gain_ref, dm_ref, *refs):
    own_refs, other_refs, (out_ref,) = refs[:CUTS], refs[CUTS : 2 * CUTS], refs[2 * CUTS :]
    own = jnp.concatenate([ref[...] for ref in own_refs], axis=1).astype(F32)
    other = jnp.concatenate([ref[...] for ref in other_refs], axis=1).astype(F32)
    x = x_ref[...].astype(F32)
    inverse = inverse_rms(x)
    normed = x * inverse
    scaled = (own + other) * gain_ref[...].astype(F32)
    out_ref[...] = dm_ref[...] + inverse * (
        scaled - normed * jnp.mean(scaled * normed, axis=-1, keepdims=True)
    )


def input_back(place, own, other, tokens, gain, d_mid, bq):
    rows, width = tokens.shape
    wide = pl.BlockSpec((bq, width), row_block)
    return call(
        input_back_kernel,
        rows // bq,
        [wide, once((1, width)), wide]
        + [pl.BlockSpec((bq, cut), row_block) for cut in cuts(width)] * 2,
        wide,
        shape((rows, width), F32),
        [],
        32,
        8,
        "input_back",
    )(place, tokens, gain[None], d_mid, *own, *other)


class Box:
    def __init__(self, v):
        self.v = v


def boxes(values):
    return [Box(v) for v in values]


def fence(*items):
    flat = []
    for item in items:
        flat += item if isinstance(item, (list, tuple)) else [item]
    for item, v in zip(flat, lax.optimization_barrier([item.v for item in flat])):
        item.v = v


def held(value, *items):
    one = Box(value)
    fence(one, *items)
    return one.v


def swap(value, axis, size, bit):
    return lax.ppermute(value, axis, [(i, i ^ bit) for i in range(size)])


class Pieces:
    def __init__(self, own, size, slabs=1):
        if size != 4 or own.shape[0] % (16 * slabs):
            slabs = 1
        self.size, self.own, self.slabs = size, own, slabs
        self.depth = own.shape[0] // slabs
        self.got = {}

    def away(self, own):
        got, bit = {0: own}, self.size // 2
        while bit > 1:
            got.update({j ^ bit: swap(p, "shard", self.size, bit) for j, p in got.items()})
            bit //= 2
        return {j: Box(p) for j, p in got.items() if j}

    def far(self, slab, *first):
        if slab >= self.slabs:
            return []
        own = held(self.own, *first)[slab * self.depth : (slab + 1) * self.depth]
        got = self.away(own)
        self.got.update({(j, slab): p for j, p in got.items()})
        return list(got.values())

    def far_by_ctx(self, contexts, *first):
        rows = self.own.shape[0] // contexts
        own = lax.dynamic_slice_in_dim(
            held(self.own, *first), lax.axis_index("ctx") * rows, rows, 0
        )
        self.parts = self.away(own)
        return list(self.parts.values())

    def spread(self):
        for j, part in self.parts.items():
            self.got[j, 0] = Box(lax.all_gather(part.v, "ctx", axis=0, tiled=True))
        return [self.got[j, 0] for j in self.parts]

    def near_own(self, *first):
        self.near = Box(swap(held(self.own, *first), "shard", self.size, 1))
        return [self.near]

    def near_rest(self, slab, *first):
        if slab >= self.slabs:
            return []
        far = [j for j in range(2, self.size, 2)]
        if first:
            fence(*[self.got[j, slab] for j in far], *first)
        for j in far:
            self.got[j ^ 1, slab] = Box(swap(self.got[j, slab].v, "shard", self.size, 1))
        return [self.got[j ^ 1, slab] for j in far]

    def all(self):
        found = [(0, 0, self.own), (1, 0, self.near.v)]
        found += [
            (j, k * self.depth, p.v) for (j, k), p in sorted(self.got.items(), key=lambda i: i[0])
        ]
        return found


class Reduction:
    def __init__(self, shards, contexts, slabs):
        self.shards, self.chain = shards, contexts == 4
        self.slabs = slabs if shards == 4 else 1
        self.keep, self.send, self.got = [], [], []
        self.own, self.one, self.two, self.three = {}, {}, {}, {}
        self.by_sum = {}

    def make(self, place, left_t, right, tf):
        keep, send = boxes(weight_grad(place.v, left_t, right, self.shards, tf))
        self.keep.append(keep)
        self.send.append(send)
        return send

    def cores(self):
        self.got.append(Box(swap(self.send[len(self.got)].v, "shard", self.shards, 1)))
        return self.got[-1]

    def pairs(self, row):
        return [[(keep.v, row), (got.v, row)] for keep, got in zip(self.keep, self.got)]

    def sum_away(self):
        rows = self.keep[0].v.shape[0]
        if self.shards == 4:
            size = rows // 2 // self.slabs
            self.away = [
                Box(add_rows(size, *self.pairs(rows // 2 + slab * size)))
                for slab in range(self.slabs)
            ]
        else:
            self.away = [Box(add_rows(rows, *self.pairs(0)))]
        return self.away

    def chips(self):
        if self.shards == 4:
            self.last = [Box(swap(part.v, "shard", 4, 2)) for part in self.away]
            return self.last
        held, bit, count = self.away[0].v, 2, self.shards // 2
        while bit < self.shards:
            size = held.shape[0] // count
            blocks = [held[at * size : (at + 1) * size] for at in range(count)]
            away = swap(jnp.concatenate(blocks[1::2], axis=0), "shard", self.shards, bit)
            here = jnp.concatenate(blocks[::2], axis=0)
            held = here if 2 * bit >= self.shards else here + away
            bit, count = 2 * bit, count // 2
        self.here, self.last = held, boxes([away])
        return self.last

    def arrived(self, slab):
        if slab >= self.slabs:
            return []
        last = self.last[slab].v
        if self.shards != 4:
            self.own[slab] = Box(self.here + last)
        elif len(self.keep) == 1:
            size = last.shape[0]
            self.own[slab] = Box(add_rows(size, self.pairs(slab * size)[0] + [(last, 0)]))
        else:
            size = last.shape[0]
            here = add_rows(size, *self.pairs(slab * size))
            self.own[slab] = Box(add_rows(size, [(here, 0), (last, 0)]))
        return [self.own[slab]]

    def whole_sum(self, slab):
        if slab >= self.slabs:
            return []
        self.by_sum[slab] = Box(lax.psum(self.own[slab].v, "ctx"))
        return [self.by_sum[slab]]

    def inward(self, slab):
        if slab >= self.slabs:
            return []
        if not self.chain:
            return self.whole_sum(slab)
        self.one[slab] = Box(lax.ppermute(self.own[slab].v, "ctx", [(0, 1), (3, 2)]))
        return [self.one[slab]]

    def middle(self, slab):
        if not self.chain or slab >= self.slabs:
            return []
        self.own[slab] = Box(self.own[slab].v + self.one[slab].v)
        self.two[slab] = Box(lax.ppermute(self.own[slab].v, "ctx", [(1, 2), (2, 1)]))
        return [self.two[slab]]

    def outward(self, slab):
        if not self.chain or slab >= self.slabs:
            return []
        self.own[slab] = Box(self.own[slab].v + self.two[slab].v)
        self.three[slab] = Box(lax.ppermute(self.own[slab].v, "ctx", [(1, 0), (2, 3)]))
        return [self.three[slab]]

    def result(self):
        place = lax.axis_index("ctx")
        inside = (place == 1) | (place == 2)
        totals = [
            self.by_sum[slab].v
            if slab in self.by_sum
            else jnp.where(inside, self.own[slab].v, self.three[slab].v)
            for slab in range(self.slabs)
        ]
        whole = totals[0] if len(totals) == 1 else jnp.concatenate(totals, axis=0)
        return whole.astype(F32)


def tree_tables(seg_row, parent_row):
    seg_count = parent_row.shape[0]
    seg_ids = jnp.arange(seg_count, dtype=jnp.int32)
    one_hot = (seg_row[:, None] == seg_ids[None, :]).astype(jnp.int32)
    lengths = jnp.sum(one_hot, axis=0, dtype=jnp.int32)
    before = seg_ids[None, :] < seg_ids[:, None]
    starts = jnp.sum(jnp.where(before, lengths[None, :], 0), axis=1, dtype=jnp.int32)
    link = (parent_row[:, None] == seg_ids[None, :]) & (parent_row[:, None] != seg_ids[:, None])
    twice = jnp.any(link[:, :, None] & link[None, :, :], axis=1)
    strict = link | twice
    padding = parent_row == seg_ids
    reach = strict | ((seg_ids[:, None] == seg_ids[None, :]) & ~padding[:, None])
    offsets = jnp.sum(jnp.where(strict, lengths[None, :], 0), axis=1, dtype=jnp.int32) - starts
    return reach, offsets


def block_lists(row_hot, col_hot, reach, col_places, row_first, bq, bk):
    segs = reach.shape[0]
    row_has = jnp.any(row_hot.reshape(-1, bq, segs), axis=1)
    col_has = jnp.any(col_hot.reshape(-1, bk, segs), axis=1)
    row_blocks, col_blocks = row_has.shape[0], col_has.shape[0]
    row_reach = jnp.any(row_has[:, :, None] & reach[None], axis=1)
    meets = jnp.any(row_reach[:, None, :] & col_has[None], axis=2)
    col_at = col_places.reshape(-1, bk)[:, 0]
    row_at = row_first + bq * jnp.arange(row_blocks, dtype=jnp.int32)
    causal = col_at[None, :] < row_at[:, None] + bq
    diagonal = causal & (col_at[None, :] + bk > row_at[:, None])
    active = ((meets & causal) | diagonal) & (col_at >= 0)[None, :]
    ids = jnp.arange(col_blocks, dtype=jnp.int32)
    rank = jnp.sum(
        (active[:, None, :] & (ids[None, :] < ids[:, None])[None]).astype(jnp.int32), axis=2
    )
    placed = active[:, :, None] & (rank[:, :, None] == ids[None, None, :])
    chosen = jnp.sum(jnp.where(placed, ids[None, :, None], 0), axis=1, dtype=jnp.int32)
    count = jnp.sum(active.astype(jnp.int32), axis=1, dtype=jnp.int32)
    places = jnp.concatenate([col_at, row_first[None]])
    return count, chosen.reshape(-1), places


def layer(
    sizes, tokens, cotangent, segment, parent, gain_attn, qkv_weight, qkv_bias,
    out_weight, gain_ffn, gate_weight, up_weight, down_weight,
):
    shards, contexts, halves = sizes["shard"], sizes["ctx"], sizes["tp"]
    rows, width = tokens.shape
    group = out_weight.shape[1] // HEAD
    shard, ctx, half = lax.axis_index("shard"), lax.axis_index("ctx"), lax.axis_index("tp")
    place = jnp.stack([shard, half]).astype(jnp.int32)
    across = [(i, i ^ 1) for i in range(halves)]

    row_first = (ctx * rows).astype(jnp.int32)
    reach, offsets = tree_tables(segment[0], parent[0])
    seg_ids = jnp.arange(reach.shape[0], dtype=jnp.int32)
    behind = [jnp.maximum(ctx - k, 0) * rows for k in range(contexts)]
    seg_back = jnp.concatenate(
        [lax.dynamic_slice_in_dim(segment[0], at, rows, 0) for at in behind]
    )
    places_back = jnp.concatenate(
        [(ctx - k) * rows + jnp.arange(rows, dtype=jnp.int32) for k in range(contexts)]
    )
    col_hot = seg_back[:, None] == seg_ids[None, :]
    row_hot = col_hot[:rows]
    own_pos = places_back[:rows] + jnp.sum(
        jnp.where(row_hot, offsets[None, :], 0), axis=1, dtype=jnp.int32
    )
    pad = ((0, 0), (0, HEAD - reach.shape[0]))
    row_reach = jnp.any(row_hot[:, :, None] & reach[None], axis=1)
    reach_rows = jnp.pad(row_reach.astype(BF16), pad)
    hot = jnp.pad(col_hot.astype(BF16), pad)
    bq = math.gcd(rows, 256)
    bk_f, bk_b = math.gcd(rows, 128), math.gcd(rows, 512)
    lists_f = block_lists(row_hot, col_hot, reach, places_back, row_first, bq, bk_f)
    lists_b = block_lists(row_hot, col_hot, reach, places_back, row_first, bq, bk_b)
    lane = jnp.arange(HEAD, dtype=jnp.int32)
    frequency = THETA ** (-2.0 * (lane % (HEAD // 2)).astype(F32) / HEAD)
    angles = own_pos.astype(F32)[:, None] * frequency[None, :]
    cosine = jnp.cos(angles)
    sine = jnp.sin(angles) * jnp.where(lane < HEAD // 2, -1.0, 1.0)

    depth = width // shards
    qkv, out_w, gate, up, down = (
        Pieces(qkv_weight, shards),
        Pieces(out_weight, shards),
        Pieces(gate_weight, shards, 3),
        Pieces(up_weight, shards),
        Pieces(down_weight, shards, 4),
    )

    def over_tp(box):
        return Box(lax.ppermute(box.v, "tp", across))

    qkv_far = qkv.far(0)
    leaves, tree = jax.tree.flatten((reach_rows, hot, lists_f, lists_b, cosine, sine))
    leaves, place = boxes(leaves), Box(place)
    fence(leaves, place, qkv_far)
    reach_rows, hot, lists_f, lists_b, cosine, sine = tree.unflatten([leaf.v for leaf in leaves])
    qkv_near = qkv.near_own(qkv_far) + qkv.near_rest(0)
    out_far = out_w.far(0, qkv_far)
    out_near = out_w.near_own(qkv_far)
    out_other = {0: Box(lax.ppermute(held(out_weight, qkv_far), "tp", across))}
    fence(mark(place), qkv_near)
    up_parts = up.far_by_ctx(contexts, qkv_near)

    queries, kv_own, hidden_one_t = mix(
        place.v, tokens, gain_attn, qkv_bias, cosine, sine, qkv.all(), depth, group, bq
    )
    kv_own = Box(kv_own)
    fence(kv_own, out_near, place)
    kv = [kv_own]
    rightward = [(i, i + 1) for i in range(contexts - 1)]
    for k in range(1, contexts):
        kv.append(Box(lax.ppermute(kv[-1].v, "ctx", rightward)))
        if k == 1:
            out_other[1] = over_tp(out_w.near)
            out_rest = out_w.near_rest(0, kv_own)
            fence(mark(place), kv, out_rest, out_far, out_other[0])
        elif k == 2:
            gate_far = gate.far(0, kv[1])
            out_other.update({j: over_tp(piece) for (j, _), piece in out_w.got.items()})
            top_grad_t = Box(held(cotangent, *kv).T)
            fence(mark(place), kv, out_other[1], up_parts)
        elif k == contexts - 1:
            fence(mark(place), kv, gate_far, top_grad_t)
            fence(kv, up_parts)
        else:
            fence(mark(place), kv)
    kv_back = jnp.concatenate([p.v for p in kv], axis=0)
    up_spread = up.spread()
    gate_far = gate.far(1, kv)
    out_other = [out_other[j] for j in range(shards)]
    upper_rows = rows // 2
    upper, *upper_sums = attention_forward(
        lists_f, queries, kv_back, reach_rows, hot, bq, bk_f, 0, upper_rows
    )
    upper, leaves = Box(upper), boxes(lists_f)
    fence(upper, leaves, out_other)
    upper_other = over_tp(upper)
    gate_far_2 = gate.far(2, upper)
    lower, *lower_sums = attention_forward(
        [leaf.v for leaf in leaves], queries, kv_back, reach_rows, hot, bq, bk_f, upper_rows,
        upper_rows,
    )
    lower = Box(lower)
    fence(lower, gate_far, place, upper_other)
    lower_other = over_tp(lower)
    gate_rest = gate.near_rest(0) + gate.near_rest(1, lower)
    attended = Box(jnp.concatenate([upper.v, lower.v], axis=0))
    lse, tops = (jnp.concatenate(both, axis=1) for both in zip(upper_sums, lower_sums))
    attended_other = lower_other
    fence(mark(place), lower_other, gate_far_2, gate_rest, up_spread, attended)
    down_far = down.far(0, attended_other)
    gate_rest = gate.near_rest(2) + up.near_rest(0)
    own_near = gate.near_own(attended_other) + up.near_own(attended_other)
    mid, hidden_two, hidden_two_t = branch(
        place.v, tokens, attended.v, upper_other.v, lower_other.v, gain_ffn, out_w.all(),
        [p.v for p in out_other], depth, bq,
    )
    mid = Box(mid)
    fence(mid, gate_rest, own_near, place, down_far)
    down_far = down.far(1, mid) + down.far(2, mid)
    down_near = down.near_own(mid)
    act, by_gate, by_up = gate_up(place.v, hidden_two, gate.all(), up.all(), depth, 512)
    act = Box(act)
    fence(act, down_far, down_near, top_grad_t, place)
    down_far = down.far(3, act)
    down_rest = down.near_rest(0, act) + down.near_rest(1) + down.near_rest(2)
    down_part = Box(whole_grad(top_grad_t.v, act.v, 512))
    fence(down_part, down_rest, down_far, place)
    down_part = Box(lax.psum_scatter(down_part.v, ("shard", "ctx"), scatter_dimension=0, tiled=True))
    down_rest = down.near_rest(3)
    fence(mark(place), down_rest)
    d_gate, d_up, *d_hidden_two = gate_up_back(
        place.v, cotangent, by_gate, by_up, gate.all(), up.all(), down.all(), depth, 512
    )

    d_hidden_two = boxes(d_hidden_two)
    gate_grad = Reduction(shards, contexts, 2)
    up_grad = Reduction(shards, contexts, 2)
    last_grad = Reduction(shards, contexts, 1)
    fence(place, d_hidden_two)
    other = [over_tp(d_hidden_two[0])]
    fence(place, gate_grad.make(place, hidden_two_t, d_gate, 512), other[0], d_hidden_two[1])
    gate_got = gate_grad.cores()
    other.append(over_tp(d_hidden_two[1]))
    fence(
        place, up_grad.make(place, hidden_two_t, d_up, 512), gate_got, other[1], d_hidden_two[2], act
    )
    up_got = up_grad.cores()
    other.append(over_tp(d_hidden_two[2]))
    fence(place, gate_grad.sum_away())
    gate_last = gate_grad.chips()
    ffn_own = Box(down_project(place.v, act.v, down.all(), width, depth, 896))
    fence(place, ffn_own, up_got, other[2], down_part)
    down_total = Box(lax.all_gather(down_part.v, "ctx", axis=0, tiled=True))
    ffn_other = over_tp(ffn_own)
    fence(place, up_grad.sum_away())
    up_last = up_grad.chips()

    d_mid, d_branch_t, d_att, delta, gain_two_part = middle_back(
        place.v, [p.v for p in d_hidden_two], [p.v for p in other], mid.v, cotangent, gain_ffn,
        attended.v, out_w.all(), depth, bq,
    )
    d_mid = Box(d_mid)
    fence(place, d_mid)
    out_sent = last_grad.make(place, d_branch_t, attended.v, 768)
    leaves = boxes(lists_b)
    fence(place, out_sent, gate_last[:1])
    out_got = last_grad.cores()
    fence(leaves, gate_grad.arrived(0))
    gate_one = gate_grad.inward(0)
    d_query, d_kv = attention_backward(
        [leaf.v for leaf in leaves], queries, d_att, lse, delta, kv_back, reach_rows, hot,
        cosine, sine, bq, bk_b,
    )
    d_kv = Box(d_kv)
    fence(d_kv, gate_one, gate_last[1:], out_got, ffn_other, mid, place)
    output = (mid.v + (ffn_own.v.astype(F32) + ffn_other.v.astype(F32))).astype(BF16)
    output = Box(output)
    leftward = [(i + 1, i) for i in range(contexts - 1)]
    d_kv_own = Box(d_kv.v[(contexts - 1) * rows :])
    for k in range(contexts - 2, -1, -1):
        got = Box(lax.ppermute(d_kv_own.v, "ctx", leftward))
        if k == contexts - 2:
            fence(got, output, gate_grad.arrived(1), gate_grad.own[0])
            gate_two = gate_grad.middle(0)
            gate_one = gate_grad.inward(1)
        elif k == 0:
            fence(mark(place), got, down_total, up_grad.arrived(0), gate_one, gate_two, up_last[1:])
        else:
            fence(mark(place), got, up_last[:1])
        d_kv_own = Box(d_kv.v[k * rows : (k + 1) * rows] + got.v)
    gate_three = gate_grad.outward(0)
    gate_two = gate_grad.middle(1)
    up_one = up_grad.inward(0)
    fence(place, d_kv_own, list(gate_grad.own.values()))
    d_mixed, bias_part, gain_one_part, *d_hidden_one = mix_back(
        place.v, d_query, d_kv_own.v, cosine, sine, tokens, qkv.all(), depth, bq
    )
    peak_own = jnp.max(tops, axis=1)
    device = shard * contexts + ctx
    spread = jnp.where(
        (jnp.arange(shards * contexts)[:, None, None] == device)
        & (jnp.arange(halves)[None, :, None] == half),
        peak_own[None, None, :],
        0.0,
    )
    bias_both = jnp.where(jnp.arange(halves)[:, None] == half, bias_part, 0.0)
    vector = Box(
        jnp.concatenate(
            [gain_one_part[0], gain_two_part[0], bias_both.reshape(-1), spread.reshape(-1)]
        )
    )
    d_hidden_one = boxes(d_hidden_one)
    fence(place, vector, d_hidden_one)

    def hop(axis, bit):
        vector.v = vector.v + swap(vector.v, axis, sizes[axis], bit)
        return vector

    back = [over_tp(d_hidden_one[0])]
    q_sent = last_grad.make(place, hidden_one_t, d_mixed, 512)
    fence(place, q_sent, back[0], d_hidden_one[1], up_grad.arrived(1))
    qkv_got = last_grad.cores()
    back.append(over_tp(d_hidden_one[1]))
    hop("shard", 1)
    fence(mark(place), qkv_got, gate_two, up_one, vector)
    up_two = up_grad.middle(0)
    up_one = up_grad.inward(1)
    gate_three += gate_grad.outward(1)
    bit = 2
    while bit < shards:
        hop("shard", bit)
        bit *= 2
    fence(place, last_grad.sum_away(), vector)
    last_last = last_grad.chips()
    hop("tp", 1)
    fence(mark(place), up_two, up_one, vector, last_last, back[1], d_hidden_one[2])
    back.append(over_tp(d_hidden_one[2]))
    vectors = Reduction(shards, contexts, 1)
    vectors.own[0] = vector
    up_three = up_grad.outward(0)
    up_two = up_grad.middle(1)
    last_grad.arrived(0)
    last_one = last_grad.inward(0) + vectors.inward(0)
    fence(mark(place), up_two, last_one, back[2], d_mid)
    up_three += up_grad.outward(1)
    last_two = last_grad.middle(0) + vectors.middle(0)
    input_grad = Box(
        input_back(
            place.v, [p.v for p in d_hidden_one], [p.v for p in back], tokens, gain_attn, d_mid.v, bq
        )
    )
    fence(input_grad, last_two, place)
    last_three = last_grad.outward(0) + vectors.outward(0)
    vector = Box(vectors.result())
    gate_total, up_total, last_total = (one.result() for one in (gate_grad, up_grad, last_grad))
    out_total = last_total[:, : out_weight.shape[1]]
    qkv_total = last_total[:, out_weight.shape[1] :]
    down_total, input_grad, output, vector = (
        down_total.v.astype(F32), input_grad.v, output.v, vector.v
    )
    bias_at = 2 * width
    spread_at = bias_at + bias_both.size
    bias_grad = lax.dynamic_slice_in_dim(
        vector[bias_at:spread_at], half * bias_part.size, bias_part.size, 0
    )
    peaks = jnp.max(vector[spread_at:].reshape(shards * contexts, halves, group), axis=0)
    peak_all = lax.dynamic_index_in_dim(peaks, half, 0, keepdims=False)
    clip_out = CLIP_BOUND / jnp.maximum(peak_all, CLIP_BOUND)
    return (
        output,
        input_grad,
        vector[:width],
        qkv_total,
        bias_grad,
        out_total,
        vector[width:bias_at],
        gate_total,
        up_total,
        down_total,
        clip_out,
    )


def solution(mesh):
    token = P(("shard", "ctx"), None)
    weight = P("shard", "tp")
    return jax.shard_map(
        functools.partial(layer, dict(mesh.shape)),
        mesh=mesh,
        in_specs=(
            token,
            token,
            P("shard", None),
            P("shard", None),
            P(),
            weight,
            P("tp"),
            weight,
            P(),
            weight,
            weight,
            weight,
        ),
        out_specs=(
            token,
            token,
            P(),
            weight,
            P("tp"),
            weight,
            P(),
            weight,
            weight,
            weight,
            P("tp"),
        ),
        check_vma=False,
    )
```

```python
import functools
import math

import jax
import jax.numpy as jnp
from jax import lax
from jax.experimental import pallas as pl
from jax.experimental.pallas import tpu as pltpu
from jax.sharding import PartitionSpec as P

HEAD = 128
EPSILON = 1e-06
THETA = 1000000.0
CLIP_BOUND = 4.0
NEG_FILL = -1e30
SCALE = HEAD ** (-0.5)
SCALE_2 = SCALE * math.log2(math.e)
MIB = 1 << 20
CUTS = 3


def cuts(width):
    return [width // 4, width // 4, width // 2]


PACE = 175_000_000


def cost(us):
    return pl.CostEstimate(flops=int(us * PACE), bytes_accessed=1000, transcendentals=0)


BF16 = jnp.bfloat16
F32 = jnp.float32


def dot_nt(left, right):
    return lax.dot_general(left, right, (((1,), (1,)), ((), ())), preferred_element_type=F32)


def dot_nn(left, right):
    return jnp.dot(left, right, preferred_element_type=F32)


def seen_block(hot, reach_rows, col_at, row_at, bk, bq):
    linked = dot_nt(hot, reach_rows) > 0.5
    cols = col_at + lax.broadcasted_iota(jnp.int32, (bk, bq), 0)
    rows = row_at + lax.broadcasted_iota(jnp.int32, (bk, bq), 1)
    return (linked & (cols <= rows)) | (cols == rows)


def attention_forward_kernel(
    group, bq, bk, blocks, first, count, chosen, places, q_ref, kv_ref, reach_ref, hot_ref,
    out_ref, lse_ref, top_ref, max_s, sum_s, acc_s,
):
    row_block = pl.program_id(0) + first
    max_s[...] = jnp.full_like(max_s, NEG_FILL)
    sum_s[...] = jnp.zeros_like(sum_s)
    acc_s[...] = jnp.zeros_like(acc_s)
    row_at = places[blocks] + row_block * bq

    def body(step, carry):
        block = chosen[row_block * blocks + step]
        here = pl.ds(pl.multiple_of(block * bk, bk), bk)
        keys = kv_ref[here, :HEAD]
        values_t = kv_ref[here, HEAD:].T
        seen = seen_block(hot_ref[here, :], reach_ref[...], places[block], row_at, bk, bq)
        for h in range(group):
            score = jnp.where(seen, dot_nt(keys, q_ref[:, h * HEAD : (h + 1) * HEAD]), NEG_FILL)
            old = max_s[h : h + 1, :]
            new = jnp.maximum(old, jnp.max(score, axis=0, keepdims=True))
            prob = jnp.exp2((score - new) * SCALE_2)
            fade = jnp.exp2((old - new) * SCALE_2)
            max_s[h : h + 1, :] = new
            sum_s[h : h + 1, :] = sum_s[h : h + 1, :] * fade + jnp.sum(prob, axis=0, keepdims=True)
            acc_s[h] = acc_s[h] * fade + dot_nn(values_t, prob.astype(BF16))
        return carry

    lax.fori_loop(0, count[row_block], body, 0)
    top_ref[...] = max_s[...] * SCALE
    lse_ref[...] = max_s[...] * SCALE_2 + jnp.log2(sum_s[...])
    for h in range(group):
        out_ref[:, h * HEAD : (h + 1) * HEAD] = (acc_s[h] / sum_s[h : h + 1, :]).T.astype(BF16)


def attention_forward(lists, queries, kv, reach_rows, hot, bq, bk, first, rows):
    width = queries.shape[1]
    first //= bq
    slots = kv.shape[0]
    group = width // HEAD
    whole = lambda *_: (0, 0)
    row = lambda i, *_: (i, 0)
    col = lambda i, *_: (0, i)
    return pl.pallas_call(
        functools.partial(attention_forward_kernel, group, bq, bk, slots // bk, first),
        grid_spec=pltpu.PrefetchScalarGridSpec(
            num_scalar_prefetch=3,
            grid=(rows // bq,),
            in_specs=[
                pl.BlockSpec((bq, width), lambda i, *_: (i + first, 0)),
                pl.BlockSpec((slots, 2 * HEAD), whole),
                pl.BlockSpec((bq, HEAD), lambda i, *_: (i + first, 0)),
                pl.BlockSpec((slots, HEAD), whole),
            ],
            out_specs=[
                pl.BlockSpec((bq, width), row),
                pl.BlockSpec((group, bq), col),
                pl.BlockSpec((group, bq), col),
            ],
            scratch_shapes=[
                pltpu.VMEM((group, bq), F32),
                pltpu.VMEM((group, bq), F32),
                pltpu.VMEM((group, HEAD, bq), F32),
            ],
        ),
        out_shape=[
            jax.ShapeDtypeStruct((rows, width), BF16),
            jax.ShapeDtypeStruct((group, rows), F32),
            jax.ShapeDtypeStruct((group, rows), F32),
        ],
        compiler_params=pltpu.CompilerParams(vmem_limit_bytes=32 * MIB),
        cost_estimate=cost(15),
        name="attention_forward",
    )(*lists, queries, kv, reach_rows, hot)


def attention_backward_kernel(
    group, bq, bk, blocks, count, chosen, places, q_ref, do_ref, lse_ref, delta_ref, kv_ref,
    reach_ref, hot_ref, cos_ref, sin_ref, dq_ref, dkv_ref, acc_s, dk_s, dv_s,
):
    row_block = pl.program_id(0)

    @pl.when(row_block == 0)
    def _():
        dk_s[...] = jnp.zeros_like(dk_s)
        dv_s[...] = jnp.zeros_like(dv_s)

    acc_s[...] = jnp.zeros_like(acc_s)
    row_at = places[blocks] + row_block * bq

    def body(step, carry):
        block = chosen[row_block * blocks + step]
        here = pl.ds(pl.multiple_of(block * bk, bk), bk)
        keys = kv_ref[here, :HEAD]
        values = kv_ref[here, HEAD:]
        keys_t = keys.T
        seen = seen_block(hot_ref[here, :], reach_ref[...], places[block], row_at, bk, bq)
        dk = jnp.zeros((bk, HEAD), F32)
        dv = jnp.zeros((bk, HEAD), F32)
        for h in range(group):
            qh = q_ref[:, h * HEAD : (h + 1) * HEAD]
            doh = do_ref[:, h * HEAD : (h + 1) * HEAD]
            prob = jnp.where(
                seen, jnp.exp2(dot_nt(keys, qh) * SCALE_2 - lse_ref[h : h + 1, :]), 0.0
            )
            ds = (prob * (dot_nt(values, doh) - delta_ref[h : h + 1, :])).astype(BF16)
            dv = dv + dot_nn(prob.astype(BF16), doh)
            dk = dk + dot_nn(ds, qh)
            acc_s[h] = acc_s[h] + dot_nn(keys_t, ds)
        dk_s[here, :] += dk
        dv_s[here, :] += dv
        return carry

    lax.fori_loop(0, count[row_block], body, 0)
    for h in range(group):
        d_query = (acc_s[h] * SCALE).T
        dq_ref[:, h * HEAD : (h + 1) * HEAD] = turned(
            d_query, cos_ref[...], -sin_ref[...]
        ).astype(BF16)

    @pl.when(row_block == pl.num_programs(0) - 1)
    def _():
        dkv_ref[:, :HEAD] = (dk_s[...] * SCALE).astype(BF16)
        dkv_ref[:, HEAD:] = dv_s[...].astype(BF16)


def attention_backward(
    lists, queries, d_att, lse, delta, kv, reach_rows, hot, cosine, sine, bq, bk
):
    rows, width = queries.shape
    slots = kv.shape[0]
    group = width // HEAD
    whole = lambda *_: (0, 0)
    row = lambda i, *_: (i, 0)
    col = lambda i, *_: (0, i)
    return pl.pallas_call(
        functools.partial(attention_backward_kernel, group, bq, bk, slots // bk),
        grid_spec=pltpu.PrefetchScalarGridSpec(
            num_scalar_prefetch=3,
            grid=(rows // bq,),
            in_specs=[
                pl.BlockSpec((bq, width), row),
                pl.BlockSpec((bq, width), row),
                pl.BlockSpec((group, bq), col),
                pl.BlockSpec((group, bq), col),
                pl.BlockSpec((slots, 2 * HEAD), whole),
                pl.BlockSpec((bq, HEAD), row),
                pl.BlockSpec((slots, HEAD), whole),
                pl.BlockSpec((bq, HEAD), row),
                pl.BlockSpec((bq, HEAD), row),
            ],
            out_specs=[
                pl.BlockSpec((bq, width), row),
                pl.BlockSpec((slots, 2 * HEAD), whole),
            ],
            scratch_shapes=[
                pltpu.VMEM((group, HEAD, bq), F32),
                pltpu.VMEM((slots, HEAD), F32),
                pltpu.VMEM((slots, HEAD), F32),
            ],
        ),
        out_shape=[
            jax.ShapeDtypeStruct((rows, width), BF16),
            jax.ShapeDtypeStruct((slots, 2 * HEAD), BF16),
        ],
        compiler_params=pltpu.CompilerParams(vmem_limit_bytes=40 * MIB),
        cost_estimate=cost(54),
        name="attention_backward",
    )(*lists, queries, d_att, lse, delta, kv, reach_rows, hot, cosine, sine)


def join(mine, depth, places, pieces, joined, at_col=None):
    cols = pieces[0].shape[1]
    where = slice(None) if at_col is None else pl.ds(pl.multiple_of(at_col, HEAD), cols)
    for (j, row), piece in zip(places, pieces):
        at = pl.multiple_of((mine ^ j) * depth + row, 16)
        joined[pl.ds(at, piece.shape[0]), where] = piece[...]


class Rows:
    def __init__(self, pieces, depth, tf=None):
        self.depth = depth
        self.places = [(j, row) for j, row, _ in pieces]
        self.arrays = [array for _, _, array in pieces]
        if tf is None:
            self.specs = [once(array.shape) for array in self.arrays]
        else:
            self.specs = [pl.BlockSpec((array.shape[0], tf), col_block) for array in self.arrays]

    def __len__(self):
        return len(self.arrays)

    def join(self, mine, refs, joined, at_col=None):
        join(mine, self.depth, self.places, refs, joined, at_col)


def whole_block(*_):
    return (0, 0)


def row_block(i, *_):
    return (i, 0)


def col_block(i, *_):
    return (0, i)


def once(shape):
    return pl.BlockSpec(shape, whole_block, pipeline_mode=pl.Buffered(1))


def call(kernel, grid, in_specs, out_specs, out_shape, scratch, vmem, us, name):
    return pl.pallas_call(
        kernel,
        grid_spec=pltpu.PrefetchScalarGridSpec(
            num_scalar_prefetch=1,
            grid=(grid,),
            in_specs=in_specs,
            out_specs=out_specs,
            scratch_shapes=scratch,
        ),
        out_shape=out_shape,
        compiler_params=pltpu.CompilerParams(vmem_limit_bytes=vmem * MIB),
        cost_estimate=cost(us),
        name=name,
    )


def shape(dims, dtype):
    return jax.ShapeDtypeStruct(dims, dtype)


def clear_tail(tail, *joined):
    if tail:

        @pl.when(pl.program_id(0) == pl.num_programs(0) - 1)
        def _():
            for one in joined:
                one[:, tail:] = jnp.zeros_like(one[:, tail:])


def gate_up_kernel(gates, ups, place, h_ref, *refs):
    gate_refs, refs = refs[: len(gates)], refs[len(gates) :]
    up_refs, refs = refs[: len(ups)], refs[len(ups) :]
    act_ref, by_gate_ref, by_up_ref, gate_s, up_s = refs
    gates.join(place[0], gate_refs, gate_s)
    ups.join(place[0], up_refs, up_s)
    gate = dot_nn(h_ref[...], gate_s[...])
    up = dot_nn(h_ref[...], up_s[...])
    sig = jax.nn.sigmoid(gate)
    silu = gate * sig
    act_ref[...] = (silu * up).astype(BF16)
    by_up_ref[...] = silu.astype(BF16)
    by_gate_ref[...] = (up * sig * (1.0 + gate * (1.0 - sig))).astype(BF16)


def gate_up(place, hidden, gates, ups, depth, tf):
    rows, width = hidden.shape
    units = gates[0][2].shape[1]
    gates, ups = Rows(gates, depth, tf), Rows(ups, depth, tf)
    return call(
        functools.partial(gate_up_kernel, gates, ups),
        pl.cdiv(units, tf),
        [once((rows, width))] + gates.specs + ups.specs,
        [pl.BlockSpec((rows, tf), col_block)] * 3,
        [shape((rows, units), BF16)] * 3,
        [pltpu.VMEM((width, tf), BF16)] * 2,
        60,
        40,
        "gate_up",
    )(place, hidden, *gates.arrays, *ups.arrays)


def gate_up_back_kernel(gates, ups, downs, tail, place, c_ref, by_gate_ref, by_up_ref, *refs):
    gate_refs, refs = refs[: len(gates)], refs[len(gates) :]
    up_refs, refs = refs[: len(ups)], refs[len(ups) :]
    down_refs, refs = refs[: len(downs)], refs[len(downs) :]
    dg_ref, du_ref, *dh_refs, gate_s, up_s, down_s, sum_s = refs
    step = pl.program_id(0)
    gates.join(place[0], gate_refs, gate_s)
    ups.join(place[0], up_refs, up_s)
    downs.join(place[0], down_refs, down_s)
    clear_tail(tail, gate_s, up_s, down_s)
    d_act = dot_nn(c_ref[...], down_s[...])
    by_gate, by_up = by_gate_ref[...].astype(F32), by_up_ref[...].astype(F32)
    if tail:
        last = step == pl.num_programs(0) - 1
        inside = lax.broadcasted_iota(jnp.int32, by_gate.shape, 1) < jnp.where(
            last, tail, by_gate.shape[1]
        )
        by_gate = jnp.where(inside, by_gate, 0.0)
        by_up = jnp.where(inside, by_up, 0.0)
    d_gate = (d_act * by_gate).astype(BF16)
    d_up = (d_act * by_up).astype(BF16)
    dg_ref[...] = d_gate
    du_ref[...] = d_up

    @pl.when(step == 0)
    def _():
        sum_s[...] = jnp.zeros_like(sum_s)

    sum_s[...] += dot_nt(d_gate, gate_s[...]) + dot_nt(d_up, up_s[...])

    @pl.when(step == pl.num_programs(0) - 1)
    def _():
        at = 0
        for dh_ref in dh_refs:
            cols = dh_ref.shape[1]
            dh_ref[...] = sum_s[:, at : at + cols].astype(BF16)
            at += cols


def gate_up_back(place, cotangent, by_gate, by_up, gates, ups, downs, depth, tf):
    rows, width = cotangent.shape
    units = by_gate.shape[1]
    gates, ups, downs = (Rows(p, depth, tf) for p in (gates, ups, downs))
    return call(
        functools.partial(gate_up_back_kernel, gates, ups, downs, units % tf),
        pl.cdiv(units, tf),
        [once((rows, width))]
        + [pl.BlockSpec((rows, tf), col_block)] * 2
        + gates.specs
        + ups.specs
        + downs.specs,
        [pl.BlockSpec((rows, tf), col_block)] * 2 + [once((rows, cut)) for cut in cuts(width)],
        [shape((rows, units), BF16)] * 2 + [shape((rows, cut), BF16) for cut in cuts(width)],
        [pltpu.VMEM((width, tf), BF16)] * 3 + [pltpu.VMEM((rows, width), F32)],
        60,
        62,
        "gate_up_back",
    )(place, cotangent, by_gate, by_up, *gates.arrays, *ups.arrays, *downs.arrays)


def whole_grad_kernel(left_ref, right_ref, out_ref):
    out_ref[...] = dot_nn(left_ref[...], right_ref[...]).astype(BF16)


def whole_grad(left_t, right, tf):
    width, rows = left_t.shape
    units = right.shape[1]
    return pl.pallas_call(
        whole_grad_kernel,
        grid=(pl.cdiv(units, tf),),
        in_specs=[once((width, rows)), pl.BlockSpec((rows, tf), col_block)],
        out_specs=pl.BlockSpec((width, tf), col_block),
        out_shape=shape((width, units), BF16),
        compiler_params=pltpu.CompilerParams(vmem_limit_bytes=48 * MIB),
        cost_estimate=cost(19 if units > 2048 else 6),
        name="whole_grad",
    )(left_t, right)


def weight_grad_kernel(depth, parts, place, left_ref, right_ref, keep_ref, send_ref):
    for j in range(parts):
        half = keep_ref if j % 2 == 0 else send_ref
        rows = pl.ds(pl.multiple_of((place[0] ^ j) * depth, 16), depth)
        at = (j // 2) * depth
        half[at : at + depth, :] = dot_nn(left_ref[rows, :], right_ref[...]).astype(BF16)


def weight_grad(place, left_t, right, parts, tf):
    width, rows = left_t.shape
    units = right.shape[1]
    return call(
        functools.partial(weight_grad_kernel, width // parts, parts),
        pl.cdiv(units, tf),
        [once((width, rows)), pl.BlockSpec((rows, tf), col_block)],
        [pl.BlockSpec((width // 2, tf), col_block)] * 2,
        [shape((width // 2, units), BF16)] * 2,
        [],
        48,
        19 if units > 2048 else 7,
        "weight_grad",
    )(place, left_t, right)


def add_kernel(counts, *refs):
    out_ref, at, col = refs[-1], 0, 0
    for count in counts:
        parts = refs[at : at + count]
        cols = parts[0].shape[1]
        total = sum(ref[...].astype(F32) for ref in parts)
        out_ref[:, col : col + cols] = total.astype(BF16)
        at, col = at + count, col + cols


def add_rows(rows, *groups):
    parts = [part for group in groups for part in group]
    cols = sum(group[0][0].shape[1] for group in groups)
    step = math.gcd(rows, 64, *[row for _, row in parts])
    return pl.pallas_call(
        functools.partial(add_kernel, [len(group) for group in groups]),
        grid=(rows // step,),
        in_specs=[
            pl.BlockSpec((step, array.shape[1]), lambda i, at=row // step: (at + i, 0))
            for array, row in parts
        ],
        out_specs=pl.BlockSpec((step, cols), lambda i: (i, 0)),
        out_shape=shape((rows, cols), BF16),
        compiler_params=pltpu.CompilerParams(vmem_limit_bytes=32 * MIB),
        cost_estimate=cost(4),
        name="add_rows",
    )(*[array for array, _ in parts])


def mark_kernel(place_ref, out_ref):
    for at in range(2):
        out_ref[at] = place_ref[at]


def mark(place):
    place.v = pl.pallas_call(
        mark_kernel,
        in_specs=[pl.BlockSpec(memory_space=pltpu.SMEM)],
        out_specs=pl.BlockSpec(memory_space=pltpu.SMEM),
        out_shape=shape((2,), jnp.int32),
        cost_estimate=cost(1),
        name="mark",
    )(place.v)
    return place


def down_project_kernel(downs, place, act_ref, *refs):
    down_refs, (out_ref, down_s, sum_s) = refs[: len(downs)], refs[len(downs) :]
    step = pl.program_id(0)
    downs.join(place[0], down_refs, down_s)

    @pl.when(step == 0)
    def _():
        sum_s[...] = jnp.zeros_like(sum_s)

    sum_s[...] += dot_nt(act_ref[...], down_s[...])

    @pl.when(step == pl.num_programs(0) - 1)
    def _():
        out_ref[...] = sum_s[...].astype(BF16)


def down_project(place, act, downs, width, depth, tf):
    rows, units = act.shape
    downs = Rows(downs, depth, tf)
    return call(
        functools.partial(down_project_kernel, downs),
        units // tf,
        [pl.BlockSpec((rows, tf), col_block)] + downs.specs,
        once((rows, width)),
        shape((rows, width), BF16),
        [pltpu.VMEM((width, tf), BF16), pltpu.VMEM((rows, width), F32)],
        48,
        24,
        "down_project",
    )(place, act, *downs.arrays)


def inverse_rms(values):
    return lax.rsqrt(jnp.mean(values * values, axis=-1, keepdims=True) + EPSILON)


def turned(values, cosine, sine):
    return values * cosine + pltpu.roll(values, HEAD // 2, 1) * sine


def mix_kernel(weight, group, place, x_ref, gain_ref, bias_ref, cos_ref, sin_ref, *refs):
    pieces, (q_ref, kv_ref, ht_ref, weight_s) = refs[: len(weight)], refs[len(weight) :]

    @pl.when(pl.program_id(0) == 0)
    def _():
        weight.join(place[0], pieces, weight_s)

    x = x_ref[...].astype(F32)
    hidden = (x * inverse_rms(x) * gain_ref[...].astype(F32)).astype(BF16)
    ht_ref[...] = hidden.T
    mixed = dot_nn(hidden, weight_s[...]) + bias_ref[...].astype(F32)
    cosine, sine = cos_ref[...], sin_ref[...]
    for h in range(group):
        at = slice(h * HEAD, (h + 1) * HEAD)
        q_ref[:, at] = turned(mixed[:, at], cosine, sine).astype(BF16)
    split = group * HEAD
    kv_ref[:, :HEAD] = turned(mixed[:, split : split + HEAD], cosine, sine).astype(BF16)
    kv_ref[:, HEAD:] = mixed[:, split + HEAD :].astype(BF16)


def mix(place, tokens, gain, bias, cosine, sine, pieces, depth, group, bq):
    rows, width = tokens.shape
    cols = pieces[0][2].shape[1]
    weight = Rows(pieces, depth)
    return call(
        functools.partial(mix_kernel, weight, group),
        rows // bq,
        [
            pl.BlockSpec((bq, width), row_block),
            once((1, width)),
            once((1, cols)),
            pl.BlockSpec((bq, HEAD), row_block),
            pl.BlockSpec((bq, HEAD), row_block),
        ]
        + weight.specs,
        [
            pl.BlockSpec((bq, group * HEAD), row_block),
            pl.BlockSpec((bq, 2 * HEAD), row_block),
            pl.BlockSpec((width, bq), col_block),
        ],
        [
            shape((rows, group * HEAD), BF16),
            shape((rows, 2 * HEAD), BF16),
            shape((width, rows), BF16),
        ],
        [pltpu.VMEM((width, cols), BF16)],
        32,
        8,
        "mix",
    )(place, tokens, gain[None], bias[None], cosine, sine, *weight.arrays)


def branch_kernel(weight, parts, place, x_ref, own_ref, upper_ref, lower_ref, gain_ref, *refs):
    own_w, other_w = refs[: len(weight)], refs[len(weight) : len(weight) + parts]
    mid_ref, h_ref, ht_ref, weight_s, att_s = refs[len(weight) + parts :]
    split = own_ref.shape[1]
    own_at = pl.multiple_of(place[1] * split, HEAD)
    other_at = pl.multiple_of((1 - place[1]) * split, HEAD)

    @pl.when(pl.program_id(0) == 0)
    def _():
        weight.join(place[0], own_w, weight_s, own_at)
        join(place[0], weight.depth, [(j, 0) for j in range(parts)], other_w, weight_s, other_at)

    att_s[:, pl.ds(own_at, split)] = own_ref[...]
    steps = pl.num_programs(0)

    @pl.when(pl.program_id(0) < steps // 2)
    def _():
        att_s[:, pl.ds(other_at, split)] = upper_ref[...]

    @pl.when(pl.program_id(0) >= steps // 2)
    def _():
        att_s[:, pl.ds(other_at, split)] = lower_ref[...]

    mid = x_ref[...].astype(F32) + dot_nt(att_s[...], weight_s[...])
    mid_ref[...] = mid
    hidden = (mid * inverse_rms(mid) * gain_ref[...].astype(F32)).astype(BF16)
    h_ref[...] = hidden
    ht_ref[...] = hidden.T


def branch(place, tokens, own, upper, lower, gain, pieces, other_pieces, depth, bq):
    rows, width = tokens.shape
    cols = own.shape[1]
    parts = width // depth
    weight = Rows(pieces, depth)
    wide = pl.BlockSpec((bq, width), row_block)
    narrow = pl.BlockSpec((bq, cols), row_block)
    other_specs = [once((depth, cols))] * parts
    half = rows // bq // 2
    return call(
        functools.partial(branch_kernel, weight, parts),
        rows // bq,
        [
            wide,
            narrow,
            pl.BlockSpec((bq, cols), lambda i, *_: (jnp.minimum(i, half - 1), 0)),
            pl.BlockSpec((bq, cols), lambda i, *_: (jnp.maximum(i - half, 0), 0)),
            once((1, width)),
        ]
        + weight.specs
        + other_specs,
        [wide, wide, pl.BlockSpec((width, bq), col_block)],
        [shape((rows, width), F32), shape((rows, width), BF16), shape((width, rows), BF16)],
        [pltpu.VMEM((width, 2 * cols), BF16), pltpu.VMEM((bq, 2 * cols), BF16)],
        40,
        12,
        "branch",
    )(place, tokens, own, upper, lower, gain[None], *weight.arrays, *other_pieces)


def middle_back_kernel(
    weight, group, place, mid_ref, c_ref, gain_ref, att_ref, *refs
):
    own_refs, other_refs, refs = refs[:CUTS], refs[CUTS : 2 * CUTS], refs[2 * CUTS :]
    pieces, refs = refs[: len(weight)], refs[len(weight) :]
    dm_ref, dbt_ref, da_ref, delta_ref, dgain_ref, weight_s = refs

    @pl.when(pl.program_id(0) == 0)
    def _():
        weight.join(place[0], pieces, weight_s)
        dgain_ref[...] = jnp.zeros_like(dgain_ref)

    mid = mid_ref[...]
    inverse = inverse_rms(mid)
    normed = mid * inverse
    own = jnp.concatenate([ref[...] for ref in own_refs], axis=1).astype(F32)
    other = jnp.concatenate([ref[...] for ref in other_refs], axis=1).astype(F32)
    dgain_ref[...] += jnp.sum(own * normed, axis=0, keepdims=True)
    scaled = (own + other) * gain_ref[...].astype(F32)
    d_mid = c_ref[...].astype(F32) + inverse * (
        scaled - normed * jnp.mean(scaled * normed, axis=-1, keepdims=True)
    )
    dm_ref[...] = d_mid
    d_branch = d_mid.astype(BF16)
    dbt_ref[...] = d_branch.T
    d_att = dot_nn(d_branch, weight_s[...]).astype(BF16)
    da_ref[...] = d_att
    product = d_att.astype(F32) * att_ref[...].astype(F32)
    for h in range(group):
        delta_ref[h : h + 1, :] = jnp.sum(
            product[:, h * HEAD : (h + 1) * HEAD].T, axis=0, keepdims=True
        )


def middle_back(place, own, other, mid, cotangent, gain, attended, pieces, depth, bq):
    rows, width = mid.shape
    cols = attended.shape[1]
    weight = Rows(pieces, depth)
    group = cols // HEAD
    wide = pl.BlockSpec((bq, width), row_block)
    narrow = pl.BlockSpec((bq, cols), row_block)
    return call(
        functools.partial(middle_back_kernel, weight, group),
        rows // bq,
        [wide, wide, once((1, width)), narrow]
        + [pl.BlockSpec((bq, cut), row_block) for cut in cuts(width)] * 2
        + weight.specs,
        [
            wide,
            pl.BlockSpec((width, bq), col_block),
            narrow,
            pl.BlockSpec((group, bq), col_block),
            pl.BlockSpec((1, width), whole_block),
        ],
        [
            shape((rows, width), F32),
            shape((width, rows), BF16),
            shape((rows, cols), BF16),
            shape((group, rows), F32),
            shape((1, width), F32),
        ],
        [pltpu.VMEM((width, cols), BF16)],
        48,
        13,
        "middle_back",
    )(place, mid, cotangent, gain[None], attended, *own, *other, *weight.arrays)


def mix_back_kernel(
    weight, group, place, dq_ref, dkv_ref, cos_ref, sin_ref, x_ref, *refs
):
    pieces, refs = refs[: len(weight)], refs[len(weight) :]
    dm_ref, dbias_ref, dgain_ref, *dh_refs, weight_s = refs

    @pl.when(pl.program_id(0) == 0)
    def _():
        weight.join(place[0], pieces, weight_s)
        dgain_ref[...] = jnp.zeros_like(dgain_ref)
        dbias_ref[...] = jnp.zeros_like(dbias_ref)

    split = group * HEAD
    dm_ref[:, :split] = dq_ref[...]
    d_keys = dkv_ref[:, :HEAD].astype(F32)
    dm_ref[:, split : split + HEAD] = turned(d_keys, cos_ref[...], -sin_ref[...]).astype(BF16)
    dm_ref[:, split + HEAD :] = dkv_ref[:, HEAD:]
    d_mixed = dm_ref[...]
    dbias_ref[...] += jnp.sum(d_mixed.astype(F32), axis=0, keepdims=True)
    d_hidden = dot_nt(d_mixed, weight_s[...])
    x = x_ref[...].astype(F32)
    dgain_ref[...] += jnp.sum(d_hidden * (x * inverse_rms(x)), axis=0, keepdims=True)
    at = 0
    for dh_ref in dh_refs:
        cols = dh_ref.shape[1]
        dh_ref[...] = d_hidden[:, at : at + cols].astype(BF16)
        at += cols


def mix_back(place, dq, dkv, cosine, sine, tokens, pieces, depth, bq):
    rows, width = tokens.shape
    cols = pieces[0][2].shape[1]
    weight = Rows(pieces, depth)
    group = dq.shape[1] // HEAD
    wide = pl.BlockSpec((bq, width), row_block)
    return call(
        functools.partial(mix_back_kernel, weight, group),
        rows // bq,
        [
            pl.BlockSpec((bq, group * HEAD), row_block),
            pl.BlockSpec((bq, 2 * HEAD), row_block),
            pl.BlockSpec((bq, HEAD), row_block),
            pl.BlockSpec((bq, HEAD), row_block),
            wide,
        ]
        + weight.specs,
        [
            pl.BlockSpec((bq, cols), row_block),
            pl.BlockSpec((1, cols), whole_block),
            pl.BlockSpec((1, width), whole_block),
        ]
        + [pl.BlockSpec((bq, cut), row_block) for cut in cuts(width)],
        [
            shape((rows, cols), BF16),
            shape((1, cols), F32),
            shape((1, width), F32),
        ]
        + [shape((rows, cut), BF16) for cut in cuts(width)],
        [pltpu.VMEM((width, cols), BF16)],
        32,
        8,
        "mix_back",
    )(place, dq, dkv, cosine, sine, tokens, *weight.arrays)


def input_back_kernel(place, x_ref, gain_ref, dm_ref, *refs):
    own_refs, other_refs, (out_ref,) = refs[:CUTS], refs[CUTS : 2 * CUTS], refs[2 * CUTS :]
    own = jnp.concatenate([ref[...] for ref in own_refs], axis=1).astype(F32)
    other = jnp.concatenate([ref[...] for ref in other_refs], axis=1).astype(F32)
    x = x_ref[...].astype(F32)
    inverse = inverse_rms(x)
    normed = x * inverse
    scaled = (own + other) * gain_ref[...].astype(F32)
    out_ref[...] = dm_ref[...] + inverse * (
        scaled - normed * jnp.mean(scaled * normed, axis=-1, keepdims=True)
    )


def input_back(place, own, other, tokens, gain, d_mid, bq):
    rows, width = tokens.shape
    wide = pl.BlockSpec((bq, width), row_block)
    return call(
        input_back_kernel,
        rows // bq,
        [wide, once((1, width)), wide]
        + [pl.BlockSpec((bq, cut), row_block) for cut in cuts(width)] * 2,
        wide,
        shape((rows, width), F32),
        [],
        32,
        8,
        "input_back",
    )(place, tokens, gain[None], d_mid, *own, *other)


class Box:
    def __init__(self, v):
        self.v = v


def boxes(values):
    return [Box(v) for v in values]


def fence(*items):
    flat = []
    for item in items:
        flat += item if isinstance(item, (list, tuple)) else [item]
    for item, v in zip(flat, lax.optimization_barrier([item.v for item in flat])):
        item.v = v


def held(value, *items):
    one = Box(value)
    fence(one, *items)
    return one.v


def swap(value, axis, size, bit):
    return lax.ppermute(value, axis, [(i, i ^ bit) for i in range(size)])


class Pieces:
    def __init__(self, own, size, slabs=1):
        if size != 4 or own.shape[0] % (16 * slabs):
            slabs = 1
        self.size, self.own, self.slabs = size, own, slabs
        self.depth = own.shape[0] // slabs
        self.got = {}

    def away(self, own):
        got, bit = {0: own}, self.size // 2
        while bit > 1:
            got.update({j ^ bit: swap(p, "shard", self.size, bit) for j, p in got.items()})
            bit //= 2
        return {j: Box(p) for j, p in got.items() if j}

    def far(self, slab, *first):
        if slab >= self.slabs:
            return []
        own = held(self.own, *first)[slab * self.depth : (slab + 1) * self.depth]
        got = self.away(own)
        self.got.update({(j, slab): p for j, p in got.items()})
        return list(got.values())

    def far_by_ctx(self, contexts, *first):
        rows = self.own.shape[0] // contexts
        own = lax.dynamic_slice_in_dim(
            held(self.own, *first), lax.axis_index("ctx") * rows, rows, 0
        )
        self.parts = self.away(own)
        return list(self.parts.values())

    def spread(self):
        for j, part in self.parts.items():
            self.got[j, 0] = Box(lax.all_gather(part.v, "ctx", axis=0, tiled=True))
        return [self.got[j, 0] for j in self.parts]

    def near_own(self, *first):
        self.near = Box(swap(held(self.own, *first), "shard", self.size, 1))
        return [self.near]

    def near_rest(self, slab, *first):
        if slab >= self.slabs:
            return []
        far = [j for j in range(2, self.size, 2)]
        if first:
            fence(*[self.got[j, slab] for j in far], *first)
        for j in far:
            self.got[j ^ 1, slab] = Box(swap(self.got[j, slab].v, "shard", self.size, 1))
        return [self.got[j ^ 1, slab] for j in far]

    def all(self):
        found = [(0, 0, self.own), (1, 0, self.near.v)]
        found += [
            (j, k * self.depth, p.v) for (j, k), p in sorted(self.got.items(), key=lambda i: i[0])
        ]
        return found


class Reduction:
    def __init__(self, shards, contexts, slabs):
        self.shards, self.chain = shards, contexts == 4
        self.slabs = slabs if shards == 4 else 1
        self.keep, self.send, self.got = [], [], []
        self.own, self.one, self.two, self.three = {}, {}, {}, {}
        self.by_sum = {}

    def make(self, place, left_t, right, tf):
        keep, send = boxes(weight_grad(place.v, left_t, right, self.shards, tf))
        self.keep.append(keep)
        self.send.append(send)
        return send

    def cores(self):
        self.got.append(Box(swap(self.send[len(self.got)].v, "shard", self.shards, 1)))
        return self.got[-1]

    def pairs(self, row):
        return [[(keep.v, row), (got.v, row)] for keep, got in zip(self.keep, self.got)]

    def sum_away(self):
        rows = self.keep[0].v.shape[0]
        if self.shards == 4:
            size = rows // 2 // self.slabs
            self.away = [
                Box(add_rows(size, *self.pairs(rows // 2 + slab * size)))
                for slab in range(self.slabs)
            ]
        else:
            self.away = [Box(add_rows(rows, *self.pairs(0)))]
        return self.away

    def chips(self):
        if self.shards == 4:
            self.last = [Box(swap(part.v, "shard", 4, 2)) for part in self.away]
            return self.last
        held, bit, count = self.away[0].v, 2, self.shards // 2
        while bit < self.shards:
            size = held.shape[0] // count
            blocks = [held[at * size : (at + 1) * size] for at in range(count)]
            away = swap(jnp.concatenate(blocks[1::2], axis=0), "shard", self.shards, bit)
            here = jnp.concatenate(blocks[::2], axis=0)
            held = here if 2 * bit >= self.shards else here + away
            bit, count = 2 * bit, count // 2
        self.here, self.last = held, boxes([away])
        return self.last

    def arrived(self, slab):
        if slab >= self.slabs:
            return []
        last = self.last[slab].v
        if self.shards != 4:
            self.own[slab] = Box(self.here + last)
        elif len(self.keep) == 1:
            size = last.shape[0]
            self.own[slab] = Box(add_rows(size, self.pairs(slab * size)[0] + [(last, 0)]))
        else:
            size = last.shape[0]
            here = add_rows(size, *self.pairs(slab * size))
            self.own[slab] = Box(add_rows(size, [(here, 0), (last, 0)]))
        return [self.own[slab]]

    def whole_sum(self, slab):
        if slab >= self.slabs:
            return []
        self.by_sum[slab] = Box(lax.psum(self.own[slab].v, "ctx"))
        return [self.by_sum[slab]]

    def inward(self, slab):
        if slab >= self.slabs:
            return []
        if not self.chain:
            return self.whole_sum(slab)
        self.one[slab] = Box(lax.ppermute(self.own[slab].v, "ctx", [(0, 1), (3, 2)]))
        return [self.one[slab]]

    def middle(self, slab):
        if not self.chain or slab >= self.slabs:
            return []
        self.own[slab] = Box(self.own[slab].v + self.one[slab].v)
        self.two[slab] = Box(lax.ppermute(self.own[slab].v, "ctx", [(1, 2), (2, 1)]))
        return [self.two[slab]]

    def outward(self, slab):
        if not self.chain or slab >= self.slabs:
            return []
        self.own[slab] = Box(self.own[slab].v + self.two[slab].v)
        self.three[slab] = Box(lax.ppermute(self.own[slab].v, "ctx", [(1, 0), (2, 3)]))
        return [self.three[slab]]

    def result(self):
        place = lax.axis_index("ctx")
        inside = (place == 1) | (place == 2)
        totals = [
            self.by_sum[slab].v
            if slab in self.by_sum
            else jnp.where(inside, self.own[slab].v, self.three[slab].v)
            for slab in range(self.slabs)
        ]
        whole = totals[0] if len(totals) == 1 else jnp.concatenate(totals, axis=0)
        return whole.astype(F32)


def tree_tables(seg_row, parent_row):
    seg_count = parent_row.shape[0]
    seg_ids = jnp.arange(seg_count, dtype=jnp.int32)
    one_hot = (seg_row[:, None] == seg_ids[None, :]).astype(jnp.int32)
    lengths = jnp.sum(one_hot, axis=0, dtype=jnp.int32)
    before = seg_ids[None, :] < seg_ids[:, None]
    starts = jnp.sum(jnp.where(before, lengths[None, :], 0), axis=1, dtype=jnp.int32)
    link = (parent_row[:, None] == seg_ids[None, :]) & (parent_row[:, None] != seg_ids[:, None])
    twice = jnp.any(link[:, :, None] & link[None, :, :], axis=1)
    strict = link | twice
    padding = parent_row == seg_ids
    reach = strict | ((seg_ids[:, None] == seg_ids[None, :]) & ~padding[:, None])
    offsets = jnp.sum(jnp.where(strict, lengths[None, :], 0), axis=1, dtype=jnp.int32) - starts
    return reach, offsets


def block_lists(row_hot, col_hot, reach, col_places, row_first, bq, bk):
    segs = reach.shape[0]
    row_has = jnp.any(row_hot.reshape(-1, bq, segs), axis=1)
    col_has = jnp.any(col_hot.reshape(-1, bk, segs), axis=1)
    row_blocks, col_blocks = row_has.shape[0], col_has.shape[0]
    row_reach = jnp.any(row_has[:, :, None] & reach[None], axis=1)
    meets = jnp.any(row_reach[:, None, :] & col_has[None], axis=2)
    col_at = col_places.reshape(-1, bk)[:, 0]
    row_at = row_first + bq * jnp.arange(row_blocks, dtype=jnp.int32)
    causal = col_at[None, :] < row_at[:, None] + bq
    diagonal = causal & (col_at[None, :] + bk > row_at[:, None])
    active = ((meets & causal) | diagonal) & (col_at >= 0)[None, :]
    ids = jnp.arange(col_blocks, dtype=jnp.int32)
    rank = jnp.sum(
        (active[:, None, :] & (ids[None, :] < ids[:, None])[None]).astype(jnp.int32), axis=2
    )
    placed = active[:, :, None] & (rank[:, :, None] == ids[None, None, :])
    chosen = jnp.sum(jnp.where(placed, ids[None, :, None], 0), axis=1, dtype=jnp.int32)
    count = jnp.sum(active.astype(jnp.int32), axis=1, dtype=jnp.int32)
    places = jnp.concatenate([col_at, row_first[None]])
    return count, chosen.reshape(-1), places


def layer(
    sizes, tokens, cotangent, segment, parent, gain_attn, qkv_weight, qkv_bias,
    out_weight, gain_ffn, gate_weight, up_weight, down_weight,
):
    shards, contexts, halves = sizes["shard"], sizes["ctx"], sizes["tp"]
    rows, width = tokens.shape
    group = out_weight.shape[1] // HEAD
    shard, ctx, half = lax.axis_index("shard"), lax.axis_index("ctx"), lax.axis_index("tp")
    place = jnp.stack([shard, half]).astype(jnp.int32)
    across = [(i, i ^ 1) for i in range(halves)]

    row_first = (ctx * rows).astype(jnp.int32)
    reach, offsets = tree_tables(segment[0], parent[0])
    seg_ids = jnp.arange(reach.shape[0], dtype=jnp.int32)
    behind = [jnp.maximum(ctx - k, 0) * rows for k in range(contexts)]
    seg_back = jnp.concatenate(
        [lax.dynamic_slice_in_dim(segment[0], at, rows, 0) for at in behind]
    )
    places_back = jnp.concatenate(
        [(ctx - k) * rows + jnp.arange(rows, dtype=jnp.int32) for k in range(contexts)]
    )
    col_hot = seg_back[:, None] == seg_ids[None, :]
    row_hot = col_hot[:rows]
    own_pos = places_back[:rows] + jnp.sum(
        jnp.where(row_hot, offsets[None, :], 0), axis=1, dtype=jnp.int32
    )
    pad = ((0, 0), (0, HEAD - reach.shape[0]))
    row_reach = jnp.any(row_hot[:, :, None] & reach[None], axis=1)
    reach_rows = jnp.pad(row_reach.astype(BF16), pad)
    hot = jnp.pad(col_hot.astype(BF16), pad)
    bq = math.gcd(rows, 256)
    bk_f, bk_b = math.gcd(rows, 128), math.gcd(rows, 512)
    lists_f = block_lists(row_hot, col_hot, reach, places_back, row_first, bq, bk_f)
    lists_b = block_lists(row_hot, col_hot, reach, places_back, row_first, bq, bk_b)
    lane = jnp.arange(HEAD, dtype=jnp.int32)
    frequency = THETA ** (-2.0 * (lane % (HEAD // 2)).astype(F32) / HEAD)
    angles = own_pos.astype(F32)[:, None] * frequency[None, :]
    cosine = jnp.cos(angles)
    sine = jnp.sin(angles) * jnp.where(lane < HEAD // 2, -1.0, 1.0)

    depth = width // shards
    qkv, out_w, gate, up, down = (
        Pieces(qkv_weight, shards),
        Pieces(out_weight, shards),
        Pieces(gate_weight, shards, 3),
        Pieces(up_weight, shards),
        Pieces(down_weight, shards, 4),
    )

    def over_tp(box):
        return Box(lax.ppermute(box.v, "tp", across))

    qkv_far = qkv.far(0)
    leaves, tree = jax.tree.flatten((reach_rows, hot, lists_f, lists_b, cosine, sine))
    leaves, place = boxes(leaves), Box(place)
    fence(leaves, place, qkv_far)
    reach_rows, hot, lists_f, lists_b, cosine, sine = tree.unflatten([leaf.v for leaf in leaves])
    qkv_near = qkv.near_own(qkv_far) + qkv.near_rest(0)
    out_far = out_w.far(0, qkv_far)
    out_near = out_w.near_own(qkv_far)
    out_other = {0: Box(lax.ppermute(held(out_weight, qkv_far), "tp", across))}
    fence(mark(place), qkv_near)
    up_parts = up.far_by_ctx(contexts, qkv_near)

    queries, kv_own, hidden_one_t = mix(
        place.v, tokens, gain_attn, qkv_bias, cosine, sine, qkv.all(), depth, group, bq
    )
    kv_own = Box(kv_own)
    fence(kv_own, out_near, place)
    kv = [kv_own]
    rightward = [(i, i + 1) for i in range(contexts - 1)]
    for k in range(1, contexts):
        kv.append(Box(lax.ppermute(kv[-1].v, "ctx", rightward)))
        if k == 1:
            out_other[1] = over_tp(out_w.near)
            out_rest = out_w.near_rest(0, kv_own)
            fence(mark(place), kv, out_rest, out_far, out_other[0])
        elif k == 2:
            gate_far = gate.far(0, kv[1])
            out_other.update({j: over_tp(piece) for (j, _), piece in out_w.got.items()})
            top_grad_t = Box(held(cotangent, *kv).T)
            fence(mark(place), kv, out_other[1], up_parts)
        elif k == contexts - 1:
            fence(mark(place), kv, gate_far, top_grad_t)
            fence(kv, up_parts)
        else:
            fence(mark(place), kv)
    kv_back = jnp.concatenate([p.v for p in kv], axis=0)
    up_spread = up.spread()
    gate_far = gate.far(1, kv)
    out_other = [out_other[j] for j in range(shards)]
    upper_rows = rows // 2
    upper, *upper_sums = attention_forward(
        lists_f, queries, kv_back, reach_rows, hot, bq, bk_f, 0, upper_rows
    )
    upper, leaves = Box(upper), boxes(lists_f)
    fence(upper, leaves, out_other)
    upper_other = over_tp(upper)
    gate_far_2 = gate.far(2, upper)
    lower, *lower_sums = attention_forward(
        [leaf.v for leaf in leaves], queries, kv_back, reach_rows, hot, bq, bk_f, upper_rows,
        upper_rows,
    )
    lower = Box(lower)
    fence(lower, gate_far, place, upper_other)
    lower_other = over_tp(lower)
    gate_rest = gate.near_rest(0) + gate.near_rest(1, lower)
    attended = Box(jnp.concatenate([upper.v, lower.v], axis=0))
    lse, tops = (jnp.concatenate(both, axis=1) for both in zip(upper_sums, lower_sums))
    attended_other = lower_other
    fence(mark(place), lower_other, gate_far_2, gate_rest, up_spread, attended)
    down_far = down.far(0, attended_other)
    gate_rest = gate.near_rest(2) + up.near_rest(0)
    own_near = gate.near_own(attended_other) + up.near_own(attended_other)
    mid, hidden_two, hidden_two_t = branch(
        place.v, tokens, attended.v, upper_other.v, lower_other.v, gain_ffn, out_w.all(),
        [p.v for p in out_other], depth, bq,
    )
    mid = Box(mid)
    fence(mid, gate_rest, own_near, place, down_far)
    down_far = down.far(1, mid) + down.far(2, mid)
    down_near = down.near_own(mid)
    act, by_gate, by_up = gate_up(place.v, hidden_two, gate.all(), up.all(), depth, 512)
    act = Box(act)
    fence(act, down_far, down_near, top_grad_t, place)
    down_far = down.far(3, act)
    down_rest = down.near_rest(0, act) + down.near_rest(1) + down.near_rest(2)
    down_part = Box(whole_grad(top_grad_t.v, act.v, 512))
    fence(down_part, down_rest, down_far, place)
    down_part = Box(lax.psum_scatter(down_part.v, ("shard", "ctx"), scatter_dimension=0, tiled=True))
    down_rest = down.near_rest(3)
    fence(mark(place), down_rest)
    d_gate, d_up, *d_hidden_two = gate_up_back(
        place.v, cotangent, by_gate, by_up, gate.all(), up.all(), down.all(), depth, 512
    )

    d_hidden_two = boxes(d_hidden_two)
    gate_grad = Reduction(shards, contexts, 2)
    up_grad = Reduction(shards, contexts, 2)
    last_grad = Reduction(shards, contexts, 1)
    fence(place, d_hidden_two)
    other = [over_tp(d_hidden_two[0])]
    fence(place, gate_grad.make(place, hidden_two_t, d_gate, 512), other[0], d_hidden_two[1])
    gate_got = gate_grad.cores()
    other.append(over_tp(d_hidden_two[1]))
    fence(
        place, up_grad.make(place, hidden_two_t, d_up, 512), gate_got, other[1], d_hidden_two[2], act
    )
    up_got = up_grad.cores()
    other.append(over_tp(d_hidden_two[2]))
    fence(place, gate_grad.sum_away())
    gate_last = gate_grad.chips()
    ffn_own = Box(down_project(place.v, act.v, down.all(), width, depth, 896))
    fence(place, ffn_own, up_got, other[2], down_part)
    down_total = Box(lax.all_gather(down_part.v, "ctx", axis=0, tiled=True))
    ffn_other = over_tp(ffn_own)
    fence(place, up_grad.sum_away())
    up_last = up_grad.chips()

    d_mid, d_branch_t, d_att, delta, gain_two_part = middle_back(
        place.v, [p.v for p in d_hidden_two], [p.v for p in other], mid.v, cotangent, gain_ffn,
        attended.v, out_w.all(), depth, bq,
    )
    d_mid = Box(d_mid)
    fence(place, d_mid)
    out_sent = last_grad.make(place, d_branch_t, attended.v, 768)
    leaves = boxes(lists_b)
    fence(place, out_sent, gate_last[:1])
    out_got = last_grad.cores()
    fence(leaves, gate_grad.arrived(0))
    gate_one = gate_grad.inward(0)
    d_query, d_kv = attention_backward(
        [leaf.v for leaf in leaves], queries, d_att, lse, delta, kv_back, reach_rows, hot,
        cosine, sine, bq, bk_b,
    )
    d_kv = Box(d_kv)
    fence(d_kv, gate_one, gate_last[1:], out_got, ffn_other, mid, place)
    output = (mid.v + (ffn_own.v.astype(F32) + ffn_other.v.astype(F32))).astype(BF16)
    output = Box(output)
    leftward = [(i + 1, i) for i in range(contexts - 1)]
    d_kv_own = Box(d_kv.v[(contexts - 1) * rows :])
    for k in range(contexts - 2, -1, -1):
        got = Box(lax.ppermute(d_kv_own.v, "ctx", leftward))
        if k == contexts - 2:
            gate_two = gate_grad.middle(0)
            gate_own = gate_grad.arrived(1)
            gate_one = gate_grad.inward(1)
            fence(mark(place), got, output, gate_two, gate_one)
        elif k == 0:
            fence(mark(place), got, down_total, up_grad.arrived(0), up_last[1:])
        else:
            fence(mark(place), got, up_last[:1])
        d_kv_own = Box(d_kv.v[k * rows : (k + 1) * rows] + got.v)
    fence(place, d_kv_own, list(gate_grad.own.values()), gate_one, gate_two, list(up_grad.own.values()))
    gate_three = gate_grad.outward(0)
    gate_two = gate_grad.middle(1)
    up_one = up_grad.inward(0)
    d_mixed, bias_part, gain_one_part, *d_hidden_one = mix_back(
        place.v, d_query, d_kv_own.v, cosine, sine, tokens, qkv.all(), depth, bq
    )
    peak_own = jnp.max(tops, axis=1)
    device = shard * contexts + ctx
    spread = jnp.where(
        (jnp.arange(shards * contexts)[:, None, None] == device)
        & (jnp.arange(halves)[None, :, None] == half),
        peak_own[None, None, :],
        0.0,
    )
    bias_both = jnp.where(jnp.arange(halves)[:, None] == half, bias_part, 0.0)
    vector = Box(
        jnp.concatenate(
            [gain_one_part[0], gain_two_part[0], bias_both.reshape(-1), spread.reshape(-1)]
        )
    )
    d_hidden_one = boxes(d_hidden_one)
    fence(place, vector, d_hidden_one)

    def hop(axis, bit):
        vector.v = vector.v + swap(vector.v, axis, sizes[axis], bit)
        return vector

    back = [over_tp(d_hidden_one[0])]
    q_sent = last_grad.make(place, hidden_one_t, d_mixed, 512)
    fence(place, q_sent, back[0], d_hidden_one[1], up_grad.arrived(1))
    qkv_got = last_grad.cores()
    back.append(over_tp(d_hidden_one[1]))
    hop("shard", 1)
    fence(mark(place), qkv_got, gate_two, up_one, vector, gate_three)
    up_two = up_grad.middle(0)
    up_one = up_grad.inward(1)
    gate_three = gate_grad.outward(1)
    bit = 2
    while bit < shards:
        hop("shard", bit)
        bit *= 2
    fence(place, last_grad.sum_away(), vector)
    last_last = last_grad.chips()
    hop("tp", 1)
    fence(mark(place), up_two, up_one, vector, last_last, back[1], d_hidden_one[2], gate_three)
    back.append(over_tp(d_hidden_one[2]))
    vectors = Reduction(shards, contexts, 1)
    vectors.own[0] = vector
    up_three = up_grad.outward(0)
    up_two = up_grad.middle(1)
    last_grad.arrived(0)
    last_one = last_grad.inward(0) + vectors.inward(0)
    fence(mark(place), up_two, last_one, back[2], d_mid, up_three)
    up_three = up_grad.outward(1)
    last_two = last_grad.middle(0) + vectors.middle(0)
    input_grad = Box(
        input_back(
            place.v, [p.v for p in d_hidden_one], [p.v for p in back], tokens, gain_attn, d_mid.v, bq
        )
    )
    fence(input_grad, last_two, place, up_three)
    last_three = last_grad.outward(0) + vectors.outward(0)
    vector = Box(vectors.result())
    gate_total, up_total, last_total = (one.result() for one in (gate_grad, up_grad, last_grad))
    out_total = last_total[:, : out_weight.shape[1]]
    qkv_total = last_total[:, out_weight.shape[1] :]
    down_total, input_grad, output, vector = (
        down_total.v.astype(F32), input_grad.v, output.v, vector.v
    )
    bias_at = 2 * width
    spread_at = bias_at + bias_both.size
    bias_grad = lax.dynamic_slice_in_dim(
        vector[bias_at:spread_at], half * bias_part.size, bias_part.size, 0
    )
    peaks = jnp.max(vector[spread_at:].reshape(shards * contexts, halves, group), axis=0)
    peak_all = lax.dynamic_index_in_dim(peaks, half, 0, keepdims=False)
    clip_out = CLIP_BOUND / jnp.maximum(peak_all, CLIP_BOUND)
    return (
        output,
        input_grad,
        vector[:width],
        qkv_total,
        bias_grad,
        out_total,
        vector[width:bias_at],
        gate_total,
        up_total,
        down_total,
        clip_out,
    )


def solution(mesh):
    token = P(("shard", "ctx"), None)
    weight = P("shard", "tp")
    return jax.shard_map(
        functools.partial(layer, dict(mesh.shape)),
        mesh=mesh,
        in_specs=(
            token,
            token,
            P("shard", None),
            P("shard", None),
            P(),
            weight,
            P("tp"),
            weight,
            P(),
            weight,
            weight,
            weight,
        ),
        out_specs=(
            token,
            token,
            P(),
            weight,
            P("tp"),
            weight,
            P(),
            weight,
            weight,
            weight,
            P("tp"),
        ),
        check_vma=False,
    )
```

```python
import functools
import math

import jax
import jax.numpy as jnp
from jax import lax
from jax.experimental import pallas as pl
from jax.experimental.pallas import tpu as pltpu
from jax.sharding import PartitionSpec as P

HEAD = 128
EPSILON = 1e-06
THETA = 1000000.0
CLIP_BOUND = 4.0
NEG_FILL = -1e30
SCALE = HEAD ** (-0.5)
SCALE_2 = SCALE * math.log2(math.e)
MIB = 1 << 20
CUTS = 3


def cuts(width):
    return [width // 4, width // 4, width // 2]


PACE = 175_000_000


def cost(us):
    return pl.CostEstimate(flops=int(us * PACE), bytes_accessed=1000, transcendentals=0)


BF16 = jnp.bfloat16
F32 = jnp.float32


def dot_nt(left, right):
    return lax.dot_general(left, right, (((1,), (1,)), ((), ())), preferred_element_type=F32)


def dot_nn(left, right):
    return jnp.dot(left, right, preferred_element_type=F32)


def seen_block(hot, reach_rows, col_at, row_at, bk, bq):
    linked = dot_nt(hot, reach_rows) > 0.5
    cols = col_at + lax.broadcasted_iota(jnp.int32, (bk, bq), 0)
    rows = row_at + lax.broadcasted_iota(jnp.int32, (bk, bq), 1)
    return (linked & (cols <= rows)) | (cols == rows)


def attention_forward_kernel(
    group, bq, bk, blocks, first, count, chosen, places, q_ref, kv_ref, reach_ref, hot_ref,
    out_ref, lse_ref, top_ref, max_s, sum_s, acc_s,
):
    row_block = pl.program_id(0) + first
    max_s[...] = jnp.full_like(max_s, NEG_FILL)
    sum_s[...] = jnp.zeros_like(sum_s)
    acc_s[...] = jnp.zeros_like(acc_s)
    row_at = places[blocks] + row_block * bq

    def body(step, carry):
        block = chosen[row_block * blocks + step]
        here = pl.ds(pl.multiple_of(block * bk, bk), bk)
        keys = kv_ref[here, :HEAD]
        values_t = kv_ref[here, HEAD:].T
        seen = seen_block(hot_ref[here, :], reach_ref[...], places[block], row_at, bk, bq)
        for h in range(group):
            score = jnp.where(seen, dot_nt(keys, q_ref[:, h * HEAD : (h + 1) * HEAD]), NEG_FILL)
            old = max_s[h : h + 1, :]
            new = jnp.maximum(old, jnp.max(score, axis=0, keepdims=True))
            prob = jnp.exp2((score - new) * SCALE_2)
            fade = jnp.exp2((old - new) * SCALE_2)
            max_s[h : h + 1, :] = new
            sum_s[h : h + 1, :] = sum_s[h : h + 1, :] * fade + jnp.sum(prob, axis=0, keepdims=True)
            acc_s[h] = acc_s[h] * fade + dot_nn(values_t, prob.astype(BF16))
        return carry

    lax.fori_loop(0, count[row_block], body, 0)
    top_ref[...] = max_s[...] * SCALE
    lse_ref[...] = max_s[...] * SCALE_2 + jnp.log2(sum_s[...])
    for h in range(group):
        out_ref[:, h * HEAD : (h + 1) * HEAD] = (acc_s[h] / sum_s[h : h + 1, :]).T.astype(BF16)


def attention_forward(lists, queries, kv, reach_rows, hot, bq, bk, first, rows):
    width = queries.shape[1]
    first //= bq
    slots = kv.shape[0]
    group = width // HEAD
    whole = lambda *_: (0, 0)
    row = lambda i, *_: (i, 0)
    col = lambda i, *_: (0, i)
    return pl.pallas_call(
        functools.partial(attention_forward_kernel, group, bq, bk, slots // bk, first),
        grid_spec=pltpu.PrefetchScalarGridSpec(
            num_scalar_prefetch=3,
            grid=(rows // bq,),
            in_specs=[
                pl.BlockSpec((bq, width), lambda i, *_: (i + first, 0)),
                pl.BlockSpec((slots, 2 * HEAD), whole),
                pl.BlockSpec((bq, HEAD), lambda i, *_: (i + first, 0)),
                pl.BlockSpec((slots, HEAD), whole),
            ],
            out_specs=[
                pl.BlockSpec((bq, width), row),
                pl.BlockSpec((group, bq), col),
                pl.BlockSpec((group, bq), col),
            ],
            scratch_shapes=[
                pltpu.VMEM((group, bq), F32),
                pltpu.VMEM((group, bq), F32),
                pltpu.VMEM((group, HEAD, bq), F32),
            ],
        ),
        out_shape=[
            jax.ShapeDtypeStruct((rows, width), BF16),
            jax.ShapeDtypeStruct((group, rows), F32),
            jax.ShapeDtypeStruct((group, rows), F32),
        ],
        compiler_params=pltpu.CompilerParams(vmem_limit_bytes=32 * MIB),
        cost_estimate=cost(15),
        name="attention_forward",
    )(*lists, queries, kv, reach_rows, hot)


def attention_backward_kernel(
    group, bq, bk, blocks, count, chosen, places, q_ref, do_ref, lse_ref, delta_ref, kv_ref,
    reach_ref, hot_ref, cos_ref, sin_ref, dq_ref, dkv_ref, acc_s, dk_s, dv_s,
):
    row_block = pl.program_id(0)

    @pl.when(row_block == 0)
    def _():
        dk_s[...] = jnp.zeros_like(dk_s)
        dv_s[...] = jnp.zeros_like(dv_s)

    acc_s[...] = jnp.zeros_like(acc_s)
    row_at = places[blocks] + row_block * bq

    def body(step, carry):
        block = chosen[row_block * blocks + step]
        here = pl.ds(pl.multiple_of(block * bk, bk), bk)
        keys = kv_ref[here, :HEAD]
        values = kv_ref[here, HEAD:]
        keys_t = keys.T
        seen = seen_block(hot_ref[here, :], reach_ref[...], places[block], row_at, bk, bq)
        dk = jnp.zeros((bk, HEAD), F32)
        dv = jnp.zeros((bk, HEAD), F32)
        for h in range(group):
            qh = q_ref[:, h * HEAD : (h + 1) * HEAD]
            doh = do_ref[:, h * HEAD : (h + 1) * HEAD]
            prob = jnp.where(
                seen, jnp.exp2(dot_nt(keys, qh) * SCALE_2 - lse_ref[h : h + 1, :]), 0.0
            )
            ds = (prob * (dot_nt(values, doh) - delta_ref[h : h + 1, :])).astype(BF16)
            dv = dv + dot_nn(prob.astype(BF16), doh)
            dk = dk + dot_nn(ds, qh)
            acc_s[h] = acc_s[h] + dot_nn(keys_t, ds)
        dk_s[here, :] += dk
        dv_s[here, :] += dv
        return carry

    lax.fori_loop(0, count[row_block], body, 0)
    for h in range(group):
        d_query = (acc_s[h] * SCALE).T
        dq_ref[:, h * HEAD : (h + 1) * HEAD] = turned(
            d_query, cos_ref[...], -sin_ref[...]
        ).astype(BF16)

    @pl.when(row_block == pl.num_programs(0) - 1)
    def _():
        dkv_ref[:, :HEAD] = (dk_s[...] * SCALE).astype(BF16)
        dkv_ref[:, HEAD:] = dv_s[...].astype(BF16)


def attention_backward(
    lists, queries, d_att, lse, delta, kv, reach_rows, hot, cosine, sine, bq, bk
):
    rows, width = queries.shape
    slots = kv.shape[0]
    group = width // HEAD
    whole = lambda *_: (0, 0)
    row = lambda i, *_: (i, 0)
    col = lambda i, *_: (0, i)
    return pl.pallas_call(
        functools.partial(attention_backward_kernel, group, bq, bk, slots // bk),
        grid_spec=pltpu.PrefetchScalarGridSpec(
            num_scalar_prefetch=3,
            grid=(rows // bq,),
            in_specs=[
                pl.BlockSpec((bq, width), row),
                pl.BlockSpec((bq, width), row),
                pl.BlockSpec((group, bq), col),
                pl.BlockSpec((group, bq), col),
                pl.BlockSpec((slots, 2 * HEAD), whole),
                pl.BlockSpec((bq, HEAD), row),
                pl.BlockSpec((slots, HEAD), whole),
                pl.BlockSpec((bq, HEAD), row),
                pl.BlockSpec((bq, HEAD), row),
            ],
            out_specs=[
                pl.BlockSpec((bq, width), row),
                pl.BlockSpec((slots, 2 * HEAD), whole),
            ],
            scratch_shapes=[
                pltpu.VMEM((group, HEAD, bq), F32),
                pltpu.VMEM((slots, HEAD), F32),
                pltpu.VMEM((slots, HEAD), F32),
            ],
        ),
        out_shape=[
            jax.ShapeDtypeStruct((rows, width), BF16),
            jax.ShapeDtypeStruct((slots, 2 * HEAD), BF16),
        ],
        compiler_params=pltpu.CompilerParams(vmem_limit_bytes=40 * MIB),
        cost_estimate=cost(54),
        name="attention_backward",
    )(*lists, queries, d_att, lse, delta, kv, reach_rows, hot, cosine, sine)


def join(mine, depth, places, pieces, joined, at_col=None):
    cols = pieces[0].shape[1]
    where = slice(None) if at_col is None else pl.ds(pl.multiple_of(at_col, HEAD), cols)
    for (j, row), piece in zip(places, pieces):
        at = pl.multiple_of((mine ^ j) * depth + row, 16)
        joined[pl.ds(at, piece.shape[0]), where] = piece[...]


class Rows:
    def __init__(self, pieces, depth, tf=None):
        self.depth = depth
        self.places = [(j, row) for j, row, _ in pieces]
        self.arrays = [array for _, _, array in pieces]
        if tf is None:
            self.specs = [once(array.shape) for array in self.arrays]
        else:
            self.specs = [pl.BlockSpec((array.shape[0], tf), col_block) for array in self.arrays]

    def __len__(self):
        return len(self.arrays)

    def join(self, mine, refs, joined, at_col=None):
        join(mine, self.depth, self.places, refs, joined, at_col)


def whole_block(*_):
    return (0, 0)


def row_block(i, *_):
    return (i, 0)


def col_block(i, *_):
    return (0, i)


def once(shape):
    return pl.BlockSpec(shape, whole_block, pipeline_mode=pl.Buffered(1))


def call(kernel, grid, in_specs, out_specs, out_shape, scratch, vmem, us, name):
    return pl.pallas_call(
        kernel,
        grid_spec=pltpu.PrefetchScalarGridSpec(
            num_scalar_prefetch=1,
            grid=(grid,),
            in_specs=in_specs,
            out_specs=out_specs,
            scratch_shapes=scratch,
        ),
        out_shape=out_shape,
        compiler_params=pltpu.CompilerParams(vmem_limit_bytes=vmem * MIB),
        cost_estimate=cost(us),
        name=name,
    )


def shape(dims, dtype):
    return jax.ShapeDtypeStruct(dims, dtype)


def clear_tail(tail, *joined):
    if tail:

        @pl.when(pl.program_id(0) == pl.num_programs(0) - 1)
        def _():
            for one in joined:
                one[:, tail:] = jnp.zeros_like(one[:, tail:])


def gate_up_kernel(gates, ups, place, h_ref, *refs):
    gate_refs, refs = refs[: len(gates)], refs[len(gates) :]
    up_refs, refs = refs[: len(ups)], refs[len(ups) :]
    act_ref, by_gate_ref, by_up_ref, gate_s, up_s = refs
    gates.join(place[0], gate_refs, gate_s)
    ups.join(place[0], up_refs, up_s)
    gate = dot_nn(h_ref[...], gate_s[...])
    up = dot_nn(h_ref[...], up_s[...])
    sig = jax.nn.sigmoid(gate)
    silu = gate * sig
    act_ref[...] = (silu * up).astype(BF16)
    by_up_ref[...] = silu.astype(BF16)
    by_gate_ref[...] = (up * sig * (1.0 + gate * (1.0 - sig))).astype(BF16)


def gate_up(place, hidden, gates, ups, depth, tf):
    rows, width = hidden.shape
    units = gates[0][2].shape[1]
    gates, ups = Rows(gates, depth, tf), Rows(ups, depth, tf)
    return call(
        functools.partial(gate_up_kernel, gates, ups),
        pl.cdiv(units, tf),
        [once((rows, width))] + gates.specs + ups.specs,
        [pl.BlockSpec((rows, tf), col_block)] * 3,
        [shape((rows, units), BF16)] * 3,
        [pltpu.VMEM((width, tf), BF16)] * 2,
        60,
        40,
        "gate_up",
    )(place, hidden, *gates.arrays, *ups.arrays)


def gate_up_back_kernel(gates, ups, downs, tail, place, c_ref, by_gate_ref, by_up_ref, *refs):
    gate_refs, refs = refs[: len(gates)], refs[len(gates) :]
    up_refs, refs = refs[: len(ups)], refs[len(ups) :]
    down_refs, refs = refs[: len(downs)], refs[len(downs) :]
    dg_ref, du_ref, *dh_refs, gate_s, up_s, down_s, sum_s = refs
    step = pl.program_id(0)
    gates.join(place[0], gate_refs, gate_s)
    ups.join(place[0], up_refs, up_s)
    downs.join(place[0], down_refs, down_s)
    clear_tail(tail, gate_s, up_s, down_s)
    d_act = dot_nn(c_ref[...], down_s[...])
    by_gate, by_up = by_gate_ref[...].astype(F32), by_up_ref[...].astype(F32)
    if tail:
        last = step == pl.num_programs(0) - 1
        inside = lax.broadcasted_iota(jnp.int32, by_gate.shape, 1) < jnp.where(
            last, tail, by_gate.shape[1]
        )
        by_gate = jnp.where(inside, by_gate, 0.0)
        by_up = jnp.where(inside, by_up, 0.0)
    d_gate = (d_act * by_gate).astype(BF16)
    d_up = (d_act * by_up).astype(BF16)
    dg_ref[...] = d_gate
    du_ref[...] = d_up

    @pl.when(step == 0)
    def _():
        sum_s[...] = jnp.zeros_like(sum_s)

    sum_s[...] += dot_nt(d_gate, gate_s[...]) + dot_nt(d_up, up_s[...])

    @pl.when(step == pl.num_programs(0) - 1)
    def _():
        at = 0
        for dh_ref in dh_refs:
            cols = dh_ref.shape[1]
            dh_ref[...] = sum_s[:, at : at + cols].astype(BF16)
            at += cols


def gate_up_back(place, cotangent, by_gate, by_up, gates, ups, downs, depth, tf):
    rows, width = cotangent.shape
    units = by_gate.shape[1]
    gates, ups, downs = (Rows(p, depth, tf) for p in (gates, ups, downs))
    return call(
        functools.partial(gate_up_back_kernel, gates, ups, downs, units % tf),
        pl.cdiv(units, tf),
        [once((rows, width))]
        + [pl.BlockSpec((rows, tf), col_block)] * 2
        + gates.specs
        + ups.specs
        + downs.specs,
        [pl.BlockSpec((rows, tf), col_block)] * 2 + [once((rows, cut)) for cut in cuts(width)],
        [shape((rows, units), BF16)] * 2 + [shape((rows, cut), BF16) for cut in cuts(width)],
        [pltpu.VMEM((width, tf), BF16)] * 3 + [pltpu.VMEM((rows, width), F32)],
        60,
        62,
        "gate_up_back",
    )(place, cotangent, by_gate, by_up, *gates.arrays, *ups.arrays, *downs.arrays)


def whole_grad_kernel(left_ref, right_ref, out_ref):
    out_ref[...] = dot_nn(left_ref[...], right_ref[...]).astype(BF16)


def whole_grad(left_t, right, tf):
    width, rows = left_t.shape
    units = right.shape[1]
    return pl.pallas_call(
        whole_grad_kernel,
        grid=(pl.cdiv(units, tf),),
        in_specs=[once((width, rows)), pl.BlockSpec((rows, tf), col_block)],
        out_specs=pl.BlockSpec((width, tf), col_block),
        out_shape=shape((width, units), BF16),
        compiler_params=pltpu.CompilerParams(vmem_limit_bytes=48 * MIB),
        cost_estimate=cost(19 if units > 2048 else 6),
        name="whole_grad",
    )(left_t, right)


def weight_grad_kernel(depth, parts, place, left_ref, right_ref, keep_ref, send_ref):
    for j in range(parts):
        half = keep_ref if j % 2 == 0 else send_ref
        rows = pl.ds(pl.multiple_of((place[0] ^ j) * depth, 16), depth)
        at = (j // 2) * depth
        half[at : at + depth, :] = dot_nn(left_ref[rows, :], right_ref[...]).astype(BF16)


def weight_grad(place, left_t, right, parts, tf):
    width, rows = left_t.shape
    units = right.shape[1]
    return call(
        functools.partial(weight_grad_kernel, width // parts, parts),
        pl.cdiv(units, tf),
        [once((width, rows)), pl.BlockSpec((rows, tf), col_block)],
        [pl.BlockSpec((width // 2, tf), col_block)] * 2,
        [shape((width // 2, units), BF16)] * 2,
        [],
        48,
        19 if units > 2048 else 7,
        "weight_grad",
    )(place, left_t, right)


def add_kernel(counts, *refs):
    out_ref, at, col = refs[-1], 0, 0
    for count in counts:
        parts = refs[at : at + count]
        cols = parts[0].shape[1]
        total = sum(ref[...].astype(F32) for ref in parts)
        out_ref[:, col : col + cols] = total.astype(BF16)
        at, col = at + count, col + cols


def add_rows(rows, *groups):
    parts = [part for group in groups for part in group]
    cols = sum(group[0][0].shape[1] for group in groups)
    step = math.gcd(rows, 64, *[row for _, row in parts])
    return pl.pallas_call(
        functools.partial(add_kernel, [len(group) for group in groups]),
        grid=(rows // step,),
        in_specs=[
            pl.BlockSpec((step, array.shape[1]), lambda i, at=row // step: (at + i, 0))
            for array, row in parts
        ],
        out_specs=pl.BlockSpec((step, cols), lambda i: (i, 0)),
        out_shape=shape((rows, cols), BF16),
        compiler_params=pltpu.CompilerParams(vmem_limit_bytes=32 * MIB),
        cost_estimate=cost(4),
        name="add_rows",
    )(*[array for array, _ in parts])


def mark_kernel(place_ref, out_ref):
    for at in range(2):
        out_ref[at] = place_ref[at]


def mark(place):
    place.v = pl.pallas_call(
        mark_kernel,
        in_specs=[pl.BlockSpec(memory_space=pltpu.SMEM)],
        out_specs=pl.BlockSpec(memory_space=pltpu.SMEM),
        out_shape=shape((2,), jnp.int32),
        cost_estimate=cost(1),
        name="mark",
    )(place.v)
    return place


def down_project_kernel(downs, place, act_ref, *refs):
    down_refs, (out_ref, down_s, sum_s) = refs[: len(downs)], refs[len(downs) :]
    step = pl.program_id(0)
    downs.join(place[0], down_refs, down_s)

    @pl.when(step == 0)
    def _():
        sum_s[...] = jnp.zeros_like(sum_s)

    sum_s[...] += dot_nt(act_ref[...], down_s[...])

    @pl.when(step == pl.num_programs(0) - 1)
    def _():
        out_ref[...] = sum_s[...].astype(BF16)


def down_project(place, act, downs, width, depth, tf):
    rows, units = act.shape
    downs = Rows(downs, depth, tf)
    return call(
        functools.partial(down_project_kernel, downs),
        units // tf,
        [pl.BlockSpec((rows, tf), col_block)] + downs.specs,
        once((rows, width)),
        shape((rows, width), BF16),
        [pltpu.VMEM((width, tf), BF16), pltpu.VMEM((rows, width), F32)],
        48,
        24,
        "down_project",
    )(place, act, *downs.arrays)


def inverse_rms(values):
    return lax.rsqrt(jnp.mean(values * values, axis=-1, keepdims=True) + EPSILON)


def turned(values, cosine, sine):
    return values * cosine + pltpu.roll(values, HEAD // 2, 1) * sine


def mix_kernel(weight, group, place, x_ref, gain_ref, bias_ref, cos_ref, sin_ref, *refs):
    pieces, (q_ref, kv_ref, ht_ref, weight_s) = refs[: len(weight)], refs[len(weight) :]

    @pl.when(pl.program_id(0) == 0)
    def _():
        weight.join(place[0], pieces, weight_s)

    x = x_ref[...].astype(F32)
    hidden = (x * inverse_rms(x) * gain_ref[...].astype(F32)).astype(BF16)
    ht_ref[...] = hidden.T
    mixed = dot_nn(hidden, weight_s[...]) + bias_ref[...].astype(F32)
    cosine, sine = cos_ref[...], sin_ref[...]
    for h in range(group):
        at = slice(h * HEAD, (h + 1) * HEAD)
        q_ref[:, at] = turned(mixed[:, at], cosine, sine).astype(BF16)
    split = group * HEAD
    kv_ref[:, :HEAD] = turned(mixed[:, split : split + HEAD], cosine, sine).astype(BF16)
    kv_ref[:, HEAD:] = mixed[:, split + HEAD :].astype(BF16)


def mix(place, tokens, gain, bias, cosine, sine, pieces, depth, group, bq):
    rows, width = tokens.shape
    cols = pieces[0][2].shape[1]
    weight = Rows(pieces, depth)
    return call(
        functools.partial(mix_kernel, weight, group),
        rows // bq,
        [
            pl.BlockSpec((bq, width), row_block),
            once((1, width)),
            once((1, cols)),
            pl.BlockSpec((bq, HEAD), row_block),
            pl.BlockSpec((bq, HEAD), row_block),
        ]
        + weight.specs,
        [
            pl.BlockSpec((bq, group * HEAD), row_block),
            pl.BlockSpec((bq, 2 * HEAD), row_block),
            pl.BlockSpec((width, bq), col_block),
        ],
        [
            shape((rows, group * HEAD), BF16),
            shape((rows, 2 * HEAD), BF16),
            shape((width, rows), BF16),
        ],
        [pltpu.VMEM((width, cols), BF16)],
        32,
        8,
        "mix",
    )(place, tokens, gain[None], bias[None], cosine, sine, *weight.arrays)


def branch_kernel(weight, parts, place, x_ref, own_ref, upper_ref, lower_ref, gain_ref, *refs):
    own_w, other_w = refs[: len(weight)], refs[len(weight) : len(weight) + parts]
    mid_ref, h_ref, ht_ref, weight_s, att_s = refs[len(weight) + parts :]
    split = own_ref.shape[1]
    own_at = pl.multiple_of(place[1] * split, HEAD)
    other_at = pl.multiple_of((1 - place[1]) * split, HEAD)

    @pl.when(pl.program_id(0) == 0)
    def _():
        weight.join(place[0], own_w, weight_s, own_at)
        join(place[0], weight.depth, [(j, 0) for j in range(parts)], other_w, weight_s, other_at)

    att_s[:, pl.ds(own_at, split)] = own_ref[...]
    steps = pl.num_programs(0)

    @pl.when(pl.program_id(0) < steps // 2)
    def _():
        att_s[:, pl.ds(other_at, split)] = upper_ref[...]

    @pl.when(pl.program_id(0) >= steps // 2)
    def _():
        att_s[:, pl.ds(other_at, split)] = lower_ref[...]

    mid = x_ref[...].astype(F32) + dot_nt(att_s[...], weight_s[...])
    mid_ref[...] = mid
    hidden = (mid * inverse_rms(mid) * gain_ref[...].astype(F32)).astype(BF16)
    h_ref[...] = hidden
    ht_ref[...] = hidden.T


def branch(place, tokens, own, upper, lower, gain, pieces, other_pieces, depth, bq):
    rows, width = tokens.shape
    cols = own.shape[1]
    parts = width // depth
    weight = Rows(pieces, depth)
    wide = pl.BlockSpec((bq, width), row_block)
    narrow = pl.BlockSpec((bq, cols), row_block)
    other_specs = [once((depth, cols))] * parts
    half = rows // bq // 2
    return call(
        functools.partial(branch_kernel, weight, parts),
        rows // bq,
        [
            wide,
            narrow,
            pl.BlockSpec((bq, cols), lambda i, *_: (jnp.minimum(i, half - 1), 0)),
            pl.BlockSpec((bq, cols), lambda i, *_: (jnp.maximum(i - half, 0), 0)),
            once((1, width)),
        ]
        + weight.specs
        + other_specs,
        [wide, wide, pl.BlockSpec((width, bq), col_block)],
        [shape((rows, width), F32), shape((rows, width), BF16), shape((width, rows), BF16)],
        [pltpu.VMEM((width, 2 * cols), BF16), pltpu.VMEM((bq, 2 * cols), BF16)],
        40,
        12,
        "branch",
    )(place, tokens, own, upper, lower, gain[None], *weight.arrays, *other_pieces)


def middle_back_kernel(
    weight, group, place, mid_ref, c_ref, gain_ref, att_ref, *refs
):
    own_refs, other_refs, refs = refs[:CUTS], refs[CUTS : 2 * CUTS], refs[2 * CUTS :]
    pieces, refs = refs[: len(weight)], refs[len(weight) :]
    dm_ref, dbt_ref, da_ref, delta_ref, dgain_ref, weight_s = refs

    @pl.when(pl.program_id(0) == 0)
    def _():
        weight.join(place[0], pieces, weight_s)
        dgain_ref[...] = jnp.zeros_like(dgain_ref)

    mid = mid_ref[...]
    inverse = inverse_rms(mid)
    normed = mid * inverse
    own = jnp.concatenate([ref[...] for ref in own_refs], axis=1).astype(F32)
    other = jnp.concatenate([ref[...] for ref in other_refs], axis=1).astype(F32)
    dgain_ref[...] += jnp.sum(own * normed, axis=0, keepdims=True)
    scaled = (own + other) * gain_ref[...].astype(F32)
    d_mid = c_ref[...].astype(F32) + inverse * (
        scaled - normed * jnp.mean(scaled * normed, axis=-1, keepdims=True)
    )
    dm_ref[...] = d_mid
    d_branch = d_mid.astype(BF16)
    dbt_ref[...] = d_branch.T
    d_att = dot_nn(d_branch, weight_s[...]).astype(BF16)
    da_ref[...] = d_att
    product = d_att.astype(F32) * att_ref[...].astype(F32)
    for h in range(group):
        delta_ref[h : h + 1, :] = jnp.sum(
            product[:, h * HEAD : (h + 1) * HEAD].T, axis=0, keepdims=True
        )


def middle_back(place, own, other, mid, cotangent, gain, attended, pieces, depth, bq):
    rows, width = mid.shape
    cols = attended.shape[1]
    weight = Rows(pieces, depth)
    group = cols // HEAD
    wide = pl.BlockSpec((bq, width), row_block)
    narrow = pl.BlockSpec((bq, cols), row_block)
    return call(
        functools.partial(middle_back_kernel, weight, group),
        rows // bq,
        [wide, wide, once((1, width)), narrow]
        + [pl.BlockSpec((bq, cut), row_block) for cut in cuts(width)] * 2
        + weight.specs,
        [
            wide,
            pl.BlockSpec((width, bq), col_block),
            narrow,
            pl.BlockSpec((group, bq), col_block),
            pl.BlockSpec((1, width), whole_block),
        ],
        [
            shape((rows, width), F32),
            shape((width, rows), BF16),
            shape((rows, cols), BF16),
            shape((group, rows), F32),
            shape((1, width), F32),
        ],
        [pltpu.VMEM((width, cols), BF16)],
        48,
        13,
        "middle_back",
    )(place, mid, cotangent, gain[None], attended, *own, *other, *weight.arrays)


def mix_back_kernel(
    weight, group, place, dq_ref, dkv_ref, cos_ref, sin_ref, x_ref, *refs
):
    pieces, refs = refs[: len(weight)], refs[len(weight) :]
    dm_ref, dbias_ref, dgain_ref, *dh_refs, weight_s = refs

    @pl.when(pl.program_id(0) == 0)
    def _():
        weight.join(place[0], pieces, weight_s)
        dgain_ref[...] = jnp.zeros_like(dgain_ref)
        dbias_ref[...] = jnp.zeros_like(dbias_ref)

    split = group * HEAD
    dm_ref[:, :split] = dq_ref[...]
    d_keys = dkv_ref[:, :HEAD].astype(F32)
    dm_ref[:, split : split + HEAD] = turned(d_keys, cos_ref[...], -sin_ref[...]).astype(BF16)
    dm_ref[:, split + HEAD :] = dkv_ref[:, HEAD:]
    d_mixed = dm_ref[...]
    dbias_ref[...] += jnp.sum(d_mixed.astype(F32), axis=0, keepdims=True)
    d_hidden = dot_nt(d_mixed, weight_s[...])
    x = x_ref[...].astype(F32)
    dgain_ref[...] += jnp.sum(d_hidden * (x * inverse_rms(x)), axis=0, keepdims=True)
    at = 0
    for dh_ref in dh_refs:
        cols = dh_ref.shape[1]
        dh_ref[...] = d_hidden[:, at : at + cols].astype(BF16)
        at += cols


def mix_back(place, dq, dkv, cosine, sine, tokens, pieces, depth, bq):
    rows, width = tokens.shape
    cols = pieces[0][2].shape[1]
    weight = Rows(pieces, depth)
    group = dq.shape[1] // HEAD
    wide = pl.BlockSpec((bq, width), row_block)
    return call(
        functools.partial(mix_back_kernel, weight, group),
        rows // bq,
        [
            pl.BlockSpec((bq, group * HEAD), row_block),
            pl.BlockSpec((bq, 2 * HEAD), row_block),
            pl.BlockSpec((bq, HEAD), row_block),
            pl.BlockSpec((bq, HEAD), row_block),
            wide,
        ]
        + weight.specs,
        [
            pl.BlockSpec((bq, cols), row_block),
            pl.BlockSpec((1, cols), whole_block),
            pl.BlockSpec((1, width), whole_block),
        ]
        + [pl.BlockSpec((bq, cut), row_block) for cut in cuts(width)],
        [
            shape((rows, cols), BF16),
            shape((1, cols), F32),
            shape((1, width), F32),
        ]
        + [shape((rows, cut), BF16) for cut in cuts(width)],
        [pltpu.VMEM((width, cols), BF16)],
        32,
        8,
        "mix_back",
    )(place, dq, dkv, cosine, sine, tokens, *weight.arrays)


def input_back_kernel(place, x_ref, gain_ref, dm_ref, *refs):
    own_refs, other_refs, (out_ref,) = refs[:CUTS], refs[CUTS : 2 * CUTS], refs[2 * CUTS :]
    own = jnp.concatenate([ref[...] for ref in own_refs], axis=1).astype(F32)
    other = jnp.concatenate([ref[...] for ref in other_refs], axis=1).astype(F32)
    x = x_ref[...].astype(F32)
    inverse = inverse_rms(x)
    normed = x * inverse
    scaled = (own + other) * gain_ref[...].astype(F32)
    out_ref[...] = dm_ref[...] + inverse * (
        scaled - normed * jnp.mean(scaled * normed, axis=-1, keepdims=True)
    )


def input_back(place, own, other, tokens, gain, d_mid, bq):
    rows, width = tokens.shape
    wide = pl.BlockSpec((bq, width), row_block)
    return call(
        input_back_kernel,
        rows // bq,
        [wide, once((1, width)), wide]
        + [pl.BlockSpec((bq, cut), row_block) for cut in cuts(width)] * 2,
        wide,
        shape((rows, width), F32),
        [],
        32,
        8,
        "input_back",
    )(place, tokens, gain[None], d_mid, *own, *other)


class Box:
    def __init__(self, v):
        self.v = v


def boxes(values):
    return [Box(v) for v in values]


def fence(*items):
    flat = []
    for item in items:
        flat += item if isinstance(item, (list, tuple)) else [item]
    for item, v in zip(flat, lax.optimization_barrier([item.v for item in flat])):
        item.v = v


def held(value, *items):
    one = Box(value)
    fence(one, *items)
    return one.v


def swap(value, axis, size, bit):
    return lax.ppermute(value, axis, [(i, i ^ bit) for i in range(size)])


class Pieces:
    def __init__(self, own, size, slabs=1):
        if size != 4 or own.shape[0] % (16 * slabs):
            slabs = 1
        self.size, self.own, self.slabs = size, own, slabs
        self.depth = own.shape[0] // slabs
        self.got, self.cuts = {}, []

    def away(self, own):
        got, bit = {0: own}, self.size // 2
        while bit > 1:
            got.update({j ^ bit: swap(p, "shard", self.size, bit) for j, p in got.items()})
            bit //= 2
        return {j: Box(p) for j, p in got.items() if j}

    def far(self, slab, *first):
        if slab >= self.slabs:
            return []
        if self.cuts:
            own = held(self.cuts[slab].v, *first)
        else:
            own = held(self.own, *first)[slab * self.depth : (slab + 1) * self.depth]
        got = self.away(own)
        self.got.update({(j, slab): p for j, p in got.items()})
        return list(got.values())

    def cut(self, *first):
        own = held(self.own, *first)
        if self.slabs > 1:
            self.cuts = boxes(
                [own[k * self.depth : (k + 1) * self.depth] for k in range(self.slabs)]
            )
        return self.cuts

    def far_by_ctx(self, contexts, *first):
        rows = self.own.shape[0] // contexts
        own = lax.dynamic_slice_in_dim(
            held(self.own, *first), lax.axis_index("ctx") * rows, rows, 0
        )
        self.parts = self.away(own)
        return list(self.parts.values())

    def spread(self):
        for j, part in self.parts.items():
            self.got[j, 0] = Box(lax.all_gather(part.v, "ctx", axis=0, tiled=True))
        return [self.got[j, 0] for j in self.parts]

    def near_own(self, *first):
        self.near = Box(swap(held(self.own, *first), "shard", self.size, 1))
        return [self.near]

    def near_rest(self, slab, *first):
        if slab >= self.slabs:
            return []
        far = [j for j in range(2, self.size, 2)]
        if first:
            fence(*[self.got[j, slab] for j in far], *first)
        for j in far:
            self.got[j ^ 1, slab] = Box(swap(self.got[j, slab].v, "shard", self.size, 1))
        return [self.got[j ^ 1, slab] for j in far]

    def all(self):
        found = [(0, 0, self.own), (1, 0, self.near.v)]
        found += [
            (j, k * self.depth, p.v) for (j, k), p in sorted(self.got.items(), key=lambda i: i[0])
        ]
        return found


class Reduction:
    def __init__(self, shards, contexts, slabs):
        self.shards, self.chain = shards, contexts == 4
        self.slabs = slabs if shards == 4 else 1
        self.keep, self.send, self.got = [], [], []
        self.own, self.one, self.two, self.three = {}, {}, {}, {}
        self.by_sum = {}

    def make(self, place, left_t, right, tf):
        keep, send = boxes(weight_grad(place.v, left_t, right, self.shards, tf))
        self.keep.append(keep)
        self.send.append(send)
        return send

    def cores(self):
        self.got.append(Box(swap(self.send[len(self.got)].v, "shard", self.shards, 1)))
        return self.got[-1]

    def pairs(self, row):
        return [[(keep.v, row), (got.v, row)] for keep, got in zip(self.keep, self.got)]

    def sum_away(self):
        rows = self.keep[0].v.shape[0]
        if self.shards == 4:
            size = rows // 2 // self.slabs
            self.away = [
                Box(add_rows(size, *self.pairs(rows // 2 + slab * size)))
                for slab in range(self.slabs)
            ]
        else:
            self.away = [Box(add_rows(rows, *self.pairs(0)))]
        return self.away

    def chips(self):
        if self.shards == 4:
            self.last = [Box(swap(part.v, "shard", 4, 2)) for part in self.away]
            return self.last
        held, bit, count = self.away[0].v, 2, self.shards // 2
        while bit < self.shards:
            size = held.shape[0] // count
            blocks = [held[at * size : (at + 1) * size] for at in range(count)]
            away = swap(jnp.concatenate(blocks[1::2], axis=0), "shard", self.shards, bit)
            here = jnp.concatenate(blocks[::2], axis=0)
            held = here if 2 * bit >= self.shards else here + away
            bit, count = 2 * bit, count // 2
        self.here, self.last = held, boxes([away])
        return self.last

    def arrived(self, slab):
        if slab >= self.slabs:
            return []
        last = self.last[slab].v
        if self.shards != 4:
            self.own[slab] = Box(self.here + last)
        elif len(self.keep) == 1:
            size = last.shape[0]
            self.own[slab] = Box(add_rows(size, self.pairs(slab * size)[0] + [(last, 0)]))
        else:
            size = last.shape[0]
            here = add_rows(size, *self.pairs(slab * size))
            self.own[slab] = Box(add_rows(size, [(here, 0), (last, 0)]))
        return [self.own[slab]]

    def whole_sum(self, slab):
        if slab >= self.slabs:
            return []
        self.by_sum[slab] = Box(lax.psum(self.own[slab].v, "ctx"))
        return [self.by_sum[slab]]

    def inward(self, slab):
        if slab >= self.slabs:
            return []
        if not self.chain:
            return self.whole_sum(slab)
        self.one[slab] = Box(lax.ppermute(self.own[slab].v, "ctx", [(0, 1), (3, 2)]))
        return [self.one[slab]]

    def middle(self, slab):
        if not self.chain or slab >= self.slabs:
            return []
        self.own[slab] = Box(self.own[slab].v + self.one[slab].v)
        self.two[slab] = Box(lax.ppermute(self.own[slab].v, "ctx", [(1, 2), (2, 1)]))
        return [self.two[slab]]

    def outward(self, slab):
        if not self.chain or slab >= self.slabs:
            return []
        self.own[slab] = Box(self.own[slab].v + self.two[slab].v)
        self.three[slab] = Box(lax.ppermute(self.own[slab].v, "ctx", [(1, 0), (2, 3)]))
        return [self.three[slab]]

    def result(self):
        place = lax.axis_index("ctx")
        inside = (place == 1) | (place == 2)
        totals = [
            self.by_sum[slab].v
            if slab in self.by_sum
            else jnp.where(inside, self.own[slab].v, self.three[slab].v)
            for slab in range(self.slabs)
        ]
        whole = totals[0] if len(totals) == 1 else jnp.concatenate(totals, axis=0)
        return whole.astype(F32)


def tree_tables(seg_row, parent_row):
    seg_count = parent_row.shape[0]
    seg_ids = jnp.arange(seg_count, dtype=jnp.int32)
    one_hot = (seg_row[:, None] == seg_ids[None, :]).astype(jnp.int32)
    lengths = jnp.sum(one_hot, axis=0, dtype=jnp.int32)
    before = seg_ids[None, :] < seg_ids[:, None]
    starts = jnp.sum(jnp.where(before, lengths[None, :], 0), axis=1, dtype=jnp.int32)
    link = (parent_row[:, None] == seg_ids[None, :]) & (parent_row[:, None] != seg_ids[:, None])
    twice = jnp.any(link[:, :, None] & link[None, :, :], axis=1)
    strict = link | twice
    padding = parent_row == seg_ids
    reach = strict | ((seg_ids[:, None] == seg_ids[None, :]) & ~padding[:, None])
    offsets = jnp.sum(jnp.where(strict, lengths[None, :], 0), axis=1, dtype=jnp.int32) - starts
    return reach, offsets


def block_lists(row_hot, col_hot, reach, col_places, row_first, bq, bk):
    segs = reach.shape[0]
    row_has = jnp.any(row_hot.reshape(-1, bq, segs), axis=1)
    col_has = jnp.any(col_hot.reshape(-1, bk, segs), axis=1)
    row_blocks, col_blocks = row_has.shape[0], col_has.shape[0]
    row_reach = jnp.any(row_has[:, :, None] & reach[None], axis=1)
    meets = jnp.any(row_reach[:, None, :] & col_has[None], axis=2)
    col_at = col_places.reshape(-1, bk)[:, 0]
    row_at = row_first + bq * jnp.arange(row_blocks, dtype=jnp.int32)
    causal = col_at[None, :] < row_at[:, None] + bq
    diagonal = causal & (col_at[None, :] + bk > row_at[:, None])
    active = ((meets & causal) | diagonal) & (col_at >= 0)[None, :]
    ids = jnp.arange(col_blocks, dtype=jnp.int32)
    rank = jnp.sum(
        (active[:, None, :] & (ids[None, :] < ids[:, None])[None]).astype(jnp.int32), axis=2
    )
    placed = active[:, :, None] & (rank[:, :, None] == ids[None, None, :])
    chosen = jnp.sum(jnp.where(placed, ids[None, :, None], 0), axis=1, dtype=jnp.int32)
    count = jnp.sum(active.astype(jnp.int32), axis=1, dtype=jnp.int32)
    places = jnp.concatenate([col_at, row_first[None]])
    return count, chosen.reshape(-1), places


def layer(
    sizes, tokens, cotangent, segment, parent, gain_attn, qkv_weight, qkv_bias,
    out_weight, gain_ffn, gate_weight, up_weight, down_weight,
):
    shards, contexts, halves = sizes["shard"], sizes["ctx"], sizes["tp"]
    rows, width = tokens.shape
    group = out_weight.shape[1] // HEAD
    shard, ctx, half = lax.axis_index("shard"), lax.axis_index("ctx"), lax.axis_index("tp")
    place = jnp.stack([shard, half]).astype(jnp.int32)
    across = [(i, i ^ 1) for i in range(halves)]

    row_first = (ctx * rows).astype(jnp.int32)
    reach, offsets = tree_tables(segment[0], parent[0])
    seg_ids = jnp.arange(reach.shape[0], dtype=jnp.int32)
    behind = [jnp.maximum(ctx - k, 0) * rows for k in range(contexts)]
    seg_back = jnp.concatenate(
        [lax.dynamic_slice_in_dim(segment[0], at, rows, 0) for at in behind]
    )
    places_back = jnp.concatenate(
        [(ctx - k) * rows + jnp.arange(rows, dtype=jnp.int32) for k in range(contexts)]
    )
    col_hot = seg_back[:, None] == seg_ids[None, :]
    row_hot = col_hot[:rows]
    own_pos = places_back[:rows] + jnp.sum(
        jnp.where(row_hot, offsets[None, :], 0), axis=1, dtype=jnp.int32
    )
    pad = ((0, 0), (0, HEAD - reach.shape[0]))
    row_reach = jnp.any(row_hot[:, :, None] & reach[None], axis=1)
    reach_rows = jnp.pad(row_reach.astype(BF16), pad)
    hot = jnp.pad(col_hot.astype(BF16), pad)
    bq = math.gcd(rows, 256)
    bk_f, bk_b = math.gcd(rows, 128), math.gcd(rows, 512)
    lists_f = block_lists(row_hot, col_hot, reach, places_back, row_first, bq, bk_f)
    lists_b = block_lists(row_hot, col_hot, reach, places_back, row_first, bq, bk_b)
    lane = jnp.arange(HEAD, dtype=jnp.int32)
    frequency = THETA ** (-2.0 * (lane % (HEAD // 2)).astype(F32) / HEAD)
    angles = own_pos.astype(F32)[:, None] * frequency[None, :]
    cosine = jnp.cos(angles)
    sine = jnp.sin(angles) * jnp.where(lane < HEAD // 2, -1.0, 1.0)

    depth = width // shards
    qkv, out_w, gate, up, down = (
        Pieces(qkv_weight, shards),
        Pieces(out_weight, shards),
        Pieces(gate_weight, shards, 3),
        Pieces(up_weight, shards),
        Pieces(down_weight, shards, 4),
    )

    def over_tp(box):
        return Box(lax.ppermute(box.v, "tp", across))

    qkv_far = qkv.far(0)
    leaves, tree = jax.tree.flatten((reach_rows, hot, lists_f, lists_b, cosine, sine))
    leaves, place = boxes(leaves), Box(place)
    fence(leaves, place, qkv_far)
    reach_rows, hot, lists_f, lists_b, cosine, sine = tree.unflatten([leaf.v for leaf in leaves])
    qkv_near = qkv.near_own(qkv_far) + qkv.near_rest(0)
    out_far = out_w.far(0, qkv_far)
    out_near = out_w.near_own(qkv_far)
    out_other = {0: Box(lax.ppermute(held(out_weight, qkv_far), "tp", across))}
    fence(mark(place), qkv_near)
    up_parts = up.far_by_ctx(contexts, qkv_near)

    queries, kv_own, hidden_one_t = mix(
        place.v, tokens, gain_attn, qkv_bias, cosine, sine, qkv.all(), depth, group, bq
    )
    kv_own = Box(kv_own)
    fence(kv_own, out_near, place)
    kv = [kv_own]
    rightward = [(i, i + 1) for i in range(contexts - 1)]
    for k in range(1, contexts):
        kv.append(Box(lax.ppermute(kv[-1].v, "ctx", rightward)))
        if k == 1:
            out_other[1] = over_tp(out_w.near)
            out_rest = out_w.near_rest(0, kv_own)
            fence(mark(place), kv, out_rest, out_far, out_other[0], gate.cut(kv_own))
        elif k == 2:
            gate_far = gate.far(0, kv[1])
            out_other.update({j: over_tp(piece) for (j, _), piece in out_w.got.items()})
            top_grad_t = Box(held(cotangent, *kv).T)
            fence(mark(place), kv, out_other[1], up_parts)
        elif k == contexts - 1:
            fence(mark(place), kv, gate_far, top_grad_t)
            fence(kv, up_parts)
        else:
            fence(mark(place), kv)
    kv_back = jnp.concatenate([p.v for p in kv], axis=0)
    up_spread = up.spread()
    gate_far = gate.far(1, kv)
    out_other = [out_other[j] for j in range(shards)]
    upper_rows = rows // 2
    upper, *upper_sums = attention_forward(
        lists_f, queries, kv_back, reach_rows, hot, bq, bk_f, 0, upper_rows
    )
    upper, leaves = Box(upper), boxes(lists_f)
    fence(upper, leaves, out_other)
    upper_other = over_tp(upper)
    gate_far_2 = gate.far(2, upper)
    lower, *lower_sums = attention_forward(
        [leaf.v for leaf in leaves], queries, kv_back, reach_rows, hot, bq, bk_f, upper_rows,
        upper_rows,
    )
    lower = Box(lower)
    fence(lower, place)
    lower_other = over_tp(lower)
    gate_rest = gate.near_rest(0) + gate.near_rest(1)
    attended = Box(jnp.concatenate([upper.v, lower.v], axis=0))
    lse, tops = (jnp.concatenate(both, axis=1) for both in zip(upper_sums, lower_sums))
    attended_other = lower_other
    cuts = down.cut(lower)
    fence(
        mark(place), lower_other, upper_other, gate_far_2, gate_rest, up_spread, attended, cuts
    )
    down_far = down.far(0, attended_other)
    gate_rest = gate.near_rest(2) + up.near_rest(0)
    own_near = gate.near_own(attended_other) + up.near_own(attended_other)
    mid, hidden_two, hidden_two_t = branch(
        place.v, tokens, attended.v, upper_other.v, lower_other.v, gain_ffn, out_w.all(),
        [p.v for p in out_other], depth, bq,
    )
    mid = Box(mid)
    fence(mid, gate_rest, own_near, place, down_far)
    down_far = down.far(1, mid) + down.far(2, mid)
    down_near = down.near_own(mid)
    act, by_gate, by_up = gate_up(place.v, hidden_two, gate.all(), up.all(), depth, 512)
    act = Box(act)
    fence(act, down_far, down_near, top_grad_t, place)
    down_far = down.far(3, act)
    down_rest = down.near_rest(0, act) + down.near_rest(1) + down.near_rest(2)
    down_part = Box(whole_grad(top_grad_t.v, act.v, 512))
    fence(down_part, down_rest, down_far, place)
    down_part = Box(lax.psum_scatter(down_part.v, ("shard", "ctx"), scatter_dimension=0, tiled=True))
    down_rest = down.near_rest(3)
    fence(mark(place), down_rest)
    d_gate, d_up, *d_hidden_two = gate_up_back(
        place.v, cotangent, by_gate, by_up, gate.all(), up.all(), down.all(), depth, 512
    )

    d_hidden_two = boxes(d_hidden_two)
    gate_grad = Reduction(shards, contexts, 2)
    up_grad = Reduction(shards, contexts, 2)
    last_grad = Reduction(shards, contexts, 1)
    fence(place, d_hidden_two)
    other = [over_tp(d_hidden_two[0])]
    fence(place, gate_grad.make(place, hidden_two_t, d_gate, 512), other[0], d_hidden_two[1])
    gate_got = gate_grad.cores()
    other.append(over_tp(d_hidden_two[1]))
    fence(
        place, up_grad.make(place, hidden_two_t, d_up, 512), gate_got, other[1], d_hidden_two[2], act
    )
    up_got = up_grad.cores()
    other.append(over_tp(d_hidden_two[2]))
    fence(place, gate_grad.sum_away())
    gate_last = gate_grad.chips()
    ffn_own = Box(down_project(place.v, act.v, down.all(), width, depth, 896))
    fence(place, ffn_own, up_got, other[2], down_part)
    down_total = Box(lax.all_gather(down_part.v, "ctx", axis=0, tiled=True))
    ffn_other = over_tp(ffn_own)
    fence(place, up_grad.sum_away())
    up_last = up_grad.chips()

    d_mid, d_branch_t, d_att, delta, gain_two_part = middle_back(
        place.v, [p.v for p in d_hidden_two], [p.v for p in other], mid.v, cotangent, gain_ffn,
        attended.v, out_w.all(), depth, bq,
    )
    d_mid = Box(d_mid)
    fence(place, d_mid)
    out_sent = last_grad.make(place, d_branch_t, attended.v, 768)
    leaves = boxes(lists_b)
    fence(place, out_sent, gate_last[:1])
    out_got = last_grad.cores()
    fence(leaves, gate_grad.arrived(0))
    gate_one = gate_grad.inward(0)
    d_query, d_kv = attention_backward(
        [leaf.v for leaf in leaves], queries, d_att, lse, delta, kv_back, reach_rows, hot,
        cosine, sine, bq, bk_b,
    )
    d_kv = Box(d_kv)
    fence(d_kv, gate_one, gate_last[1:], out_got, ffn_other, mid, place)
    output = (mid.v + (ffn_own.v.astype(F32) + ffn_other.v.astype(F32))).astype(BF16)
    output = Box(output)
    leftward = [(i + 1, i) for i in range(contexts - 1)]
    d_kv_own = Box(d_kv.v[(contexts - 1) * rows :])
    for k in range(contexts - 2, -1, -1):
        got = Box(lax.ppermute(d_kv_own.v, "ctx", leftward))
        if k == contexts - 2:
            gate_two = gate_grad.middle(0)
            gate_own = gate_grad.arrived(1)
            gate_one = gate_grad.inward(1)
            fence(mark(place), got, output, gate_two, gate_one)
        elif k == 0:
            fence(mark(place), got, down_total, up_grad.arrived(0), up_last[1:])
        else:
            fence(mark(place), got, up_last[:1])
        d_kv_own = Box(d_kv.v[k * rows : (k + 1) * rows] + got.v)
    fence(place, d_kv_own, list(gate_grad.own.values()), gate_one, gate_two, list(up_grad.own.values()))
    gate_three = gate_grad.outward(0)
    gate_two = gate_grad.middle(1)
    up_one = up_grad.inward(0)
    d_mixed, bias_part, gain_one_part, *d_hidden_one = mix_back(
        place.v, d_query, d_kv_own.v, cosine, sine, tokens, qkv.all(), depth, bq
    )
    peak_own = jnp.max(tops, axis=1)
    device = shard * contexts + ctx
    spread = jnp.where(
        (jnp.arange(shards * contexts)[:, None, None] == device)
        & (jnp.arange(halves)[None, :, None] == half),
        peak_own[None, None, :],
        0.0,
    )
    bias_both = jnp.where(jnp.arange(halves)[:, None] == half, bias_part, 0.0)
    vector = Box(
        jnp.concatenate(
            [gain_one_part[0], gain_two_part[0], bias_both.reshape(-1), spread.reshape(-1)]
        )
    )
    d_hidden_one = boxes(d_hidden_one)
    fence(place, vector, d_hidden_one)

    def hop(axis, bit):
        vector.v = vector.v + swap(vector.v, axis, sizes[axis], bit)
        return vector

    back = [over_tp(d_hidden_one[0])]
    q_sent = last_grad.make(place, hidden_one_t, d_mixed, 512)
    fence(place, q_sent, back[0], d_hidden_one[1], up_grad.arrived(1))
    qkv_got = last_grad.cores()
    back.append(over_tp(d_hidden_one[1]))
    hop("shard", 1)
    fence(mark(place), qkv_got, gate_two, up_one, vector, gate_three)
    up_two = up_grad.middle(0)
    up_one = up_grad.inward(1)
    gate_three = gate_grad.outward(1)
    bit = 2
    while bit < shards:
        hop("shard", bit)
        bit *= 2
    fence(place, last_grad.sum_away(), vector)
    last_last = last_grad.chips()
    hop("tp", 1)
    fence(mark(place), up_two, up_one, vector, last_last, back[1], d_hidden_one[2], gate_three)
    back.append(over_tp(d_hidden_one[2]))
    vectors = Reduction(shards, contexts, 1)
    vectors.own[0] = vector
    up_three = up_grad.outward(0)
    up_two = up_grad.middle(1)
    last_grad.arrived(0)
    last_one = last_grad.inward(0) + vectors.inward(0)
    fence(mark(place), up_two, last_one, back[2], d_mid, up_three)
    up_three = up_grad.outward(1)
    last_two = last_grad.middle(0) + vectors.middle(0)
    input_grad = Box(
        input_back(
            place.v, [p.v for p in d_hidden_one], [p.v for p in back], tokens, gain_attn, d_mid.v, bq
        )
    )
    fence(input_grad, last_two, place, up_three)
    last_three = last_grad.outward(0) + vectors.outward(0)
    vector = Box(vectors.result())
    gate_total, up_total, last_total = (one.result() for one in (gate_grad, up_grad, last_grad))
    out_total = last_total[:, : out_weight.shape[1]]
    qkv_total = last_total[:, out_weight.shape[1] :]
    down_total, input_grad, output, vector = (
        down_total.v.astype(F32), input_grad.v, output.v, vector.v
    )
    bias_at = 2 * width
    spread_at = bias_at + bias_both.size
    bias_grad = lax.dynamic_slice_in_dim(
        vector[bias_at:spread_at], half * bias_part.size, bias_part.size, 0
    )
    peaks = jnp.max(vector[spread_at:].reshape(shards * contexts, halves, group), axis=0)
    peak_all = lax.dynamic_index_in_dim(peaks, half, 0, keepdims=False)
    clip_out = CLIP_BOUND / jnp.maximum(peak_all, CLIP_BOUND)
    return (
        output,
        input_grad,
        vector[:width],
        qkv_total,
        bias_grad,
        out_total,
        vector[width:bias_at],
        gate_total,
        up_total,
        down_total,
        clip_out,
    )


def solution(mesh):
    token = P(("shard", "ctx"), None)
    weight = P("shard", "tp")
    return jax.shard_map(
        functools.partial(layer, dict(mesh.shape)),
        mesh=mesh,
        in_specs=(
            token,
            token,
            P("shard", None),
            P("shard", None),
            P(),
            weight,
            P("tp"),
            weight,
            P(),
            weight,
            weight,
            weight,
        ),
        out_specs=(
            token,
            token,
            P(),
            weight,
            P("tp"),
            weight,
            P(),
            weight,
            weight,
            weight,
            P("tp"),
        ),
        check_vma=False,
    )
```

```python
import functools
import math

import jax
import jax.numpy as jnp
from jax import lax
from jax.experimental import pallas as pl
from jax.experimental.pallas import tpu as pltpu
from jax.sharding import PartitionSpec as P

HEAD = 128
EPSILON = 1e-06
THETA = 1000000.0
CLIP_BOUND = 4.0
NEG_FILL = -1e30
SCALE = HEAD ** (-0.5)
SCALE_2 = SCALE * math.log2(math.e)
MIB = 1 << 20
CUTS = 3


def cuts(width):
    return [width // 4, width // 4, width // 2]


PACE = 175_000_000


def cost(us):
    return pl.CostEstimate(flops=int(us * PACE), bytes_accessed=1000, transcendentals=0)


BF16 = jnp.bfloat16
F32 = jnp.float32


def dot_nt(left, right):
    return lax.dot_general(left, right, (((1,), (1,)), ((), ())), preferred_element_type=F32)


def dot_nn(left, right):
    return jnp.dot(left, right, preferred_element_type=F32)


def seen_block(hot, reach_rows, col_at, row_at, bk, bq):
    linked = dot_nt(hot, reach_rows) > 0.5
    cols = col_at + lax.broadcasted_iota(jnp.int32, (bk, bq), 0)
    rows = row_at + lax.broadcasted_iota(jnp.int32, (bk, bq), 1)
    return (linked & (cols <= rows)) | (cols == rows)


def attention_forward_kernel(
    group, bq, bk, blocks, first, count, chosen, places, q_ref, kv_ref, reach_ref, hot_ref,
    out_ref, lse_ref, top_ref, max_s, sum_s, acc_s,
):
    row_block = pl.program_id(0) + first
    max_s[...] = jnp.full_like(max_s, NEG_FILL)
    sum_s[...] = jnp.zeros_like(sum_s)
    acc_s[...] = jnp.zeros_like(acc_s)
    row_at = places[blocks] + row_block * bq

    def body(step, carry):
        block = chosen[row_block * blocks + step]
        here = pl.ds(pl.multiple_of(block * bk, bk), bk)
        keys = kv_ref[here, :HEAD]
        values_t = kv_ref[here, HEAD:].T
        seen = seen_block(hot_ref[here, :], reach_ref[...], places[block], row_at, bk, bq)
        for h in range(group):
            score = jnp.where(seen, dot_nt(keys, q_ref[:, h * HEAD : (h + 1) * HEAD]), NEG_FILL)
            old = max_s[h : h + 1, :]
            new = jnp.maximum(old, jnp.max(score, axis=0, keepdims=True))
            prob = jnp.exp2((score - new) * SCALE_2)
            fade = jnp.exp2((old - new) * SCALE_2)
            max_s[h : h + 1, :] = new
            sum_s[h : h + 1, :] = sum_s[h : h + 1, :] * fade + jnp.sum(prob, axis=0, keepdims=True)
            acc_s[h] = acc_s[h] * fade + dot_nn(values_t, prob.astype(BF16))
        return carry

    lax.fori_loop(0, count[row_block], body, 0)
    top_ref[...] = max_s[...] * SCALE
    lse_ref[...] = max_s[...] * SCALE_2 + jnp.log2(sum_s[...])
    for h in range(group):
        out_ref[:, h * HEAD : (h + 1) * HEAD] = (acc_s[h] / sum_s[h : h + 1, :]).T.astype(BF16)


def attention_forward(lists, queries, kv, reach_rows, hot, bq, bk, first, rows):
    width = queries.shape[1]
    first //= bq
    slots = kv.shape[0]
    group = width // HEAD
    whole = lambda *_: (0, 0)
    row = lambda i, *_: (i, 0)
    col = lambda i, *_: (0, i)
    return pl.pallas_call(
        functools.partial(attention_forward_kernel, group, bq, bk, slots // bk, first),
        grid_spec=pltpu.PrefetchScalarGridSpec(
            num_scalar_prefetch=3,
            grid=(rows // bq,),
            in_specs=[
                pl.BlockSpec((bq, width), lambda i, *_: (i + first, 0)),
                pl.BlockSpec((slots, 2 * HEAD), whole),
                pl.BlockSpec((bq, HEAD), lambda i, *_: (i + first, 0)),
                pl.BlockSpec((slots, HEAD), whole),
            ],
            out_specs=[
                pl.BlockSpec((bq, width), row),
                pl.BlockSpec((group, bq), col),
                pl.BlockSpec((group, bq), col),
            ],
            scratch_shapes=[
                pltpu.VMEM((group, bq), F32),
                pltpu.VMEM((group, bq), F32),
                pltpu.VMEM((group, HEAD, bq), F32),
            ],
        ),
        out_shape=[
            jax.ShapeDtypeStruct((rows, width), BF16),
            jax.ShapeDtypeStruct((group, rows), F32),
            jax.ShapeDtypeStruct((group, rows), F32),
        ],
        compiler_params=pltpu.CompilerParams(vmem_limit_bytes=32 * MIB),
        cost_estimate=cost(15),
        name="attention_forward",
    )(*lists, queries, kv, reach_rows, hot)


def attention_backward_kernel(
    group, bq, bk, blocks, count, chosen, places, q_ref, do_ref, lse_ref, delta_ref, kv_ref,
    reach_ref, hot_ref, cos_ref, sin_ref, dq_ref, dkv_ref, acc_s, dk_s, dv_s,
):
    row_block = pl.program_id(0)

    @pl.when(row_block == 0)
    def _():
        dk_s[...] = jnp.zeros_like(dk_s)
        dv_s[...] = jnp.zeros_like(dv_s)

    acc_s[...] = jnp.zeros_like(acc_s)
    row_at = places[blocks] + row_block * bq

    def body(step, carry):
        block = chosen[row_block * blocks + step]
        here = pl.ds(pl.multiple_of(block * bk, bk), bk)
        keys = kv_ref[here, :HEAD]
        values = kv_ref[here, HEAD:]
        keys_t = keys.T
        seen = seen_block(hot_ref[here, :], reach_ref[...], places[block], row_at, bk, bq)
        dk = jnp.zeros((bk, HEAD), F32)
        dv = jnp.zeros((bk, HEAD), F32)
        for h in range(group):
            qh = q_ref[:, h * HEAD : (h + 1) * HEAD]
            doh = do_ref[:, h * HEAD : (h + 1) * HEAD]
            prob = jnp.where(
                seen, jnp.exp2(dot_nt(keys, qh) * SCALE_2 - lse_ref[h : h + 1, :]), 0.0
            )
            ds = (prob * (dot_nt(values, doh) - delta_ref[h : h + 1, :])).astype(BF16)
            dv = dv + dot_nn(prob.astype(BF16), doh)
            dk = dk + dot_nn(ds, qh)
            acc_s[h] = acc_s[h] + dot_nn(keys_t, ds)
        dk_s[here, :] += dk
        dv_s[here, :] += dv
        return carry

    lax.fori_loop(0, count[row_block], body, 0)
    for h in range(group):
        d_query = (acc_s[h] * SCALE).T
        dq_ref[:, h * HEAD : (h + 1) * HEAD] = turned(
            d_query, cos_ref[...], -sin_ref[...]
        ).astype(BF16)

    @pl.when(row_block == pl.num_programs(0) - 1)
    def _():
        dkv_ref[:, :HEAD] = (dk_s[...] * SCALE).astype(BF16)
        dkv_ref[:, HEAD:] = dv_s[...].astype(BF16)


def attention_backward(
    lists, queries, d_att, lse, delta, kv, reach_rows, hot, cosine, sine, bq, bk
):
    rows, width = queries.shape
    slots = kv.shape[0]
    group = width // HEAD
    whole = lambda *_: (0, 0)
    row = lambda i, *_: (i, 0)
    col = lambda i, *_: (0, i)
    return pl.pallas_call(
        functools.partial(attention_backward_kernel, group, bq, bk, slots // bk),
        grid_spec=pltpu.PrefetchScalarGridSpec(
            num_scalar_prefetch=3,
            grid=(rows // bq,),
            in_specs=[
                pl.BlockSpec((bq, width), row),
                pl.BlockSpec((bq, width), row),
                pl.BlockSpec((group, bq), col),
                pl.BlockSpec((group, bq), col),
                pl.BlockSpec((slots, 2 * HEAD), whole),
                pl.BlockSpec((bq, HEAD), row),
                pl.BlockSpec((slots, HEAD), whole),
                pl.BlockSpec((bq, HEAD), row),
                pl.BlockSpec((bq, HEAD), row),
            ],
            out_specs=[
                pl.BlockSpec((bq, width), row),
                pl.BlockSpec((slots, 2 * HEAD), whole),
            ],
            scratch_shapes=[
                pltpu.VMEM((group, HEAD, bq), F32),
                pltpu.VMEM((slots, HEAD), F32),
                pltpu.VMEM((slots, HEAD), F32),
            ],
        ),
        out_shape=[
            jax.ShapeDtypeStruct((rows, width), BF16),
            jax.ShapeDtypeStruct((slots, 2 * HEAD), BF16),
        ],
        compiler_params=pltpu.CompilerParams(vmem_limit_bytes=40 * MIB),
        cost_estimate=cost(54),
        name="attention_backward",
    )(*lists, queries, d_att, lse, delta, kv, reach_rows, hot, cosine, sine)


def join(mine, depth, places, pieces, joined, at_col=None):
    cols = pieces[0].shape[1]
    where = slice(None) if at_col is None else pl.ds(pl.multiple_of(at_col, HEAD), cols)
    for (j, row), piece in zip(places, pieces):
        at = pl.multiple_of((mine ^ j) * depth + row, 16)
        joined[pl.ds(at, piece.shape[0]), where] = piece[...]


class Rows:
    def __init__(self, pieces, depth, tf=None):
        self.depth = depth
        self.places = [(j, row) for j, row, _ in pieces]
        self.arrays = [array for _, _, array in pieces]
        if tf is None:
            self.specs = [once(array.shape) for array in self.arrays]
        else:
            self.specs = [pl.BlockSpec((array.shape[0], tf), col_block) for array in self.arrays]

    def __len__(self):
        return len(self.arrays)

    def join(self, mine, refs, joined, at_col=None):
        join(mine, self.depth, self.places, refs, joined, at_col)


def whole_block(*_):
    return (0, 0)


def row_block(i, *_):
    return (i, 0)


def col_block(i, *_):
    return (0, i)


def once(shape):
    return pl.BlockSpec(shape, whole_block, pipeline_mode=pl.Buffered(1))


def call(kernel, grid, in_specs, out_specs, out_shape, scratch, vmem, us, name):
    return pl.pallas_call(
        kernel,
        grid_spec=pltpu.PrefetchScalarGridSpec(
            num_scalar_prefetch=1,
            grid=(grid,),
            in_specs=in_specs,
            out_specs=out_specs,
            scratch_shapes=scratch,
        ),
        out_shape=out_shape,
        compiler_params=pltpu.CompilerParams(vmem_limit_bytes=vmem * MIB),
        cost_estimate=cost(us),
        name=name,
    )


def shape(dims, dtype):
    return jax.ShapeDtypeStruct(dims, dtype)


def clear_tail(tail, *joined):
    if tail:

        @pl.when(pl.program_id(0) == pl.num_programs(0) - 1)
        def _():
            for one in joined:
                one[:, tail:] = jnp.zeros_like(one[:, tail:])


def gate_up_kernel(gates, ups, place, h_ref, *refs):
    gate_refs, refs = refs[: len(gates)], refs[len(gates) :]
    up_refs, refs = refs[: len(ups)], refs[len(ups) :]
    act_ref, by_gate_ref, by_up_ref, gate_s, up_s = refs
    gates.join(place[0], gate_refs, gate_s)
    ups.join(place[0], up_refs, up_s)
    gate = dot_nn(h_ref[...], gate_s[...])
    up = dot_nn(h_ref[...], up_s[...])
    sig = jax.nn.sigmoid(gate)
    silu = gate * sig
    act_ref[...] = (silu * up).astype(BF16)
    by_up_ref[...] = silu.astype(BF16)
    by_gate_ref[...] = (up * sig * (1.0 + gate * (1.0 - sig))).astype(BF16)


def gate_up(place, hidden, gates, ups, depth, tf):
    rows, width = hidden.shape
    units = gates[0][2].shape[1]
    gates, ups = Rows(gates, depth, tf), Rows(ups, depth, tf)
    return call(
        functools.partial(gate_up_kernel, gates, ups),
        pl.cdiv(units, tf),
        [once((rows, width))] + gates.specs + ups.specs,
        [pl.BlockSpec((rows, tf), col_block)] * 3,
        [shape((rows, units), BF16)] * 3,
        [pltpu.VMEM((width, tf), BF16)] * 2,
        60,
        40,
        "gate_up",
    )(place, hidden, *gates.arrays, *ups.arrays)


def gate_up_back_kernel(gates, ups, downs, tail, place, c_ref, by_gate_ref, by_up_ref, *refs):
    gate_refs, refs = refs[: len(gates)], refs[len(gates) :]
    up_refs, refs = refs[: len(ups)], refs[len(ups) :]
    down_refs, refs = refs[: len(downs)], refs[len(downs) :]
    dg_ref, du_ref, *dh_refs, gate_s, up_s, down_s, sum_s = refs
    step = pl.program_id(0)
    gates.join(place[0], gate_refs, gate_s)
    ups.join(place[0], up_refs, up_s)
    downs.join(place[0], down_refs, down_s)
    clear_tail(tail, gate_s, up_s, down_s)
    d_act = dot_nn(c_ref[...], down_s[...])
    by_gate, by_up = by_gate_ref[...].astype(F32), by_up_ref[...].astype(F32)
    if tail:
        last = step == pl.num_programs(0) - 1
        inside = lax.broadcasted_iota(jnp.int32, by_gate.shape, 1) < jnp.where(
            last, tail, by_gate.shape[1]
        )
        by_gate = jnp.where(inside, by_gate, 0.0)
        by_up = jnp.where(inside, by_up, 0.0)
    d_gate = (d_act * by_gate).astype(BF16)
    d_up = (d_act * by_up).astype(BF16)
    dg_ref[...] = d_gate
    du_ref[...] = d_up

    @pl.when(step == 0)
    def _():
        sum_s[...] = jnp.zeros_like(sum_s)

    sum_s[...] += dot_nt(d_gate, gate_s[...]) + dot_nt(d_up, up_s[...])

    @pl.when(step == pl.num_programs(0) - 1)
    def _():
        at = 0
        for dh_ref in dh_refs:
            cols = dh_ref.shape[1]
            dh_ref[...] = sum_s[:, at : at + cols].astype(BF16)
            at += cols


def gate_up_back(place, cotangent, by_gate, by_up, gates, ups, downs, depth, tf):
    rows, width = cotangent.shape
    units = by_gate.shape[1]
    gates, ups, downs = (Rows(p, depth, tf) for p in (gates, ups, downs))
    return call(
        functools.partial(gate_up_back_kernel, gates, ups, downs, units % tf),
        pl.cdiv(units, tf),
        [once((rows, width))]
        + [pl.BlockSpec((rows, tf), col_block)] * 2
        + gates.specs
        + ups.specs
        + downs.specs,
        [pl.BlockSpec((rows, tf), col_block)] * 2 + [once((rows, cut)) for cut in cuts(width)],
        [shape((rows, units), BF16)] * 2 + [shape((rows, cut), BF16) for cut in cuts(width)],
        [pltpu.VMEM((width, tf), BF16)] * 3 + [pltpu.VMEM((rows, width), F32)],
        60,
        62,
        "gate_up_back",
    )(place, cotangent, by_gate, by_up, *gates.arrays, *ups.arrays, *downs.arrays)


def whole_grad_kernel(left_ref, right_ref, out_ref):
    out_ref[...] = dot_nn(left_ref[...], right_ref[...]).astype(BF16)


def whole_grad(left_t, right, tf):
    width, rows = left_t.shape
    units = right.shape[1]
    return pl.pallas_call(
        whole_grad_kernel,
        grid=(pl.cdiv(units, tf),),
        in_specs=[once((width, rows)), pl.BlockSpec((rows, tf), col_block)],
        out_specs=pl.BlockSpec((width, tf), col_block),
        out_shape=shape((width, units), BF16),
        compiler_params=pltpu.CompilerParams(vmem_limit_bytes=48 * MIB),
        cost_estimate=cost(19 if units > 2048 else 6),
        name="whole_grad",
    )(left_t, right)


def weight_grad_kernel(depth, parts, place, left_ref, right_ref, keep_ref, send_ref):
    for j in range(parts):
        half = keep_ref if j % 2 == 0 else send_ref
        rows = pl.ds(pl.multiple_of((place[0] ^ j) * depth, 16), depth)
        at = (j // 2) * depth
        half[at : at + depth, :] = dot_nn(left_ref[rows, :], right_ref[...]).astype(BF16)


def weight_grad(place, left_t, right, parts, tf):
    width, rows = left_t.shape
    units = right.shape[1]
    return call(
        functools.partial(weight_grad_kernel, width // parts, parts),
        pl.cdiv(units, tf),
        [once((width, rows)), pl.BlockSpec((rows, tf), col_block)],
        [pl.BlockSpec((width // 2, tf), col_block)] * 2,
        [shape((width // 2, units), BF16)] * 2,
        [],
        48,
        19 if units > 2048 else 7,
        "weight_grad",
    )(place, left_t, right)


def add_kernel(counts, *refs):
    out_ref, at, col = refs[-1], 0, 0
    for count in counts:
        parts = refs[at : at + count]
        cols = parts[0].shape[1]
        total = sum(ref[...].astype(F32) for ref in parts)
        out_ref[:, col : col + cols] = total.astype(BF16)
        at, col = at + count, col + cols


def add_rows(rows, *groups):
    parts = [part for group in groups for part in group]
    cols = sum(group[0][0].shape[1] for group in groups)
    step = math.gcd(rows, 64, *[row for _, row in parts])
    return pl.pallas_call(
        functools.partial(add_kernel, [len(group) for group in groups]),
        grid=(rows // step,),
        in_specs=[
            pl.BlockSpec((step, array.shape[1]), lambda i, at=row // step: (at + i, 0))
            for array, row in parts
        ],
        out_specs=pl.BlockSpec((step, cols), lambda i: (i, 0)),
        out_shape=shape((rows, cols), BF16),
        compiler_params=pltpu.CompilerParams(vmem_limit_bytes=32 * MIB),
        cost_estimate=cost(4),
        name="add_rows",
    )(*[array for array, _ in parts])


def mark_kernel(place_ref, out_ref):
    for at in range(2):
        out_ref[at] = place_ref[at]


def mark(place):
    place.v = pl.pallas_call(
        mark_kernel,
        in_specs=[pl.BlockSpec(memory_space=pltpu.SMEM)],
        out_specs=pl.BlockSpec(memory_space=pltpu.SMEM),
        out_shape=shape((2,), jnp.int32),
        cost_estimate=cost(1),
        name="mark",
    )(place.v)
    return place


def down_project_kernel(downs, place, act_ref, *refs):
    down_refs, (out_ref, down_s, sum_s) = refs[: len(downs)], refs[len(downs) :]
    step = pl.program_id(0)
    downs.join(place[0], down_refs, down_s)

    @pl.when(step == 0)
    def _():
        sum_s[...] = jnp.zeros_like(sum_s)

    sum_s[...] += dot_nt(act_ref[...], down_s[...])

    @pl.when(step == pl.num_programs(0) - 1)
    def _():
        out_ref[...] = sum_s[...].astype(BF16)


def down_project(place, act, downs, width, depth, tf):
    rows, units = act.shape
    downs = Rows(downs, depth, tf)
    return call(
        functools.partial(down_project_kernel, downs),
        units // tf,
        [pl.BlockSpec((rows, tf), col_block)] + downs.specs,
        once((rows, width)),
        shape((rows, width), BF16),
        [pltpu.VMEM((width, tf), BF16), pltpu.VMEM((rows, width), F32)],
        48,
        24,
        "down_project",
    )(place, act, *downs.arrays)


def inverse_rms(values):
    return lax.rsqrt(jnp.mean(values * values, axis=-1, keepdims=True) + EPSILON)


def turned(values, cosine, sine):
    return values * cosine + pltpu.roll(values, HEAD // 2, 1) * sine


def mix_kernel(weight, group, place, x_ref, gain_ref, bias_ref, cos_ref, sin_ref, *refs):
    pieces, (q_ref, kv_ref, ht_ref, weight_s) = refs[: len(weight)], refs[len(weight) :]

    @pl.when(pl.program_id(0) == 0)
    def _():
        weight.join(place[0], pieces, weight_s)

    x = x_ref[...].astype(F32)
    hidden = (x * inverse_rms(x) * gain_ref[...].astype(F32)).astype(BF16)
    ht_ref[...] = hidden.T
    mixed = dot_nn(hidden, weight_s[...]) + bias_ref[...].astype(F32)
    cosine, sine = cos_ref[...], sin_ref[...]
    for h in range(group):
        at = slice(h * HEAD, (h + 1) * HEAD)
        q_ref[:, at] = turned(mixed[:, at], cosine, sine).astype(BF16)
    split = group * HEAD
    kv_ref[:, :HEAD] = turned(mixed[:, split : split + HEAD], cosine, sine).astype(BF16)
    kv_ref[:, HEAD:] = mixed[:, split + HEAD :].astype(BF16)


def mix(place, tokens, gain, bias, cosine, sine, pieces, depth, group, bq):
    rows, width = tokens.shape
    cols = pieces[0][2].shape[1]
    weight = Rows(pieces, depth)
    return call(
        functools.partial(mix_kernel, weight, group),
        rows // bq,
        [
            pl.BlockSpec((bq, width), row_block),
            once((1, width)),
            once((1, cols)),
            pl.BlockSpec((bq, HEAD), row_block),
            pl.BlockSpec((bq, HEAD), row_block),
        ]
        + weight.specs,
        [
            pl.BlockSpec((bq, group * HEAD), row_block),
            pl.BlockSpec((bq, 2 * HEAD), row_block),
            pl.BlockSpec((width, bq), col_block),
        ],
        [
            shape((rows, group * HEAD), BF16),
            shape((rows, 2 * HEAD), BF16),
            shape((width, rows), BF16),
        ],
        [pltpu.VMEM((width, cols), BF16)],
        32,
        8,
        "mix",
    )(place, tokens, gain[None], bias[None], cosine, sine, *weight.arrays)


def branch_kernel(weight, parts, place, x_ref, own_ref, upper_ref, lower_ref, gain_ref, *refs):
    own_w, other_w = refs[: len(weight)], refs[len(weight) : len(weight) + parts]
    mid_ref, h_ref, ht_ref, weight_s, att_s = refs[len(weight) + parts :]
    split = own_ref.shape[1]
    own_at = pl.multiple_of(place[1] * split, HEAD)
    other_at = pl.multiple_of((1 - place[1]) * split, HEAD)

    @pl.when(pl.program_id(0) == 0)
    def _():
        weight.join(place[0], own_w, weight_s, own_at)
        join(place[0], weight.depth, [(j, 0) for j in range(parts)], other_w, weight_s, other_at)

    att_s[:, pl.ds(own_at, split)] = own_ref[...]
    steps = pl.num_programs(0)

    @pl.when(pl.program_id(0) < steps // 2)
    def _():
        att_s[:, pl.ds(other_at, split)] = upper_ref[...]

    @pl.when(pl.program_id(0) >= steps // 2)
    def _():
        att_s[:, pl.ds(other_at, split)] = lower_ref[...]

    mid = x_ref[...].astype(F32) + dot_nt(att_s[...], weight_s[...])
    mid_ref[...] = mid
    hidden = (mid * inverse_rms(mid) * gain_ref[...].astype(F32)).astype(BF16)
    h_ref[...] = hidden
    ht_ref[...] = hidden.T


def branch(place, tokens, own, upper, lower, gain, pieces, other_pieces, depth, bq):
    rows, width = tokens.shape
    cols = own.shape[1]
    parts = width // depth
    weight = Rows(pieces, depth)
    wide = pl.BlockSpec((bq, width), row_block)
    narrow = pl.BlockSpec((bq, cols), row_block)
    other_specs = [once((depth, cols))] * parts
    half = rows // bq // 2
    return call(
        functools.partial(branch_kernel, weight, parts),
        rows // bq,
        [
            wide,
            narrow,
            pl.BlockSpec((bq, cols), lambda i, *_: (jnp.minimum(i, half - 1), 0)),
            pl.BlockSpec((bq, cols), lambda i, *_: (jnp.maximum(i - half, 0), 0)),
            once((1, width)),
        ]
        + weight.specs
        + other_specs,
        [wide, wide, pl.BlockSpec((width, bq), col_block)],
        [shape((rows, width), F32), shape((rows, width), BF16), shape((width, rows), BF16)],
        [pltpu.VMEM((width, 2 * cols), BF16), pltpu.VMEM((bq, 2 * cols), BF16)],
        40,
        12,
        "branch",
    )(place, tokens, own, upper, lower, gain[None], *weight.arrays, *other_pieces)


def middle_back_kernel(
    weight, group, place, mid_ref, c_ref, gain_ref, att_ref, *refs
):
    own_refs, other_refs, refs = refs[:CUTS], refs[CUTS : 2 * CUTS], refs[2 * CUTS :]
    pieces, refs = refs[: len(weight)], refs[len(weight) :]
    dm_ref, dbt_ref, da_ref, delta_ref, dgain_ref, weight_s = refs

    @pl.when(pl.program_id(0) == 0)
    def _():
        weight.join(place[0], pieces, weight_s)
        dgain_ref[...] = jnp.zeros_like(dgain_ref)

    mid = mid_ref[...]
    inverse = inverse_rms(mid)
    normed = mid * inverse
    own = jnp.concatenate([ref[...] for ref in own_refs], axis=1).astype(F32)
    other = jnp.concatenate([ref[...] for ref in other_refs], axis=1).astype(F32)
    dgain_ref[...] += jnp.sum(own * normed, axis=0, keepdims=True)
    scaled = (own + other) * gain_ref[...].astype(F32)
    d_mid = c_ref[...].astype(F32) + inverse * (
        scaled - normed * jnp.mean(scaled * normed, axis=-1, keepdims=True)
    )
    dm_ref[...] = d_mid
    d_branch = d_mid.astype(BF16)
    dbt_ref[...] = d_branch.T
    d_att = dot_nn(d_branch, weight_s[...]).astype(BF16)
    da_ref[...] = d_att
    product = d_att.astype(F32) * att_ref[...].astype(F32)
    for h in range(group):
        delta_ref[h : h + 1, :] = jnp.sum(
            product[:, h * HEAD : (h + 1) * HEAD].T, axis=0, keepdims=True
        )


def middle_back(place, own, other, mid, cotangent, gain, attended, pieces, depth, bq):
    rows, width = mid.shape
    cols = attended.shape[1]
    weight = Rows(pieces, depth)
    group = cols // HEAD
    wide = pl.BlockSpec((bq, width), row_block)
    narrow = pl.BlockSpec((bq, cols), row_block)
    return call(
        functools.partial(middle_back_kernel, weight, group),
        rows // bq,
        [wide, wide, once((1, width)), narrow]
        + [pl.BlockSpec((bq, cut), row_block) for cut in cuts(width)] * 2
        + weight.specs,
        [
            wide,
            pl.BlockSpec((width, bq), col_block),
            narrow,
            pl.BlockSpec((group, bq), col_block),
            pl.BlockSpec((1, width), whole_block),
        ],
        [
            shape((rows, width), F32),
            shape((width, rows), BF16),
            shape((rows, cols), BF16),
            shape((group, rows), F32),
            shape((1, width), F32),
        ],
        [pltpu.VMEM((width, cols), BF16)],
        48,
        13,
        "middle_back",
    )(place, mid, cotangent, gain[None], attended, *own, *other, *weight.arrays)


def mix_back_kernel(
    weight, group, place, dq_ref, dkv_ref, cos_ref, sin_ref, x_ref, *refs
):
    pieces, refs = refs[: len(weight)], refs[len(weight) :]
    dm_ref, dbias_ref, dgain_ref, *dh_refs, weight_s = refs

    @pl.when(pl.program_id(0) == 0)
    def _():
        weight.join(place[0], pieces, weight_s)
        dgain_ref[...] = jnp.zeros_like(dgain_ref)
        dbias_ref[...] = jnp.zeros_like(dbias_ref)

    split = group * HEAD
    dm_ref[:, :split] = dq_ref[...]
    d_keys = dkv_ref[:, :HEAD].astype(F32)
    dm_ref[:, split : split + HEAD] = turned(d_keys, cos_ref[...], -sin_ref[...]).astype(BF16)
    dm_ref[:, split + HEAD :] = dkv_ref[:, HEAD:]
    d_mixed = dm_ref[...]
    dbias_ref[...] += jnp.sum(d_mixed.astype(F32), axis=0, keepdims=True)
    d_hidden = dot_nt(d_mixed, weight_s[...])
    x = x_ref[...].astype(F32)
    dgain_ref[...] += jnp.sum(d_hidden * (x * inverse_rms(x)), axis=0, keepdims=True)
    at = 0
    for dh_ref in dh_refs:
        cols = dh_ref.shape[1]
        dh_ref[...] = d_hidden[:, at : at + cols].astype(BF16)
        at += cols


def mix_back(place, dq, dkv, cosine, sine, tokens, pieces, depth, bq):
    rows, width = tokens.shape
    cols = pieces[0][2].shape[1]
    weight = Rows(pieces, depth)
    group = dq.shape[1] // HEAD
    wide = pl.BlockSpec((bq, width), row_block)
    return call(
        functools.partial(mix_back_kernel, weight, group),
        rows // bq,
        [
            pl.BlockSpec((bq, group * HEAD), row_block),
            pl.BlockSpec((bq, 2 * HEAD), row_block),
            pl.BlockSpec((bq, HEAD), row_block),
            pl.BlockSpec((bq, HEAD), row_block),
            wide,
        ]
        + weight.specs,
        [
            pl.BlockSpec((bq, cols), row_block),
            pl.BlockSpec((1, cols), whole_block),
            pl.BlockSpec((1, width), whole_block),
        ]
        + [pl.BlockSpec((bq, cut), row_block) for cut in cuts(width)],
        [
            shape((rows, cols), BF16),
            shape((1, cols), F32),
            shape((1, width), F32),
        ]
        + [shape((rows, cut), BF16) for cut in cuts(width)],
        [pltpu.VMEM((width, cols), BF16)],
        32,
        8,
        "mix_back",
    )(place, dq, dkv, cosine, sine, tokens, *weight.arrays)


def input_back_kernel(place, x_ref, gain_ref, dm_ref, *refs):
    own_refs, other_refs, (out_ref,) = refs[:CUTS], refs[CUTS : 2 * CUTS], refs[2 * CUTS :]
    own = jnp.concatenate([ref[...] for ref in own_refs], axis=1).astype(F32)
    other = jnp.concatenate([ref[...] for ref in other_refs], axis=1).astype(F32)
    x = x_ref[...].astype(F32)
    inverse = inverse_rms(x)
    normed = x * inverse
    scaled = (own + other) * gain_ref[...].astype(F32)
    out_ref[...] = dm_ref[...] + inverse * (
        scaled - normed * jnp.mean(scaled * normed, axis=-1, keepdims=True)
    )


def input_back(place, own, other, tokens, gain, d_mid, bq):
    rows, width = tokens.shape
    wide = pl.BlockSpec((bq, width), row_block)
    return call(
        input_back_kernel,
        rows // bq,
        [wide, once((1, width)), wide]
        + [pl.BlockSpec((bq, cut), row_block) for cut in cuts(width)] * 2,
        wide,
        shape((rows, width), F32),
        [],
        32,
        8,
        "input_back",
    )(place, tokens, gain[None], d_mid, *own, *other)


class Box:
    def __init__(self, v):
        self.v = v


def boxes(values):
    return [Box(v) for v in values]


def fence(*items):
    flat = []
    for item in items:
        flat += item if isinstance(item, (list, tuple)) else [item]
    for item, v in zip(flat, lax.optimization_barrier([item.v for item in flat])):
        item.v = v


def held(value, *items):
    one = Box(value)
    fence(one, *items)
    return one.v


def swap(value, axis, size, bit):
    return lax.ppermute(value, axis, [(i, i ^ bit) for i in range(size)])


class Pieces:
    def __init__(self, own, size, slabs=1):
        if size != 4 or own.shape[0] % (16 * slabs):
            slabs = 1
        self.size, self.own, self.slabs = size, own, slabs
        self.depth = own.shape[0] // slabs
        self.got, self.cuts = {}, []

    def away(self, own):
        got, bit = {0: own}, self.size // 2
        while bit > 1:
            got.update({j ^ bit: swap(p, "shard", self.size, bit) for j, p in got.items()})
            bit //= 2
        return {j: Box(p) for j, p in got.items() if j}

    def far(self, slab, *first):
        if slab >= self.slabs:
            return []
        if self.cuts:
            own = held(self.cuts[slab].v, *first)
        else:
            own = held(self.own, *first)[slab * self.depth : (slab + 1) * self.depth]
        got = self.away(own)
        self.got.update({(j, slab): p for j, p in got.items()})
        return list(got.values())

    def cut(self, *first):
        own = held(self.own, *first)
        if self.slabs > 1:
            self.cuts = boxes(
                [own[k * self.depth : (k + 1) * self.depth] for k in range(self.slabs)]
            )
        return self.cuts

    def far_by_ctx(self, contexts, *first):
        rows = self.own.shape[0] // contexts
        own = lax.dynamic_slice_in_dim(
            held(self.own, *first), lax.axis_index("ctx") * rows, rows, 0
        )
        self.parts = self.away(own)
        return list(self.parts.values())

    def spread(self):
        for j, part in self.parts.items():
            self.got[j, 0] = Box(lax.all_gather(part.v, "ctx", axis=0, tiled=True))
        return [self.got[j, 0] for j in self.parts]

    def near_own(self, *first):
        self.near = Box(swap(held(self.own, *first), "shard", self.size, 1))
        return [self.near]

    def near_rest(self, slab, *first):
        if slab >= self.slabs:
            return []
        far = [j for j in range(2, self.size, 2)]
        if first:
            fence(*[self.got[j, slab] for j in far], *first)
        for j in far:
            self.got[j ^ 1, slab] = Box(swap(self.got[j, slab].v, "shard", self.size, 1))
        return [self.got[j ^ 1, slab] for j in far]

    def all(self):
        found = [(0, 0, self.own), (1, 0, self.near.v)]
        found += [
            (j, k * self.depth, p.v) for (j, k), p in sorted(self.got.items(), key=lambda i: i[0])
        ]
        return found


class Reduction:
    def __init__(self, shards, contexts, slabs):
        self.shards, self.chain = shards, contexts == 4
        self.slabs = slabs if shards == 4 else 1
        self.keep, self.send, self.got = [], [], []
        self.own, self.one, self.two, self.three = {}, {}, {}, {}
        self.by_sum = {}

    def make(self, place, left_t, right, tf):
        keep, send = boxes(weight_grad(place.v, left_t, right, self.shards, tf))
        self.keep.append(keep)
        self.send.append(send)
        return send

    def cores(self):
        self.got.append(Box(swap(self.send[len(self.got)].v, "shard", self.shards, 1)))
        return self.got[-1]

    def pairs(self, row):
        return [[(keep.v, row), (got.v, row)] for keep, got in zip(self.keep, self.got)]

    def sum_away(self):
        rows = self.keep[0].v.shape[0]
        if self.shards == 4:
            size = rows // 2 // self.slabs
            self.away = [
                Box(add_rows(size, *self.pairs(rows // 2 + slab * size)))
                for slab in range(self.slabs)
            ]
        else:
            self.away = [Box(add_rows(rows, *self.pairs(0)))]
        return self.away

    def chips(self):
        if self.shards == 4:
            self.last = [Box(swap(part.v, "shard", 4, 2)) for part in self.away]
            return self.last
        held, bit, count = self.away[0].v, 2, self.shards // 2
        while bit < self.shards:
            size = held.shape[0] // count
            blocks = [held[at * size : (at + 1) * size] for at in range(count)]
            away = swap(jnp.concatenate(blocks[1::2], axis=0), "shard", self.shards, bit)
            here = jnp.concatenate(blocks[::2], axis=0)
            held = here if 2 * bit >= self.shards else here + away
            bit, count = 2 * bit, count // 2
        self.here, self.last = held, boxes([away])
        return self.last

    def arrived(self, slab):
        if slab >= self.slabs:
            return []
        last = self.last[slab].v
        if self.shards != 4:
            self.own[slab] = Box(self.here + last)
        elif len(self.keep) == 1:
            size = last.shape[0]
            self.own[slab] = Box(add_rows(size, self.pairs(slab * size)[0] + [(last, 0)]))
        else:
            size = last.shape[0]
            here = add_rows(size, *self.pairs(slab * size))
            self.own[slab] = Box(add_rows(size, [(here, 0), (last, 0)]))
        return [self.own[slab]]

    def whole_sum(self, slab):
        if slab >= self.slabs:
            return []
        self.by_sum[slab] = Box(lax.psum(self.own[slab].v, "ctx"))
        return [self.by_sum[slab]]

    def inward(self, slab):
        if slab >= self.slabs:
            return []
        if not self.chain:
            return self.whole_sum(slab)
        self.one[slab] = Box(lax.ppermute(self.own[slab].v, "ctx", [(0, 1), (3, 2)]))
        return [self.one[slab]]

    def middle(self, slab):
        if not self.chain or slab >= self.slabs:
            return []
        self.own[slab] = Box(self.own[slab].v + self.one[slab].v)
        self.two[slab] = Box(lax.ppermute(self.own[slab].v, "ctx", [(1, 2), (2, 1)]))
        return [self.two[slab]]

    def outward(self, slab):
        if not self.chain or slab >= self.slabs:
            return []
        self.own[slab] = Box(self.own[slab].v + self.two[slab].v)
        self.three[slab] = Box(lax.ppermute(self.own[slab].v, "ctx", [(1, 0), (2, 3)]))
        return [self.three[slab]]

    def result(self):
        place = lax.axis_index("ctx")
        inside = (place == 1) | (place == 2)
        totals = [
            self.by_sum[slab].v
            if slab in self.by_sum
            else jnp.where(inside, self.own[slab].v, self.three[slab].v)
            for slab in range(self.slabs)
        ]
        whole = totals[0] if len(totals) == 1 else jnp.concatenate(totals, axis=0)
        return whole.astype(F32)


def tree_tables(seg_row, parent_row):
    seg_count = parent_row.shape[0]
    seg_ids = jnp.arange(seg_count, dtype=jnp.int32)
    one_hot = (seg_row[:, None] == seg_ids[None, :]).astype(jnp.int32)
    lengths = jnp.sum(one_hot, axis=0, dtype=jnp.int32)
    before = seg_ids[None, :] < seg_ids[:, None]
    starts = jnp.sum(jnp.where(before, lengths[None, :], 0), axis=1, dtype=jnp.int32)
    link = (parent_row[:, None] == seg_ids[None, :]) & (parent_row[:, None] != seg_ids[:, None])
    twice = jnp.any(link[:, :, None] & link[None, :, :], axis=1)
    strict = link | twice
    padding = parent_row == seg_ids
    reach = strict | ((seg_ids[:, None] == seg_ids[None, :]) & ~padding[:, None])
    offsets = jnp.sum(jnp.where(strict, lengths[None, :], 0), axis=1, dtype=jnp.int32) - starts
    return reach, offsets


def block_lists(row_hot, col_hot, reach, col_places, row_first, bq, bk):
    segs = reach.shape[0]
    row_has = jnp.any(row_hot.reshape(-1, bq, segs), axis=1)
    col_has = jnp.any(col_hot.reshape(-1, bk, segs), axis=1)
    row_blocks, col_blocks = row_has.shape[0], col_has.shape[0]
    row_reach = jnp.any(row_has[:, :, None] & reach[None], axis=1)
    meets = jnp.any(row_reach[:, None, :] & col_has[None], axis=2)
    col_at = col_places.reshape(-1, bk)[:, 0]
    row_at = row_first + bq * jnp.arange(row_blocks, dtype=jnp.int32)
    causal = col_at[None, :] < row_at[:, None] + bq
    diagonal = causal & (col_at[None, :] + bk > row_at[:, None])
    active = ((meets & causal) | diagonal) & (col_at >= 0)[None, :]
    ids = jnp.arange(col_blocks, dtype=jnp.int32)
    rank = jnp.sum(
        (active[:, None, :] & (ids[None, :] < ids[:, None])[None]).astype(jnp.int32), axis=2
    )
    placed = active[:, :, None] & (rank[:, :, None] == ids[None, None, :])
    chosen = jnp.sum(jnp.where(placed, ids[None, :, None], 0), axis=1, dtype=jnp.int32)
    count = jnp.sum(active.astype(jnp.int32), axis=1, dtype=jnp.int32)
    places = jnp.concatenate([col_at, row_first[None]])
    return count, chosen.reshape(-1), places


def layer(
    sizes, tokens, cotangent, segment, parent, gain_attn, qkv_weight, qkv_bias,
    out_weight, gain_ffn, gate_weight, up_weight, down_weight,
):
    shards, contexts, halves = sizes["shard"], sizes["ctx"], sizes["tp"]
    rows, width = tokens.shape
    group = out_weight.shape[1] // HEAD
    shard, ctx, half = lax.axis_index("shard"), lax.axis_index("ctx"), lax.axis_index("tp")
    place = jnp.stack([shard, half]).astype(jnp.int32)
    across = [(i, i ^ 1) for i in range(halves)]

    row_first = (ctx * rows).astype(jnp.int32)
    reach, offsets = tree_tables(segment[0], parent[0])
    seg_ids = jnp.arange(reach.shape[0], dtype=jnp.int32)
    behind = [jnp.maximum(ctx - k, 0) * rows for k in range(contexts)]
    seg_back = jnp.concatenate(
        [lax.dynamic_slice_in_dim(segment[0], at, rows, 0) for at in behind]
    )
    places_back = jnp.concatenate(
        [(ctx - k) * rows + jnp.arange(rows, dtype=jnp.int32) for k in range(contexts)]
    )
    col_hot = seg_back[:, None] == seg_ids[None, :]
    row_hot = col_hot[:rows]
    own_pos = places_back[:rows] + jnp.sum(
        jnp.where(row_hot, offsets[None, :], 0), axis=1, dtype=jnp.int32
    )
    pad = ((0, 0), (0, HEAD - reach.shape[0]))
    row_reach = jnp.any(row_hot[:, :, None] & reach[None], axis=1)
    reach_rows = jnp.pad(row_reach.astype(BF16), pad)
    hot = jnp.pad(col_hot.astype(BF16), pad)
    bq = math.gcd(rows, 256)
    bk_f, bk_b = math.gcd(rows, 128), math.gcd(rows, 512)
    lists_f = block_lists(row_hot, col_hot, reach, places_back, row_first, bq, bk_f)
    lists_b = block_lists(row_hot, col_hot, reach, places_back, row_first, bq, bk_b)
    lane = jnp.arange(HEAD, dtype=jnp.int32)
    frequency = THETA ** (-2.0 * (lane % (HEAD // 2)).astype(F32) / HEAD)
    angles = own_pos.astype(F32)[:, None] * frequency[None, :]
    cosine = jnp.cos(angles)
    sine = jnp.sin(angles) * jnp.where(lane < HEAD // 2, -1.0, 1.0)

    depth = width // shards
    qkv, out_w, gate, up, down = (
        Pieces(qkv_weight, shards),
        Pieces(out_weight, shards),
        Pieces(gate_weight, shards, 3),
        Pieces(up_weight, shards),
        Pieces(down_weight, shards, 4),
    )

    def over_tp(box):
        return Box(lax.ppermute(box.v, "tp", across))

    qkv_far = qkv.far(0)
    turns, place = boxes((cosine, sine)), Box(place)
    fence(turns, place, qkv_far)
    cosine, sine = (turn.v for turn in turns)
    leaves, tree = jax.tree.flatten((reach_rows, hot, lists_f, lists_b))
    leaves = boxes(leaves)
    qkv_near = qkv.near_own(qkv_far) + qkv.near_rest(0)
    out_far = out_w.far(0, qkv_far)
    out_near = out_w.near_own(qkv_far)
    out_other = {0: Box(lax.ppermute(held(out_weight, qkv_far), "tp", across))}
    fence(mark(place), qkv_near)
    up_parts = up.far_by_ctx(contexts, qkv_near)

    queries, kv_own, hidden_one_t = mix(
        place.v, tokens, gain_attn, qkv_bias, cosine, sine, qkv.all(), depth, group, bq
    )
    kv_own = Box(kv_own)
    fence(kv_own, out_near, place)
    kv = [kv_own]
    rightward = [(i, i + 1) for i in range(contexts - 1)]
    for k in range(1, contexts):
        kv.append(Box(lax.ppermute(kv[-1].v, "ctx", rightward)))
        if k == 1:
            out_other[1] = over_tp(out_w.near)
            out_rest = out_w.near_rest(0, kv_own)
            fence(mark(place), kv, out_rest, out_far, out_other[0], gate.cut(kv_own))
        elif k == 2:
            gate_far = gate.far(0, kv[1])
            out_other.update({j: over_tp(piece) for (j, _), piece in out_w.got.items()})
            top_grad_t = Box(held(cotangent, *kv).T)
            fence(mark(place), kv, out_other[1], up_parts, leaves)
        elif k == contexts - 1:
            fence(mark(place), kv, gate_far, top_grad_t)
            fence(kv, up_parts)
        else:
            fence(mark(place), kv)
    reach_rows, hot, lists_f, lists_b = tree.unflatten([leaf.v for leaf in leaves])
    kv_back = jnp.concatenate([p.v for p in kv], axis=0)
    up_spread = up.spread()
    gate_far = gate.far(1, kv)
    out_other = [out_other[j] for j in range(shards)]
    upper_rows = rows // 2
    upper, *upper_sums = attention_forward(
        lists_f, queries, kv_back, reach_rows, hot, bq, bk_f, 0, upper_rows
    )
    upper, leaves = Box(upper), boxes(lists_f)
    fence(upper, leaves, out_other)
    upper_other = over_tp(upper)
    gate_far_2 = gate.far(2, upper)
    lower, *lower_sums = attention_forward(
        [leaf.v for leaf in leaves], queries, kv_back, reach_rows, hot, bq, bk_f, upper_rows,
        upper_rows,
    )
    lower = Box(lower)
    fence(lower, place)
    lower_other = over_tp(lower)
    gate_rest = gate.near_rest(0) + gate.near_rest(1)
    attended = Box(jnp.concatenate([upper.v, lower.v], axis=0))
    lse, tops = (jnp.concatenate(both, axis=1) for both in zip(upper_sums, lower_sums))
    attended_other = lower_other
    cuts = down.cut(lower)
    fence(
        mark(place), lower_other, upper_other, gate_far_2, gate_rest, up_spread, attended, cuts
    )
    down_far = down.far(0, attended_other)
    gate_rest = gate.near_rest(2) + up.near_rest(0)
    own_near = gate.near_own(attended_other) + up.near_own(attended_other)
    mid, hidden_two, hidden_two_t = branch(
        place.v, tokens, attended.v, upper_other.v, lower_other.v, gain_ffn, out_w.all(),
        [p.v for p in out_other], depth, bq,
    )
    mid = Box(mid)
    fence(mid, gate_rest, own_near, place, down_far)
    down_far = down.far(1, mid) + down.far(2, mid)
    down_near = down.near_own(mid)
    act, by_gate, by_up = gate_up(place.v, hidden_two, gate.all(), up.all(), depth, 512)
    act = Box(act)
    fence(act, down_far, down_near, top_grad_t, place)
    down_far = down.far(3, act)
    down_rest = down.near_rest(0, act) + down.near_rest(1) + down.near_rest(2)
    down_part = Box(whole_grad(top_grad_t.v, act.v, 512))
    fence(down_part, down_rest, down_far, place)
    down_part = Box(lax.psum_scatter(down_part.v, ("shard", "ctx"), scatter_dimension=0, tiled=True))
    down_rest = down.near_rest(3)
    fence(mark(place), down_rest)
    d_gate, d_up, *d_hidden_two = gate_up_back(
        place.v, cotangent, by_gate, by_up, gate.all(), up.all(), down.all(), depth, 512
    )

    d_hidden_two = boxes(d_hidden_two)
    gate_grad = Reduction(shards, contexts, 2)
    up_grad = Reduction(shards, contexts, 2)
    last_grad = Reduction(shards, contexts, 1)
    fence(place, d_hidden_two)
    other = [over_tp(d_hidden_two[0])]
    fence(place, gate_grad.make(place, hidden_two_t, d_gate, 512), other[0], d_hidden_two[1])
    gate_got = gate_grad.cores()
    other.append(over_tp(d_hidden_two[1]))
    fence(
        place, up_grad.make(place, hidden_two_t, d_up, 512), gate_got, other[1], d_hidden_two[2], act
    )
    up_got = up_grad.cores()
    other.append(over_tp(d_hidden_two[2]))
    fence(place, gate_grad.sum_away())
    gate_last = gate_grad.chips()
    ffn_own = Box(down_project(place.v, act.v, down.all(), width, depth, 896))
    fence(place, ffn_own, up_got, other[2], down_part)
    down_total = Box(lax.all_gather(down_part.v, "ctx", axis=0, tiled=True))
    ffn_other = over_tp(ffn_own)
    fence(place, up_grad.sum_away())
    up_last = up_grad.chips()

    d_mid, d_branch_t, d_att, delta, gain_two_part = middle_back(
        place.v, [p.v for p in d_hidden_two], [p.v for p in other], mid.v, cotangent, gain_ffn,
        attended.v, out_w.all(), depth, bq,
    )
    d_mid = Box(d_mid)
    fence(place, d_mid)
    out_sent = last_grad.make(place, d_branch_t, attended.v, 768)
    leaves = boxes(lists_b)
    fence(place, out_sent, gate_last[:1])
    out_got = last_grad.cores()
    fence(leaves, gate_grad.arrived(0))
    gate_one = gate_grad.inward(0)
    d_query, d_kv = attention_backward(
        [leaf.v for leaf in leaves], queries, d_att, lse, delta, kv_back, reach_rows, hot,
        cosine, sine, bq, bk_b,
    )
    d_kv = Box(d_kv)
    fence(d_kv, gate_one, gate_last[1:], out_got, ffn_other, mid, place)
    output = (mid.v + (ffn_own.v.astype(F32) + ffn_other.v.astype(F32))).astype(BF16)
    output = Box(output)
    leftward = [(i + 1, i) for i in range(contexts - 1)]
    d_kv_own = Box(d_kv.v[(contexts - 1) * rows :])
    for k in range(contexts - 2, -1, -1):
        got = Box(lax.ppermute(d_kv_own.v, "ctx", leftward))
        if k == contexts - 2:
            gate_two = gate_grad.middle(0)
            gate_own = gate_grad.arrived(1)
            gate_one = gate_grad.inward(1)
            fence(mark(place), got, output, gate_two, gate_one)
        elif k == 0:
            fence(mark(place), got, down_total, up_grad.arrived(0), up_last[1:])
        else:
            fence(mark(place), got, up_last[:1])
        d_kv_own = Box(d_kv.v[k * rows : (k + 1) * rows] + got.v)
    fence(place, d_kv_own, list(gate_grad.own.values()), gate_one, gate_two, list(up_grad.own.values()))
    gate_three = gate_grad.outward(0)
    gate_two = gate_grad.middle(1)
    up_one = up_grad.inward(0)
    d_mixed, bias_part, gain_one_part, *d_hidden_one = mix_back(
        place.v, d_query, d_kv_own.v, cosine, sine, tokens, qkv.all(), depth, bq
    )
    peak_own = jnp.max(tops, axis=1)
    device = shard * contexts + ctx
    spread = jnp.where(
        (jnp.arange(shards * contexts)[:, None, None] == device)
        & (jnp.arange(halves)[None, :, None] == half),
        peak_own[None, None, :],
        0.0,
    )
    bias_both = jnp.where(jnp.arange(halves)[:, None] == half, bias_part, 0.0)
    vector = Box(
        jnp.concatenate(
            [gain_one_part[0], gain_two_part[0], bias_both.reshape(-1), spread.reshape(-1)]
        )
    )
    d_hidden_one = boxes(d_hidden_one)
    fence(place, vector, d_hidden_one)

    def hop(axis, bit):
        vector.v = vector.v + swap(vector.v, axis, sizes[axis], bit)
        return vector

    back = [over_tp(d_hidden_one[0])]
    q_sent = last_grad.make(place, hidden_one_t, d_mixed, 512)
    fence(place, q_sent, back[0], d_hidden_one[1], up_grad.arrived(1))
    qkv_got = last_grad.cores()
    back.append(over_tp(d_hidden_one[1]))
    hop("shard", 1)
    fence(mark(place), qkv_got, gate_two, up_one, vector, gate_three)
    up_two = up_grad.middle(0)
    up_one = up_grad.inward(1)
    gate_three = gate_grad.outward(1)
    bit = 2
    while bit < shards:
        hop("shard", bit)
        bit *= 2
    fence(place, last_grad.sum_away(), vector)
    last_last = last_grad.chips()
    hop("tp", 1)
    fence(mark(place), up_two, up_one, vector, last_last, back[1], d_hidden_one[2], gate_three)
    back.append(over_tp(d_hidden_one[2]))
    vectors = Reduction(shards, contexts, 1)
    vectors.own[0] = vector
    up_three = up_grad.outward(0)
    up_two = up_grad.middle(1)
    last_grad.arrived(0)
    last_one = last_grad.inward(0) + vectors.inward(0)
    fence(mark(place), up_two, last_one, back[2], d_mid, up_three)
    up_three = up_grad.outward(1)
    last_two = last_grad.middle(0) + vectors.middle(0)
    input_grad = Box(
        input_back(
            place.v, [p.v for p in d_hidden_one], [p.v for p in back], tokens, gain_attn, d_mid.v, bq
        )
    )
    fence(input_grad, last_two, place, up_three)
    last_three = last_grad.outward(0) + vectors.outward(0)
    vector = Box(vectors.result())
    gate_total, up_total, last_total = (one.result() for one in (gate_grad, up_grad, last_grad))
    out_total = last_total[:, : out_weight.shape[1]]
    qkv_total = last_total[:, out_weight.shape[1] :]
    down_total, input_grad, output, vector = (
        down_total.v.astype(F32), input_grad.v, output.v, vector.v
    )
    bias_at = 2 * width
    spread_at = bias_at + bias_both.size
    bias_grad = lax.dynamic_slice_in_dim(
        vector[bias_at:spread_at], half * bias_part.size, bias_part.size, 0
    )
    peaks = jnp.max(vector[spread_at:].reshape(shards * contexts, halves, group), axis=0)
    peak_all = lax.dynamic_index_in_dim(peaks, half, 0, keepdims=False)
    clip_out = CLIP_BOUND / jnp.maximum(peak_all, CLIP_BOUND)
    return (
        output,
        input_grad,
        vector[:width],
        qkv_total,
        bias_grad,
        out_total,
        vector[width:bias_at],
        gate_total,
        up_total,
        down_total,
        clip_out,
    )


def solution(mesh):
    token = P(("shard", "ctx"), None)
    weight = P("shard", "tp")
    return jax.shard_map(
        functools.partial(layer, dict(mesh.shape)),
        mesh=mesh,
        in_specs=(
            token,
            token,
            P("shard", None),
            P("shard", None),
            P(),
            weight,
            P("tp"),
            weight,
            P(),
            weight,
            weight,
            weight,
        ),
        out_specs=(
            token,
            token,
            P(),
            weight,
            P("tp"),
            weight,
            P(),
            weight,
            weight,
            weight,
            P("tp"),
        ),
        check_vma=False,
    )
```
